32 devices in a mesh: seq: 4 (over y, x), tp: 8 (over z, core).
Axes of the slice: x: 2, y: 2, z: 4, core: 2. Of those that a mesh axis runs over, the one named last changes fastest.
Arguments:
- inputs: bfloat16 [8, 1024, 1280], P(None, 'seq'), may hold values from -6 to 6
- starts: int32 [8, 1024], P(None, 'seq'), may hold values from 0 to 1, as said below
- first_proj: bfloat16 [1280, 640], P(None, 'tp'), may hold values from -0.15625 to 0.15625
- dilated_conv: bfloat16 [5, 640, 640], P(None, None, 'tp'), may hold values from -0.109375 to 0.109375
- last_proj: bfloat16 [640, 1280], P('tp'), may hold values from -0.25 to 0.25
- first_norm_gain: float32 [1280], replicated, may hold values from 0.25 to 1.75
- second_norm_gain: float32 [640], P('tp'), may hold values from 0.25 to 1.75
- third_norm_gain: float32 [640], P('tp'), may hold values from 0.25 to 1.75
- cotangent: bfloat16 [8, 1024, 1280], P(None, 'seq', 'tp'), may hold values from -6 to 6
Outputs:
- outputs: bfloat16 [8, 1024, 1280], P(None, 'seq', 'tp')
- grad_inputs: bfloat16 [8, 1024, 1280], P(None, 'seq')
- grad_first: float32 [1280, 640], P(None, 'tp')
- grad_conv: float32 [5, 640, 640], P(None, None, 'tp')
- grad_last: float32 [640, 1280], P('tp')
- grad_gain_outer: float32 [1280], P('tp')
- second_gain_gradient: float32 [640], P('tp')
- third_gain_gradient: float32 [640], P('tp')
The draws below stay inside these ranges and needn't reach their ends.
Inputs may be any that keep to these rules, and one draw needn't show every extreme that they name: `starts`: 1 where a new document begins in its packed row; in one packed row, drawn from the seed, no document begins; the other rows begin about 8 documents each.
All inputs are finite; a program needn't handle non-finite values.
Results may differ from the reference program's by a relative error of at most 0.0073.
Values may be sent and summed in bfloat16 or wider, within the bound.
A program may use at most 256 MiB of HBM per device.

```python
import jax
import jax.numpy as jnp
from jax import lax

D = 1280
H = 640
TAP_COUNT = 5
DILATION_STEP = 2
TAP_REACH = 4
ROWS = 8
LENGTH = 1024


def draw_starts(key, part):
    key = jax.random.fold_in(key, 7)
    key_flags, key_row, key_place = jax.random.split(key, 3)
    draws_int = jax.random.randint(key_flags, (ROWS, LENGTH), 0, LENGTH)
    begins = (draws_int < 8).astype(jnp.int32)
    chosen = jax.random.randint(key_row, (), 0, ROWS)
    forced_row = (chosen + 1) % ROWS
    forced_place = jax.random.randint(key_place, (), 0, LENGTH)
    row_ids = lax.broadcasted_iota(jnp.int32, (ROWS, LENGTH), 0)
    place_ids = lax.broadcasted_iota(jnp.int32, (ROWS, LENGTH), 1)
    begins = jnp.where((row_ids == forced_row) & (place_ids == forced_place), 1, begins)
    return jnp.where(row_ids == chosen, 0, begins).astype(jnp.int32)


def block_levels(own_key, shape, cuts, low, high):
    level, own = 1.0, jax.random.fold_in(own_key, 6)
    for position, shards_of in cuts:
        draws = jnp.exp(jax.random.uniform(jax.random.fold_in(own, position), (shards_of,), jnp.float32, low / len(cuts), high / len(cuts)))
        level = level * jnp.repeat(draws, shape[position] // shards_of).reshape([-1 if axis == position else 1 for axis in range(len(shape))])
    return level


def centred(rng, dims, scale, most, shards=(), kind=jnp.bfloat16):
    entries = scale * jax.random.normal(rng, dims, jnp.float32)
    if shards:
        entries = entries * block_levels(rng, dims, shards, -0.22, 0.18)
    return jnp.clip(entries, -most, most).astype(kind)


def setup_inputs(seed: int = 0) -> dict:
    seeds = jax.random.split(jax.random.key(seed), 10)
    inputs = centred(seeds[0], (ROWS, LENGTH, D), 1.0, 6.0, ((1, 4),))
    starts = draw_starts(jax.random.fold_in(seeds[9], 71), 0)
    first_proj = centred(seeds[2], (D, H), D ** -0.5, 0.15625, ((1, 8),))
    dilated_conv = centred(seeds[3], (TAP_COUNT, H, H), (TAP_COUNT * H) ** -0.5, 0.109375, ((2, 8),))
    last_proj = centred(seeds[4], (H, D), H ** -0.5, 0.25, ((0, 8),))
    first_norm_gain = jnp.clip(1.0 + 0.15 * jax.random.normal(seeds[5], (D,), jnp.float32), 0.25, 1.75)
    second_norm_gain = jnp.clip(1.0 + 0.15 * jax.random.normal(seeds[6], (H,), jnp.float32), 0.25, 1.75)
    third_norm_gain = jnp.clip(1.0 + 0.15 * jax.random.normal(seeds[7], (H,), jnp.float32), 0.25, 1.75)
    cotangent = centred(seeds[8], (ROWS, LENGTH, D), 1.0, 6.0, ((1, 4), (2, 8)))
    return {"inputs": inputs, "starts": starts, "first_proj": first_proj, "dilated_conv": dilated_conv, "last_proj": last_proj, "first_norm_gain": first_norm_gain, "second_norm_gain": second_norm_gain, "third_norm_gain": third_norm_gain, "cotangent": cotangent}


EPS = 1e-05
HIGHEST = lax.Precision.HIGHEST

@jax.custom_vjp
def low(v):
    return lax.optimization_barrier(v.astype(jnp.bfloat16)).astype(jnp.float32)

@jax.custom_vjp
def low_back(v):
    return v

def low_keep(v):
    return (low(v), None)

def low_pass(kept, grad):
    return (grad,)

def back_keep(v):
    return (v, None)

def back_low(kept, grad):
    return (low(grad),)
low.defvjp(low_keep, low_pass)
low_back.defvjp(back_keep, back_low)

def layer_norm(values, norm_gain):
    centre_tap = lax.optimization_barrier(jnp.mean(values, axis=-1, keepdims=True))
    spread = lax.optimization_barrier(jnp.mean(values * values, axis=-1, keepdims=True)) - centre_tap * centre_tap
    return (values - centre_tap) * lax.rsqrt(spread + EPS) * norm_gain

def exact_gelu_fn(values):
    return jax.nn.gelu(values, approximate=False)

def tap_masks(flags_row):
    counts = jnp.cumsum(flags_row).astype(jnp.int32)
    padded = jnp.pad(counts, (TAP_REACH, TAP_REACH), mode='edge')
    length = flags_row.shape[0]
    masks = []
    for tap_position_index in range(TAP_COUNT):
        tap_offset = DILATION_STEP * tap_position_index - TAP_REACH
        moved = lax.slice_in_dim(padded, TAP_REACH + tap_offset, TAP_REACH + tap_offset + length)
        masks.append((moved == counts).astype(jnp.float32))
    return masks

def dilated(active, kernel, masks):
    length = active.shape[0]
    padded = jnp.pad(active, ((TAP_REACH, TAP_REACH), (0, 0)))
    total = jnp.zeros((length, kernel.shape[2]), jnp.float32)
    for tap_position_index in range(TAP_COUNT):
        tap_offset = DILATION_STEP * tap_position_index - TAP_REACH
        piece = lax.slice_in_dim(padded, TAP_REACH + tap_offset, TAP_REACH + tap_offset + length, axis=0)
        piece = piece * masks[tap_position_index][:, None]
        total = total + jnp.dot(piece, kernel[tap_position_index], precision=HIGHEST)
    return total

def layer(inputs, first_proj, dilated_conv, last_proj, first_norm_gain, second_norm_gain, third_norm_gain, masks):
    outer_activation = low(exact_gelu_fn(layer_norm(inputs, first_norm_gain)))
    second_hidden = low_back(jnp.dot(outer_activation, first_proj, precision=HIGHEST))
    active_mid = low(exact_gelu_fn(layer_norm(second_hidden, second_norm_gain)))
    third_hidden = low_back(dilated(active_mid, dilated_conv, masks))
    active_last = low(exact_gelu_fn(layer_norm(third_hidden, third_norm_gain)))
    return inputs + jnp.dot(active_last, last_proj, precision=HIGHEST)

def reference(inputs, starts, first_proj, dilated_conv, last_proj, first_norm_gain, second_norm_gain, third_norm_gain, cotangent):
    params = (first_proj.astype(jnp.float32), dilated_conv.astype(jnp.float32), last_proj.astype(jnp.float32), first_norm_gain.astype(jnp.float32), second_norm_gain.astype(jnp.float32), third_norm_gain.astype(jnp.float32))

    def one_row(carry, row):
        input_row, grad_row, flag_row = row
        masks = tap_masks(flag_row)

        def forward(values, *weights):
            return layer(values, *weights, masks)
        result, pullback = jax.vjp(forward, input_row, *params)
        grads = pullback(grad_row)
        summed = tuple((total + part for total, part in zip(carry, grads[1:])))
        return (summed, (result.astype(jnp.bfloat16), grads[0].astype(jnp.bfloat16)))
    start = tuple((jnp.zeros(weight.shape, jnp.float32) for weight in params))
    totals, (outputs, grad_inputs) = lax.scan(one_row, start, (inputs.astype(jnp.float32), cotangent.astype(jnp.float32), starts.astype(jnp.int32)))
    return (outputs, grad_inputs, totals[0], totals[1], totals[2], totals[3], totals[4], totals[5])
```

```python
import functools
from types import SimpleNamespace

import jax
import jax.numpy as jnp
from jax import lax
from jax.experimental import pallas as pl
from jax.experimental.pallas import tpu as pltpu
from jax.sharding import PartitionSpec as P

MESH = pl.DeviceIdType.MESH
F32 = jnp.float32
BF16 = jnp.bfloat16

TAPS = 5
STEP = 2
REACH = 4
EPS = 1e-05
LANES = 128
RIM = 16
PAD = 8
STAGES = 4
HALF_ROOT = 0.7071067811865476
PEAK = 0.3989422804014327

NT = (((1,), (1,)), ((), ()))
OFFSETS = [STEP * k - REACH for k in range(TAPS)]


class Sizes:
    def __init__(self, mesh, inputs, starts, first_proj, cotangent):
        self.S = mesh.shape["seq"]
        self.T = mesh.shape["tp"]
        self.Z = self.T // 2
        self.R, self.N, self.D = inputs.shape
        assert self.R == self.T and self.N % LANES == 0
        self.Hs = first_proj.shape[1]
        self.H = self.Hs * self.T
        self.Hp = -(-self.Hs // 16) * 16
        self.HP = self.Hp * self.T
        assert self.HP % LANES == 0 and self.D % LANES == 0
        self.E = self.N + 2 * RIM
        self.nd = self.D // LANES
        self.nh = self.HP // LANES
        self.units = 2 * self.nd + TAPS * self.nh
        self.NR = -(-self.units // self.S)
        self.Dt = cotangent.shape[2]
        self.wide = self.Dt // LANES * LANES
        self.rem = self.Dt - self.wide
        self.fold = LANES // self.rem if self.rem else 1
        cuts = [round(i * self.NR / STAGES) for i in range(STAGES + 1)]
        self.chunks = list(zip(cuts[:-1], cuts[1:]))
        self.square = self.S == 4


def cells(ref, row, count):
    return ref[pl.ds(row, count), :]


def gelu_parts(v):
    whole = 0.5 * (1.0 + lax.erf(v * HALF_ROOT))
    slope = whole + v * (PEAK * jnp.exp(-0.5 * v * v))
    return v * whole, slope


def fold_narrow(z, part):
    rows = z.N // z.fold
    return jnp.concatenate([part[i * rows : (i + 1) * rows] for i in range(z.fold)], axis=1)


def unfold_narrow(z, part):
    return jnp.concatenate([part[:, i * z.rem : (i + 1) * z.rem] for i in range(z.fold)], axis=0)


def kernel(z, names, *refs):
    r = SimpleNamespace(**dict(zip(names, refs, strict=True)))
    S, T, Z, N, D, E, H, Hp, HP, NR = z.S, z.T, z.Z, z.N, z.D, z.E, z.H, z.Hp, z.HP, z.NR
    s, t = lax.axis_index("seq"), lax.axis_index("tp")
    core, layer = lax.rem(t, 2), t // 2
    slot = core * Z + layer
    mine = core * Z
    theirs = (1 - core) * Z
    partner = (s, t + 1 - 2 * core)

    send, recv, local = r.send, r.recv, r.local
    counts = {"remote": 0, "local": 0}
    sent = []

    def remote(src, dst, device):
        i = counts["remote"]
        counts["remote"] += 1
        return pltpu.make_async_remote_copy(
            src_ref=src,
            dst_ref=dst,
            send_sem=send.at[i],
            recv_sem=recv.at[i],
            device_id=device,
            device_id_type=MESH,
        )

    def push(src, dst, device):
        copy = remote(src, dst, device)
        copy.start()
        sent.append(copy)
        return copy

    def move(src, dst):
        i = counts["local"]
        counts["local"] += 1
        copy = pltpu.make_async_copy(src, dst, local.at[i])
        copy.start()
        return copy

    def z_at(i):
        return lax.rem(layer + i + Z, Z)

    def dev_z(i):
        return (s, 2 * z_at(i) + core)

    def seq_at(i):
        return lax.rem(s + i + S, S)

    right, left = (seq_at(1), t), (seq_at(-1), t)
    if z.square:
        sx, sy, sd = s ^ 1, s ^ 2, s ^ 3
        x_side, y_side = (sx, t), (sy, t)

    barrier = pltpu.get_barrier_semaphore()
    for i in range(1, T):
        pl.semaphore_signal(barrier, inc=1, device_id=(s, lax.rem(t + i, T)), device_id_type=MESH)
    for i in range(1, S):
        pl.semaphore_signal(barrier, inc=1, device_id=(seq_at(i), t), device_id_type=MESH)
    pl.semaphore_wait(barrier, T + S - 2)

    pack, wg = r.pack, r.wg
    along = {}
    own_core = {}
    own_local = {}
    for k, (a, b) in enumerate(z.chunks):
        for i in range(1, Z):
            along[k, i] = push(
                pack.at[s, pl.ds(a, b - a)], wg.at[s, pl.ds(a, b - a), slot], dev_z(i)
            )
        own_local[k] = move(pack.at[:, pl.ds(a, b - a)], wg.at[:, pl.ds(a, b - a), slot])
        own_core[k] = push(pack.at[:, pl.ds(a, b - a)], wg.at[:, pl.ds(a, b - a), slot], partner)
        if k == 0:
            xe = r.xe
            row_in = move(r.x.at[t], xe.at[pl.ds(RIM, N)])
            rim_r = push(r.x.at[t, pl.ds(N - RIM, RIM)], xe.at[pl.ds(0, RIM)], right)
            rim_l = push(r.x.at[t, pl.ds(0, RIM)], xe.at[pl.ds(RIM + N, RIM)], left)
            flags_r = push(r.starts, r.flags_left, right)
            flags_l = push(r.starts, r.flags_right, left)
            gain_copies = [
                push(r.gl, r.gslots.at[slot], (s, lax.rem(t + i, T))) for i in range(1, T)
            ]
            gain_own = move(r.gl, r.gslots.at[slot])

    cot = r.cot
    cot_copies, cot_local = [], []
    if z.rem:
        for row in range(T):
            r.cot_fold[row] = fold_narrow(z, cot[row, :, z.wide : z.Dt])
    for i in range(1, T):
        to = lax.rem(t + i, T)
        if z.wide:
            cot_copies.append(
                push(cot.at[to, :, pl.ds(0, z.wide)], r.cot_wide.at[t], (s, to))
            )
        if z.rem:
            cot_copies.append(push(r.cot_fold.at[to], r.cot_narrow.at[t], (s, to)))
    if z.wide:
        cot_local.append(move(cot.at[t, :, pl.ds(0, z.wide)], r.cot_wide.at[t]))
    if z.rem:
        cot_local.append(move(r.cot_fold.at[t], r.cot_narrow.at[t]))

    plane_x, plane_y, plane_d, plane_any = {}, {}, {}, {}
    across = {}

    def weights_along(k):
        a, b = z.chunks[k]
        span = pl.ds(a, b - a)
        for i in range(1, Z):
            along[k, i].wait_recv()
            place = wg.at[s, span, mine + z_at(-i)]
            if z.square:
                plane_x[k, i] = push(place, place, x_side)
                plane_y[k, i] = push(place, place, y_side)
            else:
                for j in range(1, S):
                    plane_any[k, i, j] = push(place, place, (seq_at(j), t))

    def weights_corner(k):
        a, b = z.chunks[k]
        span = pl.ds(a, b - a)
        if not z.square:
            return
        for i in range(1, Z):
            plane_x[k, i].wait_recv()
            plane_y[k, i].wait_recv()
            if (k * (Z - 1) + i) % 2:
                place = wg.at[sx, span, mine + z_at(-i)]
                plane_d[k, i] = push(place, place, y_side)
            else:
                place = wg.at[sy, span, mine + z_at(-i)]
                plane_d[k, i] = push(place, place, x_side)

    def weights_across(k):
        a, b = z.chunks[k]
        span = pl.ds(a, b - a)
        for i in range(1, Z):
            if z.square:
                plane_d[k, i].wait_recv()
            else:
                for j in range(1, S):
                    plane_any[k, i, j].wait_recv()
            place = wg.at[:, span, mine + z_at(-i)]
            across[k, i] = push(place, place, partner)

    def weights_ready(k):
        own_local[k].wait()
        own_core[k].wait_recv()
        for i in range(1, Z):
            across[k, i].wait_recv()

    def unit(ref, u):
        return ref[u % S, u // S].reshape(HP, LANES)

    def weights(first, count):
        return jnp.concatenate([unit(wg, u) for u in range(first, first + count)], axis=1)

    def first_weight():
        return weights(0, z.nd)

    def tap_weight(k):
        return weights(z.nd + k * z.nh, z.nh)

    def last_weight():
        return weights(z.nd + TAPS * z.nh, z.nd)

    flags_r.wait_recv()
    flags_l.wait_recv()
    here = r.starts[pl.ds(t, 1), :]
    before = r.flags_left[pl.ds(t, 1), :]
    after = r.flags_right[pl.ds(t, 1), :]
    window = jnp.concatenate([before[:, N - LANES :], here, after[:, :LANES]], axis=1).astype(F32)
    window = jnp.broadcast_to(window, (E, N + 2 * LANES))
    at = lax.broadcasted_iota(jnp.int32, window.shape, 1) - LANES
    place = lax.broadcasted_iota(jnp.int32, window.shape, 0) - RIM
    rows = lax.broadcasted_iota(jnp.int32, (E, 1), 0) - RIM + s * N
    for k, offset in enumerate(OFFSETS):
        low, high = min(offset, 0), max(offset, 0)
        begun = jnp.sum(
            jnp.where((at > place + low) & (at <= place + high), window, 0.0), axis=1, keepdims=True
        )
        moved = rows + offset
        inside = (begun == 0.0) & (moved >= 0) & (moved < S * N)
        r.mask[:, k : k + 1] = inside.astype(F32)

    gain_own.wait()
    for copy in gain_copies:
        copy.wait_recv()
    for j in range(T):
        r.gains[0:2, j * Hp : (j + 1) * Hp] = r.gslots[j, 0:2, :Hp]

    row_in.wait()
    rim_r.wait_recv()
    rim_l.wait_recv()

    def first_norm(i, carry):
        row = pl.multiple_of(i * 16, 16)
        v = cells(xe, row, 16).astype(F32)
        mean = jnp.sum(v, axis=1, keepdims=True) / D
        spread = jnp.sum(v * v, axis=1, keepdims=True) / D - mean * mean
        scale = lax.rsqrt(spread + EPS)
        act, slope = gelu_parts((v - mean) * scale * r.g1[0:1, :])
        r.act0[pl.ds(row, 16), :] = act.astype(BF16)
        r.slope0[pl.ds(row, 16), :] = slope
        r.mean0[pl.ds(row, 16), :] = mean
        r.scale0[pl.ds(row, 16), :] = scale
        return carry

    lax.fori_loop(0, E // 16, first_norm, 0)

    weights_along(0)
    weights_along(1)
    weights_corner(0)
    weights_along(2)
    weights_corner(1)
    weights_across(0)

    weights_ready(0)
    r.hid[...] = lax.dot_general(
        r.act0[...], first_weight(), NT, preferred_element_type=F32
    )

    weights_along(3)
    weights_corner(2)
    weights_across(1)

    def inner_norm(which, act_store):
        gain = r.gains[which : which + 1, :]
        xhat_ref, slope_ref, scale_ref = (
            (r.xhat1, r.slope1, r.scale1),
            (r.xhat2, r.slope2, r.scale2),
        )[which]

        def body(i, carry):
            row = pl.multiple_of(i * 16, 16)
            v = cells(r.hid, row, 16)
            mean = jnp.sum(v, axis=1, keepdims=True) / H
            spread = jnp.sum(v * v, axis=1, keepdims=True) / H - mean * mean
            scale = lax.rsqrt(spread + EPS)
            xhat = (v - mean) * scale
            act, slope = gelu_parts(xhat * gain)
            act_store(row, act)
            xhat_ref[pl.ds(row, 16), :] = xhat
            slope_ref[pl.ds(row, 16), :] = slope
            scale_ref[pl.ds(row, 16), :] = scale
            return carry

        lax.fori_loop(0, E // 16, body, 0)

    act1, taps = r.act1, r.taps
    act1[0:PAD, :] = jnp.zeros((PAD, HP), F32)
    act1[PAD + E :, :] = jnp.zeros((PAD, HP), F32)

    def keep_act1(row, act):
        act1[pl.ds(pl.multiple_of(row + PAD, 8), 16), :] = act.astype(BF16).astype(F32)

    inner_norm(0, keep_act1)
    for k, offset in enumerate(OFFSETS):
        taps[:, k * HP : (k + 1) * HP] = (
            act1[PAD + offset : PAD + offset + E, :] * r.mask[:, k : k + 1]
        ).astype(BF16)

    weights_corner(3)
    weights_across(2)

    weights_ready(1)
    weights_ready(2)
    total = None
    for k in range(TAPS):
        term = lax.dot_general(
            taps[:, k * HP : (k + 1) * HP], tap_weight(k), NT, preferred_element_type=F32
        )
        total = term if total is None else total + term
    r.hid[...] = total

    act2 = r.act2

    def keep_act2(row, act):
        act2[pl.ds(row, 16), :] = act.astype(BF16)

    inner_norm(1, keep_act2)
    weights_across(3)

    for copy in cot_local:
        copy.wait()
    for copy in cot_copies:
        copy.wait_recv()
    cote = r.cote
    for j in range(T):
        base = j * z.Dt
        if z.wide:
            cote[RIM : RIM + N, base : base + z.wide] = r.cot_wide[j]
        if z.rem:
            cote[RIM : RIM + N, base + z.wide : base + z.Dt] = unfold_narrow(z, r.cot_narrow[j])
    edge_r = push(cote.at[pl.ds(N, RIM)], cote.at[pl.ds(0, RIM)], right)
    edge_l = push(cote.at[pl.ds(RIM, RIM)], cote.at[pl.ds(RIM + N, RIM)], left)

    weights_ready(3)
    big = r.big
    big[...] = jnp.dot(act2[RIM : RIM + N, :], last_weight(), preferred_element_type=F32)
    big[...] = big[...] + xe[RIM : RIM + N, :].astype(F32)
    out_copies, out_local = [], []
    for j in range(T):
        base = j * z.Dt
        if z.wide:
            r.out_wide[j] = big[:, base : base + z.wide].astype(BF16)
        if z.rem:
            r.out_fold[j] = fold_narrow(z, big[:, base + z.wide : base + z.Dt]).astype(BF16)
    for i in range(1, T):
        to = lax.rem(t + i, T)
        if z.wide:
            out_copies.append(push(r.out_wide.at[to], r.got_wide.at[t], (s, to)))
        if z.rem:
            out_copies.append(push(r.out_fold.at[to], r.got_fold.at[t], (s, to)))
    if z.wide:
        out_local.append(move(r.out_wide.at[t], r.got_wide.at[t]))
    if z.rem:
        out_local.append(move(r.out_fold.at[t], r.got_fold.at[t]))

    edge_r.wait_recv()
    edge_l.wait_recv()
    r.hid[...] = lax.dot_general(cote[...], last_weight(), NT, preferred_element_type=F32)
    r.acc1[...] = jnp.zeros_like(r.acc1)
    r.acc2[...] = jnp.zeros_like(r.acc2)
    r.acc0[...] = jnp.zeros_like(r.acc0)

    def inner_norm_back(which, first, count, grad_store, acc_ref, own):
        gain = r.gains[which : which + 1, :]
        xhat_ref, slope_ref, scale_ref = (
            (r.xhat1, r.slope1, r.scale1),
            (r.xhat2, r.slope2, r.scale2),
        )[which]

        def body(i, carry):
            row = pl.multiple_of(i * 16, 16)
            xhat = cells(xhat_ref, row, 16)
            dpre = cells(r.hid, row, 16) * cells(slope_ref, row, 16)
            if own:
                dgain = dpre * xhat
                acc_ref[...] += dgain[0:8] + dgain[8:16]
            dx = dpre * gain
            plain = jnp.sum(dx, axis=1, keepdims=True) / H
            cross = jnp.sum(dx * xhat, axis=1, keepdims=True) / H
            grad_store(row, cells(scale_ref, row, 16) * (dx - plain - xhat * cross))
            return carry

        lax.fori_loop(first, first + count, body, 0)

    dhid2 = r.dhid2
    dhid2[0:PAD, :] = jnp.zeros((PAD, HP), F32)
    dhid2[PAD + E :, :] = jnp.zeros((PAD, HP), F32)

    def keep_dhid2(row, grad):
        dhid2[pl.ds(pl.multiple_of(row + PAD, 8), 16), :] = grad.astype(BF16).astype(F32)

    n16 = N // 16
    inner_norm_back(1, 0, 1, keep_dhid2, r.acc2, False)
    inner_norm_back(1, 1, n16, keep_dhid2, r.acc2, True)
    inner_norm_back(1, 1 + n16, 1, keep_dhid2, r.acc2, False)

    back = r.back
    for j, offset in enumerate(OFFSETS):
        first = PAD + RIM + offset
        back[:, j * HP : (j + 1) * HP] = (
            dhid2[first : first + N, :] * r.mask[RIM : RIM + N, j : j + 1]
        ).astype(BF16)
    total = None
    for j in range(TAPS):
        term = jnp.dot(
            back[:, j * HP : (j + 1) * HP], tap_weight(TAPS - 1 - j), preferred_element_type=F32
        )
        total = term if total is None else total + term
    r.hid[RIM : RIM + N, :] = total

    dhid1 = r.dhid1

    def keep_dhid1(row, grad):
        dhid1[pl.ds(pl.multiple_of(row - RIM, 16), 16), :] = grad.astype(BF16)

    inner_norm_back(0, 1, n16, keep_dhid1, r.acc1, True)

    big[...] = jnp.dot(dhid1[...], first_weight(), preferred_element_type=F32)

    def first_norm_back(i, carry):
        row = pl.multiple_of(i * 16, 16)
        wide = pl.multiple_of(row + RIM, 16)
        scale = cells(r.scale0, wide, 16)
        xhat = (cells(xe, wide, 16).astype(F32) - cells(r.mean0, wide, 16)) * scale
        dpre = cells(big, row, 16) * cells(r.slope0, wide, 16)
        dgain = dpre * xhat
        r.acc0[...] += dgain[0:8] + dgain[8:16]
        dx = dpre * r.g1[0:1, :]
        plain = jnp.sum(dx, axis=1, keepdims=True) / D
        cross = jnp.sum(dx * xhat, axis=1, keepdims=True) / D
        grad = scale * (dx - plain - xhat * cross)
        r.gi_own[pl.ds(row, 16), :] = (cells(cote, wide, 16).astype(F32) + grad).astype(BF16)
        return carry

    lax.fori_loop(0, n16, first_norm_back, 0)

    gi, gi_own = r.gi, r.gi_own
    own_row = move(gi_own, gi.at[t])
    to_core = push(gi_own, gi.at[t], partner)
    parts = 2
    part = N // parts
    chain = {}
    for q in range(parts):
        for way in (1, -1):
            for h in range(Z):
                row = t - 2 * way * h
                span = pl.ds(q * part, part)
                src = gi_own.at[span] if h == 0 else gi.at[row, span]
                onward = remote(src, gi.at[row, span], (s, t + 2 * way)) if h < Z - 1 else None
                sideways = remote(src, gi.at[row, span], partner) if h else None
                chain[q, way, h] = (onward, sideways)

    def has(way, h):
        return layer - h >= 0 if way == 1 else layer + h < Z

    def goes(way):
        return layer + 1 < Z if way == 1 else layer >= 1

    def chain_start(q):
        for way in (1, -1):

            @pl.when(goes(way))
            def _():
                chain[q, way, 0][0].start()

    def chain_step(q, h):
        for way in (1, -1):

            @pl.when(has(way, h))
            def _():
                chain[q, way, h - 1][0].wait_recv()
                chain[q, way, h][1].start()

            if h < Z - 1:

                @pl.when(has(way, h) & goes(way))
                def _():
                    chain[q, way, h][0].start()

    def chain_end():
        for q in range(parts):
            for way in (1, -1):
                for h in range(Z):
                    if h == 0:

                        @pl.when(goes(way))
                        def _():
                            chain[q, way, 0][0].wait_send()

                    else:

                        @pl.when(has(way, h))
                        def _():
                            chain[q, way, h][1].wait()

                        if h < Z - 1:

                            @pl.when(has(way, h) & goes(way))
                            def _():
                                chain[q, way, h][0].wait_send()

    for q in range(parts):
        chain_start(q)

    vec = r.vec
    sum0 = jnp.sum(r.acc0[...], axis=0, keepdims=True)
    sum1 = jnp.sum(r.acc1[...], axis=0, keepdims=True)
    sum2 = jnp.sum(r.acc2[...], axis=0, keepdims=True)
    vec[...] = jnp.zeros_like(vec)
    for j in range(z.nd):
        vec[j : j + 1, :] = sum0[:, j * LANES : (j + 1) * LANES]
    for j in range(z.nh):
        vec[z.nd + j : z.nd + j + 1, :] = sum1[:, j * LANES : (j + 1) * LANES]
        vec[z.nd + z.nh + j : z.nd + z.nh + j + 1, :] = sum2[:, j * LANES : (j + 1) * LANES]
    vec_plane = [push(vec, r.vec_plane.at[i], (seq_at(i), t)) for i in range(1, S)]

    g = r.g

    def grad_units(first, lhs, rhs, count):
        for j in range(0, count, 2):
            width = min(2, count - j)
            block = jnp.dot(
                lhs, rhs(j * LANES, width * LANES), preferred_element_type=F32
            ).astype(BF16)
            for i in range(width):
                u = first + j + i
                g[u % S, u // S] = block[:, i * LANES : (i + 1) * LANES].reshape(T, Hp, LANES)

    rc = r.rc
    swaps, plane1, plane2, along_back, spread_out = {}, {}, {}, {}, {}

    def swap(k):
        a, b = z.chunks[k]
        span = pl.ds(a, b - a)
        swaps[k] = push(g.at[:, span, pl.ds(theirs, Z)], rc.at[:, span], partner)

    low, high = pl.ds(0, Z // 2), pl.ds(Z // 2, Z // 2)

    def to_plane(k):
        a, b = z.chunks[k]
        span = pl.ds(a, b - a)
        swaps[k].wait_recv()
        for q in range(S):
            for n in range(a, b):
                g[q, n, pl.ds(mine, Z)] = (
                    g[q, n, pl.ds(mine, Z)].astype(F32) + rc[q, n].astype(F32)
                ).astype(BF16)
        if z.square:
            near, far = pl.ds(mine, Z // 2), pl.ds(mine + Z // 2, Z // 2)
            plane1[k] = [
                push(g.at[sx, span, near], r.rx.at[0, span], x_side),
                push(g.at[sd, span, near], r.rx.at[1, span], x_side),
                push(g.at[sy, span, far], r.ry.at[0, span], y_side),
                push(g.at[sd, span, far], r.ry.at[1, span], y_side),
            ]
        else:
            plane1[k] = [
                push(g.at[seq_at(i), span, pl.ds(mine, Z)], r.rd.at[i, span], (seq_at(i), t))
                for i in range(1, S)
            ]

    def add_into(q, n, where, count, other):
        g[q, n, pl.ds(where, count)] = (
            g[q, n, pl.ds(where, count)].astype(F32) + other.astype(F32)
        ).astype(BF16)

    def turn_plane(k):
        a, b = z.chunks[k]
        span = pl.ds(a, b - a)
        for copy in plane1[k]:
            copy.wait_recv()
        if not z.square:
            return
        half = Z // 2
        near, far = mine, mine + half
        for n in range(a, b):
            add_into(sy, n, near, half, r.rx[1, n])
            add_into(sx, n, far, half, r.ry[1, n])
        plane2[k] = [
            push(g.at[sy, span, pl.ds(near, half)], r.ry2.at[span], y_side),
            push(g.at[sx, span, pl.ds(far, half)], r.rx2.at[span], x_side),
        ]
        for n in range(a, b):
            add_into(s, n, near, half, r.rx[0, n])
            add_into(s, n, far, half, r.ry[0, n])

    def to_z(k):
        a, b = z.chunks[k]
        span = pl.ds(a, b - a)
        half = Z // 2
        if z.square:
            for copy in plane2[k]:
                copy.wait_recv()
            for n in range(a, b):
                add_into(s, n, mine, half, r.ry2[n])
                add_into(s, n, mine + half, half, r.rx2[n])
        else:
            for n in range(a, b):
                sums = g[s, n, pl.ds(mine, Z)].astype(F32)
                for i in range(1, S):
                    sums = sums + r.rd[i, n].astype(F32)
                g[s, n, pl.ds(mine, Z)] = sums.astype(BF16)
        along_back[k] = [
            push(g.at[s, span, mine + z_at(i)], r.rz.at[i, span], dev_z(i))
            for i in range(1, Z)
        ]

    ff = r.ff

    def to_all(k):
        a, b = z.chunks[k]
        span = pl.ds(a, b - a)
        for copy in along_back[k]:
            copy.wait_recv()
        for n in range(a, b):
            sums = g[s, n, slot].astype(F32)
            for i in range(1, Z):
                sums = sums + r.rz[i, n].astype(F32)
            ff[s, n] = sums.astype(BF16)
        spread_out[k] = [
            push(ff.at[s, span], ff.at[s, span], (seq_at(i), t)) for i in range(1, S)
        ]

    def all_here(k):
        for copy in spread_out[k]:
            copy.wait_recv()

    for u in range(z.units, S * NR):
        g[u % S, u // S] = jnp.zeros((T, Hp, LANES), BF16)
    own = slice(RIM, RIM + N)
    act2_t = act2[own, :].astype(F32).T.astype(BF16)
    grad_units(z.nd + TAPS * z.nh, act2_t, lambda c, w: cote[own, c : c + w], z.nd)
    swap(3)
    dhid2_t = dhid2[PAD + RIM : PAD + RIM + N, :].T.astype(BF16)
    grad_units(z.nd, dhid2_t, lambda c, w: taps[own, c : c + w], TAPS * z.nh)
    swap(2)
    swap(1)
    to_plane(3)
    dhid1_t = dhid1[...].astype(F32).T.astype(BF16)
    grad_units(0, dhid1_t, lambda c, w: r.act0[own, c : c + w], z.nd)
    swap(0)
    to_plane(2)

    chain_step(0, 1)
    turn_plane(3)
    to_plane(1)
    chain_step(1, 1)

    for copy in vec_plane:
        copy.wait_recv()
    vec_sum = r.vec_sum
    vec_sum[...] = sum((r.vec_plane[i] for i in range(1, S)), vec[...])
    vec_z = [push(vec_sum, r.vec_z.at[i - 1], dev_z(i)) for i in range(1, Z)]

    turn_plane(2)
    to_z(3)
    to_plane(0)
    if Z > 2:
        chain_step(0, 2)
    turn_plane(1)
    to_z(2)
    to_all(3)
    if Z > 2:
        chain_step(1, 2)

    for copy in vec_z:
        copy.wait_recv()
    vec_pair = r.vec_pair
    vec_pair[0] = sum((r.vec_z[i - 1] for i in range(1, Z)), vec_sum[...])
    vec_core = push(vec_pair.at[0], vec_pair.at[1], partner)

    turn_plane(0)
    to_z(1)
    to_all(2)
    for h in range(3, Z):
        chain_step(0, h)
    to_z(0)
    to_all(1)
    all_here(3)
    for h in range(3, Z):
        chain_step(1, h)
    to_all(0)
    for k in range(3):
        all_here(k)

    vec_core.wait_recv()
    gain_sums = vec_pair[0] + vec_pair[1]

    def line(first, count):
        return jnp.concatenate([gain_sums[j : j + 1, :] for j in range(first, first + count)], axis=1)

    def picked(row, width, step, index, count):
        return sum(
            jnp.where(index == j, row[:, j * step : j * step + width], 0.0) for j in range(count)
        )

    r.grad_gain[...] = picked(line(0, z.nd), z.Dt, z.Dt, t, T)
    r.grad_gain1[...] = picked(line(z.nd, z.nh), z.Hs, Hp, slot, T)
    r.grad_gain2[...] = picked(line(z.nd + z.nh, z.nh), z.Hs, Hp, slot, T)

    def summed(first, count):
        return jnp.concatenate(
            [ff[u % S, u // S].astype(F32) for u in range(first, first + count)], axis=1
        )

    r.grad_first[...] = summed(0, z.nd).T[:, : z.Hs]
    r.grad_last[...] = summed(z.nd + TAPS * z.nh, z.nd)[: z.Hs]
    for k in range(TAPS):
        turned = summed(z.nd + k * z.nh, z.nh).T[:, : z.Hs]
        for j in range(T):
            to = 2 * (j % Z) + j // Z
            r.grad_conv[k, to * z.Hs : (to + 1) * z.Hs, :] = turned[j * Hp : j * Hp + z.Hs, :]

    for copy in out_local:
        copy.wait()
    for copy in out_copies:
        copy.wait_recv()
    for row in range(T):
        if z.wide:
            r.out[row, :, 0 : z.wide] = r.got_wide[row]
        if z.rem:
            r.out[row, :, z.wide : z.Dt] = unfold_narrow(z, r.got_fold[row])

    to_core.wait_recv()
    own_row.wait()
    chain_end()
    for copy in sent:
        copy.wait_send()


def packed_weights(z, first_proj, dilated_conv, last_proj):
    more = z.Hp - z.Hs

    def rows(cells_):
        return jnp.pad(cells_, ((0, more), (0, 0)))

    first = rows(first_proj.T)
    conv = dilated_conv.reshape(TAPS, z.Z, 2, z.Hs, z.Hs).transpose(0, 4, 2, 1, 3)
    conv = jnp.pad(conv, ((0, 0), (0, more), (0, 0), (0, 0), (0, more)))
    conv = conv.reshape(TAPS, z.Hp, z.nh, LANES).transpose(0, 2, 1, 3)
    units = jnp.concatenate(
        [
            first.reshape(z.Hp, z.nd, LANES).transpose(1, 0, 2),
            conv.reshape(TAPS * z.nh, z.Hp, LANES),
            rows(last_proj).reshape(z.Hp, z.nd, LANES).transpose(1, 0, 2),
            jnp.zeros((z.S * z.NR - z.units, z.Hp, LANES), BF16),
        ]
    )
    return units.reshape(z.NR, z.S, z.Hp, LANES).transpose(1, 0, 2, 3)


def shards(
    mesh,
    inputs,
    starts,
    first_proj,
    dilated_conv,
    last_proj,
    first_norm_gain,
    second_norm_gain,
    third_norm_gain,
    cotangent,
):
    z = Sizes(mesh, inputs, starts, first_proj, cotangent)
    S, T, Z, N, D, E, HP, Hp, NR = z.S, z.T, z.Z, z.N, z.D, z.E, z.HP, z.Hp, z.NR
    pack = packed_weights(z, first_proj, dilated_conv, last_proj)
    gains = jnp.pad(
        jnp.stack([second_norm_gain, third_norm_gain]), ((0, 6), (0, LANES - z.Hs))
    )
    vm, anywhere = pltpu.VMEM, pl.ANY
    ins = dict(
        x=(inputs, anywhere),
        starts=(starts, vm),
        pack=(pack, anywhere),
        gl=(gains, vm),
        g1=(first_norm_gain.reshape(1, D), vm),
        cot=(cotangent, vm),
    )
    outs = dict(
        out=((z.R, N, z.Dt), BF16, vm),
        gi=((z.R, N, D), BF16, anywhere),
        grad_first=((D, z.Hs), F32, vm),
        grad_conv=((TAPS, z.H, z.Hs), F32, vm),
        grad_last=((z.Hs, D), F32, vm),
        grad_gain=((1, z.Dt), F32, vm),
        grad_gain1=((1, z.Hs), F32, vm),
        grad_gain2=((1, z.Hs), F32, vm),
    )
    fold_rows, fold_cols = N // z.fold, max(z.rem * z.fold, 1)
    wide = max(z.wide, 1)
    scratch = dict(
        send=pltpu.SemaphoreType.DMA((400,)),
        recv=pltpu.SemaphoreType.DMA((400,)),
        local=pltpu.SemaphoreType.DMA((16,)),
        xe=vm((E, D), BF16),
        cote=vm((E, D), BF16),
        act0=vm((E, D), BF16),
        slope0=vm((E, D), F32),
        mean0=vm((E, 1), F32),
        scale0=vm((E, 1), F32),
        mask=vm((E, LANES), F32),
        flags_left=vm((z.R, N), jnp.int32),
        flags_right=vm((z.R, N), jnp.int32),
        gslots=vm((T, 8, LANES), F32),
        gains=vm((8, HP), F32),
        wg=vm((S, NR, T, Hp, LANES), BF16),
        hid=vm((E, HP), F32),
        xhat1=vm((E, HP), F32),
        slope1=vm((E, HP), F32),
        scale1=vm((E, 1), F32),
        xhat2=vm((E, HP), F32),
        slope2=vm((E, HP), F32),
        scale2=vm((E, 1), F32),
        act1=vm((E + 2 * PAD, HP), F32),
        dhid2=vm((E + 2 * PAD, HP), F32),
        taps=vm((E, TAPS * HP), BF16),
        back=vm((N, TAPS * HP), BF16),
        act2=vm((E, HP), BF16),
        dhid1=vm((N, HP), BF16),
        big=vm((N, D), F32),
        gi_own=vm((N, D), BF16),
        acc0=vm((8, D), F32),
        acc1=vm((8, HP), F32),
        acc2=vm((8, HP), F32),
        cot_fold=vm((T, fold_rows, fold_cols), BF16),
        cot_wide=vm((T, N, wide), BF16),
        cot_narrow=vm((T, fold_rows, fold_cols), BF16),
        out_wide=vm((T, N, wide), BF16),
        out_fold=vm((T, fold_rows, fold_cols), BF16),
        got_wide=vm((T, N, wide), BF16),
        got_fold=vm((T, fold_rows, fold_cols), BF16),
        g=vm((S, NR, T, Hp, LANES), BF16),
        rc=vm((S, NR, Z, Hp, LANES), BF16),
        rz=vm((Z, NR, Hp, LANES), BF16),
        ff=vm((S, NR, Hp, LANES), BF16),
        vec=vm((24, LANES), F32),
        vec_sum=vm((24, LANES), F32),
        vec_plane=vm((S, 24, LANES), F32),
        vec_z=vm((Z, 24, LANES), F32),
        vec_pair=vm((2, 24, LANES), F32),
    )
    if z.square:
        scratch.update(rx=vm((2, NR, Z // 2, Hp, LANES), BF16))
        scratch.update(ry=vm((2, NR, Z // 2, Hp, LANES), BF16))
        scratch.update(rx2=vm((NR, Z // 2, Hp, LANES), BF16))
        scratch.update(ry2=vm((NR, Z // 2, Hp, LANES), BF16))
    else:
        scratch.update(rd=vm((S, NR, Z, Hp, LANES), BF16))
    names = [*ins, *outs, *scratch]
    results = pl.pallas_call(
        functools.partial(kernel, z, names),
        out_shape=[jax.ShapeDtypeStruct(shape, kind) for shape, kind, _ in outs.values()],
        in_specs=[pl.BlockSpec(memory_space=space) for _, space in ins.values()],
        out_specs=[pl.BlockSpec(memory_space=space) for *_, space in outs.values()],
        scratch_shapes=list(scratch.values()),
        compiler_params=pltpu.CompilerParams(
            collective_id=0, has_side_effects=True, vmem_limit_bytes=63 * 2**20
        ),
    )(*[array for array, _ in ins.values()])
    out, gi, grad_first, grad_conv, grad_last, grad_gain, grad_gain1, grad_gain2 = results
    return (
        out,
        gi,
        grad_first,
        grad_conv,
        grad_last,
        grad_gain.reshape(-1),
        grad_gain1.reshape(-1),
        grad_gain2.reshape(-1),
    )


def solution(mesh):
    placed = (
        P(None, "seq", None),
        P(None, "seq"),
        P(None, "tp"),
        P(None, None, "tp"),
        P("tp", None),
        P(),
        P("tp"),
        P("tp"),
        P(None, "seq", "tp"),
    )
    return jax.shard_map(
        functools.partial(shards, mesh),
        mesh=mesh,
        in_specs=placed,
        out_specs=(
            P(None, "seq", "tp"),
            P(None, "seq", None),
            P(None, "tp"),
            P(None, None, "tp"),
            P("tp", None),
            P("tp"),
            P("tp"),
            P("tp"),
        ),
        check_vma=False,
    )
```

```python
import functools
from types import SimpleNamespace

import jax
import jax.numpy as jnp
from jax import lax
from jax.experimental import pallas as pl
from jax.experimental.pallas import tpu as pltpu
from jax.sharding import PartitionSpec as P

MESH = pl.DeviceIdType.MESH
F32 = jnp.float32
BF16 = jnp.bfloat16

TAPS = 5
STEP = 2
REACH = 4
EPS = 1e-05
LANES = 128
RIM = 16
PAD = 8
STAGES = 4
BLOCK = 32
HALF_ROOT = 0.7071067811865476
PEAK = 0.3989422804014327

NT = (((1,), (1,)), ((), ()))
OFFSETS = [STEP * k - REACH for k in range(TAPS)]


class Sizes:
    def __init__(self, mesh, inputs, starts, first_proj, cotangent):
        self.S = mesh.shape["seq"]
        self.T = mesh.shape["tp"]
        self.Z = self.T // 2
        self.R, self.N, self.D = inputs.shape
        assert self.R == self.T and self.N % LANES == 0
        self.Hs = first_proj.shape[1]
        self.H = self.Hs * self.T
        self.Hp = -(-self.Hs // 16) * 16
        self.HP = self.Hp * self.T
        assert self.HP % LANES == 0 and self.D % LANES == 0
        self.E = self.N + 2 * RIM
        self.nd = self.D // LANES
        self.nh = self.HP // LANES
        self.units = 2 * self.nd + TAPS * self.nh
        self.NR = -(-self.units // self.S)
        self.Dt = cotangent.shape[2]
        assert self.Dt % 16 == 0
        cuts = [round(i * self.NR / STAGES) for i in range(STAGES + 1)]
        self.chunks = list(zip(cuts[:-1], cuts[1:]))
        self.square = self.S == 4
        self.line = self.Z == 4


def cells(ref, row, count):
    return ref[pl.ds(row, count), :]


def gelu_parts(v):
    whole = 0.5 * (1.0 + lax.erf(v * HALF_ROOT))
    slope = whole + v * (PEAK * jnp.exp(-0.5 * v * v))
    return v * whole, slope


def kernel(z, names, *refs):
    r = SimpleNamespace(**dict(zip(names, refs, strict=True)))
    S, T, Z, N, D, E, H, Hp, HP, NR = z.S, z.T, z.Z, z.N, z.D, z.E, z.H, z.Hp, z.HP, z.NR
    s, t = lax.axis_index("seq"), lax.axis_index("tp")
    core, layer = lax.rem(t, 2), t // 2
    partner = (s, t + 1 - 2 * core)

    send, recv, local = r.send, r.recv, r.local
    counts = [0, 0, 0]
    sent, sent_if = [], []

    def remote(src, dst, device, arrival=None):
        counts[0] += 1
        return pltpu.make_async_remote_copy(
            src_ref=src,
            dst_ref=dst,
            send_sem=send.at[counts[0] - 1],
            recv_sem=recv.at[arrivals(1) if arrival is None else arrival],
            device_id=device,
            device_id_type=MESH,
        )

    def arrivals(count):
        counts[1] += count
        return counts[1] - count

    def arrived(arrival, place):
        pltpu.make_async_remote_copy(
            src_ref=place,
            dst_ref=place,
            send_sem=send.at[0],
            recv_sem=recv.at[arrival],
            device_id=partner,
            device_id_type=MESH,
        ).wait_recv()

    def push(src, dst, device, arrival=None):
        copy = remote(src, dst, device, arrival)
        copy.start()
        sent.append(copy)
        return copy

    def push_if(when, copy):
        @pl.when(when)
        def _():
            copy.start()

        sent_if.append((when, copy))

    def move(src, dst):
        counts[2] += 1
        copy = pltpu.make_async_copy(src, dst, local.at[counts[2] - 1])
        copy.start()
        return copy

    def z_at(i):
        return lax.rem(layer + i + Z, Z)

    def dev_z(i):
        return (s, 2 * z_at(i) + core)

    def seq_at(i):
        return lax.rem(s + i + S, S)

    steps = range(1, Z)
    if z.line:
        upper = layer // 2
        inner = lax.rem((layer + 1) // 2, 2)
        end, middle = 3 * upper, 1 + upper
        first = inner * (3 - layer) + (1 - inner) * middle
        second = inner * end + (1 - inner) * (3 - middle)
        origins = [None, first, second, 3 - end]
        own_to = [(first, 2 - inner), (second, 3 - 2 * inner)]
        passed = {1: (end, 2), 3: (end, 3)}
        passed_all = {**passed, 2: (3 - layer, 3)}
    else:
        origins = [None] + [z_at(-i) for i in steps]
        own_to = [(z_at(i), i) for i in steps]
        passed, passed_all, inner = {}, {}, 0

    def at_layer(to):
        return (s, 2 * to + core)

    def take(base, j, place, onward, at_end, passing):
        if base + j not in onwards:
            extra = None
            if j in passing:
                to, then = passing[j]
                extra = remote(place, place, at_layer(to), base + then)
                sent_if.append((inner == 1, extra))
            onwards[base + j] = (extra, onward(j, place))
            sent.extend(onwards[base + j][1])

        def go():
            extra, copies = onwards[base + j]
            arrived(base + j, place)
            if extra is not None and not at_end:
                extra.start()
            for copy in copies:
                copy.start()

        if z.line:
            pl.when(inner == 1 - at_end)(go)
        elif at_end:
            go()

    onwards = {}
    right, left = (seq_at(1), t), (seq_at(-1), t)
    if z.square:
        sx, sy, sd = s ^ 1, s ^ 2, s ^ 3
        x_side, y_side = (sx, t), (sy, t)

    xe, cot, cot_t = r.xe, r.cot, r.cot_t

    def features(who):
        return pl.ds(pl.multiple_of(who * z.Dt, 16), z.Dt)

    weights_in = [move(r.w1, r.w1_in), move(r.wc, r.wc_in), move(r.w3, r.w3_in)]
    row_in = move(r.x.at[t], xe.at[pl.ds(RIM, N)])
    cot_own = move(cot.at[t], cot_t.at[features(t)])

    barrier = pltpu.get_barrier_semaphore()
    for i in range(1, T):
        pl.semaphore_signal(barrier, inc=1, device_id=(s, lax.rem(t + i, T)), device_id_type=MESH)
    for i in range(1, S):
        pl.semaphore_signal(barrier, inc=1, device_id=(seq_at(i), t), device_id_type=MESH)
    pl.semaphore_wait(barrier, T + S - 2)

    rim_r = push(r.x.at[t, pl.ds(N - RIM, RIM)], xe.at[pl.ds(0, RIM)], right)
    rim_l = push(r.x.at[t, pl.ds(0, RIM)], xe.at[pl.ds(RIM + N, RIM)], left)
    flags_r = push(r.starts, r.flags_left, right)
    flags_l = push(r.starts, r.flags_right, left)
    r.gl[0:1, : z.Hs] = r.g2[...]
    r.gl[1:2, : z.Hs] = r.g3[...]
    gain_copies = [push(r.gl, r.gslots.at[t], (s, lax.rem(t + i, T))) for i in range(1, T)]
    gain_own = move(r.gl, r.gslots.at[t])

    wg = r.wg
    bases, own_core = {}, {}
    plane_x, plane_y, plane_d, plane_any, across = {}, {}, {}, {}, {}

    def unit_in(u):
        if u < z.nd:
            return r.w1_in[:, u * LANES : (u + 1) * LANES]
        u -= z.nd
        if u < TAPS * z.nh:
            return r.wc_in[u // z.nh, :, u % z.nh * LANES : (u % z.nh + 1) * LANES]
        u -= TAPS * z.nh
        if u < z.nd:
            return r.w3_in[:, u * LANES : (u + 1) * LANES]
        return jnp.zeros((Hp, LANES), BF16)

    def rounds(k):
        a, b = z.chunks[k]
        return pl.ds(a, b - a)

    def weights_own(k):
        for q in range(S):
            for n in range(*z.chunks[k]):
                wg[q, n, layer, core] = unit_in(n * S + q)
        place = wg.at[s, rounds(k), layer, core]
        bases[k] = arrivals(Z)
        for to, j in own_to:
            push(place, place, at_layer(to), bases[k] + j)
        place = wg.at[:, rounds(k), layer, core]
        own_core[k] = push(place, place, partner)

    def weights_along(k, at_end, js=steps):
        def onward(j, place):
            if not z.square:
                plane_any[k, j] = [remote(place, place, (seq_at(i), t)) for i in range(1, S)]
                return plane_any[k, j]
            plane_x[k, j] = remote(place, place, x_side)
            plane_y[k, j] = remote(place, place, y_side)
            return [plane_x[k, j], plane_y[k, j]]

        for j in js:
            take(bases[k], j, wg.at[s, rounds(k), origins[j], core], onward, at_end, passed)

    def weights_corner(k):
        if not z.square:
            return
        for j in steps:
            across[k, j] = []
            over_y = (k + j) % 2
            place = wg.at[sx if over_y else sy, rounds(k), origins[j], core]
            plane_x[k, j].wait_recv()
            plane_y[k, j].wait_recv()
            plane_d[k, j] = push(place, place, y_side if over_y else x_side)
            for q in (s, sx, sy):
                place = wg.at[q, rounds(k), origins[j], core]
                across[k, j].append(push(place, place, partner))

    def weights_across(k):
        for j in steps:
            if z.square:
                plane_d[k, j].wait_recv()
                place = wg.at[sd, rounds(k), origins[j], core]
                across[k, j].append(push(place, place, partner))
            else:
                for copy in plane_any[k, j]:
                    copy.wait_recv()
                place = wg.at[:, rounds(k), origins[j], core]
                across[k, j] = [push(place, place, partner)]

    def weights_ready(k):
        own_core[k].wait_recv()
        for j in steps:
            for copy in across[k, j]:
                copy.wait_recv()

    cot_copies = []

    def cotangent_out():
        for i in range(1, T):
            to = lax.rem(t + i, T)
            cot_copies.append(push(cot.at[to], cot_t.at[features(t)], (s, to)))

    weights_in[0].wait()
    weights_in[1].wait()
    weights_own(0)
    weights_own(1)
    weights_in[2].wait()
    weights_own(2)
    weights_own(3)
    for k in range(STAGES):
        weights_along(k, False)
        weights_along(k, True, [1])

    def unit(ref, u):
        return ref[u % S, u // S].reshape(HP, LANES)

    def weights(first, count):
        return jnp.concatenate([unit(wg, u) for u in range(first, first + count)], axis=1)

    def first_weight():
        return weights(0, z.nd)

    def tap_weight(k):
        return weights(z.nd + k * z.nh, z.nh)

    def last_weight():
        return weights(z.nd + TAPS * z.nh, z.nd)

    row_in.wait()
    rim_r.wait_recv()
    rim_l.wait_recv()

    gain0 = jnp.concatenate([r.g1[j : j + 1, :] for j in range(z.nd)], axis=1)

    def first_norm(i, carry):
        row = pl.multiple_of(i * BLOCK, BLOCK)
        v = cells(xe, row, BLOCK).astype(F32)
        mean = jnp.sum(v, axis=1, keepdims=True) / D
        spread = jnp.sum(v * v, axis=1, keepdims=True) / D - mean * mean
        scale = lax.rsqrt(spread + EPS)
        act, slope = gelu_parts((v - mean) * scale * gain0)
        r.act0[pl.ds(row, BLOCK), :] = act.astype(BF16)
        r.slope0[pl.ds(row, BLOCK), :] = slope
        r.mean0[pl.ds(row, BLOCK), :] = mean
        r.scale0[pl.ds(row, BLOCK), :] = scale
        return carry

    lax.fori_loop(0, E // BLOCK, first_norm, 0)

    gain_own.wait()
    for copy in gain_copies:
        copy.wait_recv()
    for j in range(T):
        r.gains[0:2, j * Hp : (j + 1) * Hp] = r.gslots[j, 0:2, :Hp]

    flags_r.wait_recv()
    flags_l.wait_recv()
    here = r.starts[pl.ds(t, 1), :]
    before = r.flags_left[pl.ds(t, 1), :]
    after = r.flags_right[pl.ds(t, 1), :]
    window = jnp.concatenate([before[:, N - LANES :], here, after[:, :LANES]], axis=1).astype(F32)
    window = jnp.broadcast_to(window, (E, N + 2 * LANES))
    at = lax.broadcasted_iota(jnp.int32, window.shape, 1) - LANES
    place = lax.broadcasted_iota(jnp.int32, window.shape, 0) - RIM
    rows = lax.broadcasted_iota(jnp.int32, (E, 1), 0) - RIM + s * N
    for k, offset in enumerate(OFFSETS):
        low, high = min(offset, 0), max(offset, 0)
        begun = jnp.sum(
            jnp.where((at > place + low) & (at <= place + high), window, 0.0), axis=1, keepdims=True
        )
        moved = rows + offset
        inside = (begun == 0.0) & (moved >= 0) & (moved < S * N)
        r.mask[:, k : k + 1] = inside.astype(F32)

    weights_along(0, True, steps[1:])
    weights_along(1, True, steps[1:])
    weights_corner(0)
    weights_along(2, True, steps[1:])
    weights_corner(1)
    cotangent_out()
    weights_along(3, True, steps[1:])
    weights_corner(2)
    weights_across(0)
    weights_corner(3)

    weights_ready(0)
    r.hid[...] = lax.dot_general(r.act0[...], first_weight(), NT, preferred_element_type=F32)
    weights_across(1)

    def inner_norm(which, act_store):
        gain = r.gains[which : which + 1, :]
        xhat_ref, slope_ref, scale_ref = (
            (r.xhat1, r.slope1, r.scale1),
            (r.xhat2, r.slope2, r.scale2),
        )[which]

        def body(i, carry):
            row = pl.multiple_of(i * BLOCK, BLOCK)
            v = cells(r.hid, row, BLOCK)
            mean = jnp.sum(v, axis=1, keepdims=True) / H
            spread = jnp.sum(v * v, axis=1, keepdims=True) / H - mean * mean
            scale = lax.rsqrt(spread + EPS)
            xhat = (v - mean) * scale
            act, slope = gelu_parts(xhat * gain)
            act_store(row, act)
            xhat_ref[pl.ds(row, BLOCK), :] = xhat
            slope_ref[pl.ds(row, BLOCK), :] = slope
            scale_ref[pl.ds(row, BLOCK), :] = scale
            return carry

        lax.fori_loop(0, E // BLOCK, body, 0)

    act1, taps = r.act1, r.taps
    act1[0:PAD, :] = jnp.zeros((PAD, HP), F32)
    act1[PAD + E :, :] = jnp.zeros((PAD, HP), F32)

    def keep_act1(row, act):
        act1[pl.ds(pl.multiple_of(row + PAD, 8), BLOCK), :] = act.astype(BF16).astype(F32)

    inner_norm(0, keep_act1)
    for k, offset in enumerate(OFFSETS):
        taps[:, k * HP : (k + 1) * HP] = (
            act1[PAD + offset : PAD + offset + E, :] * r.mask[:, k : k + 1]
        ).astype(BF16)

    weights_across(2)

    weights_ready(1)
    weights_ready(2)
    total = None
    for k in range(TAPS):
        if k == TAPS - 2:
            weights_across(3)
        term = lax.dot_general(
            taps[:, k * HP : (k + 1) * HP], tap_weight(k), NT, preferred_element_type=F32
        )
        total = term if total is None else total + term
    r.hid[...] = total

    cot_own.wait()
    for copy in cot_copies:
        copy.wait_recv()
    cote = r.cote
    cote[RIM : RIM + N, :] = cot_t[...].T
    edge_r = push(cote.at[pl.ds(N, RIM)], cote.at[pl.ds(0, RIM)], right)
    edge_l = push(cote.at[pl.ds(RIM, RIM)], cote.at[pl.ds(RIM + N, RIM)], left)

    act2 = r.act2

    def keep_act2(row, act):
        act2[pl.ds(row, BLOCK), :] = act.astype(BF16)

    inner_norm(1, keep_act2)

    weights_ready(3)
    big = r.big
    big[...] = jnp.dot(act2[RIM : RIM + N, :], last_weight(), preferred_element_type=F32)
    out_t = r.out_t
    out_t[...] = (big[...] + xe[RIM : RIM + N, :].astype(F32)).astype(BF16).T
    out_copies = []
    for i in range(1, T):
        to = lax.rem(t + i, T)
        out_copies.append(push(out_t.at[features(to)], r.out.at[t], (s, to)))
    out_own = move(out_t.at[features(t)], r.out.at[t])

    g = r.g

    def grad_units(first, lhs, rhs, count):
        for j in range(0, count, 2):
            width = min(2, count - j)
            block = jnp.dot(
                lhs, rhs(j * LANES, width * LANES), preferred_element_type=F32
            ).astype(BF16)
            for i in range(width):
                u = first + j + i
                g[u % S, u // S] = block[:, i * LANES : (i + 1) * LANES].reshape(Z, 2, Hp, LANES)

    rc = r.rc
    swaps, plane1, plane2, along_back, spread_out = {}, {}, {}, {}, {}
    beside, over, own_sums = {}, {}, []

    def swap(k):
        a, b = z.chunks[k]
        span = pl.ds(a, b - a)
        swaps[k] = push(g.at[:, span, :, 1 - core], rc.at[:, span], partner)

    near, far = pl.ds(0, Z // 2), pl.ds(Z // 2, Z // 2)

    def to_plane(k):
        a, b = z.chunks[k]
        span = pl.ds(a, b - a)
        swaps[k].wait_recv()
        for q in range(S):
            for n in range(a, b):
                g[q, n, :, core] = (g[q, n, :, core].astype(F32) + rc[q, n].astype(F32)).astype(BF16)
        if z.square:
            plane1[k] = [
                push(g.at[sx, span, near, core], r.rx.at[0, span], x_side),
                push(g.at[sd, span, near, core], r.rx.at[1, span], x_side),
                push(g.at[sy, span, far, core], r.ry.at[0, span], y_side),
                push(g.at[sd, span, far, core], r.ry.at[1, span], y_side),
            ]
        else:
            plane1[k] = [
                push(g.at[seq_at(i), span, :, core], r.rd.at[i, span], (seq_at(i), t))
                for i in range(1, S)
            ]

    def add_into(q, n, where, other):
        g[q, n, where, core] = (g[q, n, where, core].astype(F32) + other.astype(F32)).astype(BF16)

    def turn_plane(k):
        a, b = z.chunks[k]
        span = pl.ds(a, b - a)
        for copy in plane1[k]:
            copy.wait_recv()
        if not z.square:
            return
        for n in range(a, b):
            add_into(sy, n, near, r.rx[1, n])
            add_into(sx, n, far, r.ry[1, n])
        plane2[k] = [
            push(g.at[sy, span, near, core], r.ry2.at[span], y_side),
            push(g.at[sx, span, far, core], r.rx2.at[span], x_side),
        ]
        for n in range(a, b):
            add_into(s, n, near, r.rx[0, n])
            add_into(s, n, far, r.ry[0, n])

    def to_z(k):
        a, b = z.chunks[k]
        span = pl.ds(a, b - a)
        if z.square:
            for copy in plane2[k]:
                copy.wait_recv()
            for n in range(a, b):
                add_into(s, n, near, r.ry2[n])
                add_into(s, n, far, r.rx2[n])
        else:
            for n in range(a, b):
                sums = g[s, n, :, core].astype(F32)
                for i in range(1, S):
                    sums = sums + r.rd[i, n].astype(F32)
                g[s, n, :, core] = sums.astype(BF16)

    def z_start(k):
        if z.line:
            beside[k] = arrivals(1)
            copy = remote(
                g.at[s, rounds(k), pl.ds(1 - upper, 3), core],
                r.rz_end.at[rounds(k)],
                at_layer(middle),
                beside[k],
            )
            push_if(inner == 0, copy)
        else:
            along_back[k] = [
                push(g.at[s, rounds(k), z_at(i), core], r.rz.at[i, rounds(k)], dev_z(i))
                for i in steps
            ]

    def z_over(k):
        if z.line:
            over[k] = arrivals(1)
            pair = pl.ds(2 - 2 * upper, 2)
            copy = remote(
                g.at[s, rounds(k), pair, core], r.rz_pair.at[rounds(k)], at_layer(3 - layer), over[k]
            )
            sent_if.append((inner == 1, copy))

            @pl.when(inner == 1)
            def _():
                arrived(beside[k], r.rz_end.at[rounds(k)])
                for n in range(*z.chunks[k]):
                    add_into(s, n, pair, r.rz_end[n, pl.ds(1 - upper, 2)])
                copy.start()

    def z_middle(k):
        if z.line:
            along_back[k] = remote(
                g.at[s, rounds(k), end, core], r.rz_one.at[rounds(k)], at_layer(end)
            )
            sent_if.append((inner == 1, along_back[k]))

            @pl.when(inner == 1)
            def _():
                arrived(over[k], r.rz_pair.at[rounds(k)])
                for n in range(*z.chunks[k]):
                    add_into(s, n, pl.ds(2 * upper, 2), r.rz_pair[n])
                along_back[k].start()
                for n in range(*z.chunks[k]):
                    sums = g[s, n, layer, core].astype(F32) + r.rz_end[n, 2 * upper].astype(F32)
                    r.ff_own[n] = sums.astype(BF16)

    def to_all(k):
        a, b = z.chunks[k]
        span = pl.ds(a, b - a)
        if z.line:

            @pl.when(inner == 0)
            def _():
                along_back[k].wait_recv()
                for n in range(a, b):
                    sums = g[s, n, layer, core].astype(F32) + r.rz_one[n].astype(F32)
                    r.ff_own[n] = sums.astype(BF16)
        else:
            for copy in along_back[k]:
                copy.wait_recv()
            for n in range(a, b):
                sums = g[s, n, layer, core].astype(F32)
                for i in steps:
                    sums = sums + r.rz[i, n].astype(F32)
                r.ff_own[n] = sums.astype(BF16)
        spread_out[k] = [
            push(r.ff_own.at[span], r.ff.at[s, span], (seq_at(i), t)) for i in range(1, S)
        ]
        own_sums.append(move(r.ff_own.at[span], r.ff.at[s, span]))

    def all_here(k):
        for copy in spread_out[k]:
            copy.wait_recv()

    for u in range(z.units, S * NR):
        g[u % S, u // S] = jnp.zeros((Z, 2, Hp, LANES), BF16)
    own = slice(RIM, RIM + N)
    act2_t = act2[own, :].astype(F32).T.astype(BF16)
    grad_units(z.nd + TAPS * z.nh, act2_t, lambda c, w: cote[own, c : c + w], z.nd)
    swap(3)
    edge_r.wait_recv()
    edge_l.wait_recv()
    r.hid[...] = lax.dot_general(cote[...], last_weight(), NT, preferred_element_type=F32)
    r.acc1[...] = jnp.zeros_like(r.acc1)
    r.acc2[...] = jnp.zeros_like(r.acc2)
    r.acc0[...] = jnp.zeros_like(r.acc0)

    def inner_norm_back(which, first, count, size, grad_store, acc_ref=None):
        gain = r.gains[which : which + 1, :]
        xhat_ref, slope_ref, scale_ref = (
            (r.xhat1, r.slope1, r.scale1),
            (r.xhat2, r.slope2, r.scale2),
        )[which]

        def body(i, carry):
            row = pl.multiple_of(first + i * size, 16)
            xhat = cells(xhat_ref, row, size)
            dpre = cells(r.hid, row, size) * cells(slope_ref, row, size)
            if acc_ref is not None:
                dgain = dpre * xhat
                acc_ref[...] += sum(dgain[n : n + 8] for n in range(0, size, 8))
            dx = dpre * gain
            plain = jnp.sum(dx, axis=1, keepdims=True) / H
            cross = jnp.sum(dx * xhat, axis=1, keepdims=True) / H
            grad_store(row, cells(scale_ref, row, size) * (dx - plain - xhat * cross))
            return carry

        lax.fori_loop(0, count, body, 0)

    dhid2 = r.dhid2
    dhid2[0:PAD, :] = jnp.zeros((PAD, HP), F32)
    dhid2[PAD + E :, :] = jnp.zeros((PAD, HP), F32)

    def keep_dhid2(row, grad):
        dhid2[pl.ds(pl.multiple_of(row + PAD, 8), grad.shape[0]), :] = grad.astype(BF16).astype(F32)

    inner_norm_back(1, 0, 1, RIM, keep_dhid2)
    inner_norm_back(1, RIM, N // BLOCK, BLOCK, keep_dhid2, r.acc2)
    inner_norm_back(1, RIM + N, 1, RIM, keep_dhid2)

    back = r.back
    for j, offset in enumerate(OFFSETS):
        first = PAD + RIM + offset
        back[:, j * HP : (j + 1) * HP] = (
            dhid2[first : first + N, :] * r.mask[RIM : RIM + N, j : j + 1]
        ).astype(BF16)
    total = None
    for j in range(TAPS):
        term = jnp.dot(
            back[:, j * HP : (j + 1) * HP], tap_weight(TAPS - 1 - j), preferred_element_type=F32
        )
        total = term if total is None else total + term
    r.hid[RIM : RIM + N, :] = total

    to_plane(3)
    dhid1 = r.dhid1

    def keep_dhid1(row, grad):
        dhid1[pl.ds(pl.multiple_of(row - RIM, 16), grad.shape[0]), :] = grad.astype(BF16)

    inner_norm_back(0, RIM, N // BLOCK, BLOCK, keep_dhid1, r.acc1)

    big[...] = jnp.dot(dhid1[...], first_weight(), preferred_element_type=F32)

    def first_norm_back(i, carry):
        row = pl.multiple_of(i * BLOCK, BLOCK)
        wide = pl.multiple_of(row + RIM, 16)
        scale = cells(r.scale0, wide, BLOCK)
        xhat = (cells(xe, wide, BLOCK).astype(F32) - cells(r.mean0, wide, BLOCK)) * scale
        dpre = cells(big, row, BLOCK) * cells(r.slope0, wide, BLOCK)
        dgain = dpre * xhat
        r.acc0[...] += sum(dgain[n : n + 8] for n in range(0, BLOCK, 8))
        dx = dpre * gain0
        plain = jnp.sum(dx, axis=1, keepdims=True) / D
        cross = jnp.sum(dx * xhat, axis=1, keepdims=True) / D
        grad = scale * (dx - plain - xhat * cross)
        r.gi_own[pl.ds(row, BLOCK), :] = (cells(cote, wide, BLOCK).astype(F32) + grad).astype(BF16)
        return carry

    gi, gi_own = r.gi, r.gi_own
    parts = 4
    part = N // parts
    per_part = part // BLOCK
    row_bases, to_core = {}, {}

    def rows_along(qs, js, at_end):
        def onward(j, place):
            to_core[q, j] = remote(place, place, partner)
            return [to_core[q, j]]

        for j in js:
            for q in qs:
                span = pl.ds(q * part, part)
                place = gi.at[2 * origins[j] + core, span]
                take(row_bases[q], j, place, onward, at_end, passed_all)

    def rows_own(q):
        span = pl.ds(q * part, part)
        copies = [
            remote(gi_own.at[span], gi.at[t, span], at_layer(to), row_bases[q] + j)
            for to, j in own_to
        ]
        if z.line:
            sent.append(copies[0])
            push_if(inner == 1, copies[1])
            copies[0].start()
        else:
            sent.extend(copies)
            for copy in copies:
                copy.start()

    own_pair = []
    for q in range(parts):
        lax.fori_loop(q * per_part, (q + 1) * per_part, first_norm_back, 0)
        span = pl.ds(q * part, part)
        row_bases[q] = arrivals(Z)
        rows_own(q)
        own_pair.append(push(gi_own.at[span], gi.at[t, span], partner))
    own_row = move(gi_own, gi.at[t])

    vec = r.vec
    sum0 = jnp.sum(r.acc0[...], axis=0, keepdims=True)
    sum1 = jnp.sum(r.acc1[...], axis=0, keepdims=True)
    sum2 = jnp.sum(r.acc2[...], axis=0, keepdims=True)
    vec[...] = jnp.zeros_like(vec)
    for j in range(z.nd):
        vec[j : j + 1, :] = sum0[:, j * LANES : (j + 1) * LANES]
    for j in range(z.nh):
        vec[z.nd + j : z.nd + j + 1, :] = sum1[:, j * LANES : (j + 1) * LANES]
        vec[z.nd + z.nh + j : z.nd + z.nh + j + 1, :] = sum2[:, j * LANES : (j + 1) * LANES]
    vec_plane = [push(vec, r.vec_plane.at[i], (seq_at(i), t)) for i in range(1, S)]

    dhid2_t = dhid2[PAD + RIM : PAD + RIM + N, :].T.astype(BF16)
    grad_units(z.nd, dhid2_t, lambda c, w: taps[own, c : c + w], TAPS * z.nh)
    swap(2)
    swap(1)
    dhid1_t = dhid1[...].astype(F32).T.astype(BF16)
    grad_units(0, dhid1_t, lambda c, w: r.act0[own, c : c + w], z.nd)
    swap(0)
    to_plane(2)
    turn_plane(3)
    to_plane(1)
    rows_along([0], [1, 2], False)
    rows_along([1], [1, 2], False)
    turn_plane(2)
    to_plane(0)
    to_z(3)
    z_start(3)
    rows_along([2], [1, 2], False)
    turn_plane(1)
    rows_along([3], [1, 2], False)

    for copy in vec_plane:
        copy.wait_recv()
    vec_sum = r.vec_sum
    vec_sum[...] = sum((r.vec_plane[i] for i in range(1, S)), vec[...])
    vec_z = [push(vec_sum, r.vec_z.at[i - 1], dev_z(i)) for i in range(1, Z)]

    z_over(3)
    to_z(2)
    z_start(2)
    rows_along([0], [3], False)
    rows_along([0, 1, 2, 3], [1], True)
    turn_plane(0)
    rows_along([1], [3], False)
    z_middle(3)
    z_over(2)
    to_z(1)
    z_start(1)
    rows_along([2], [3], False)
    to_z(0)
    z_start(0)
    z_middle(2)
    z_over(1)
    rows_along([3], [3], False)
    to_all(3)
    rows_along([0, 1], [2], True)
    z_over(0)
    z_middle(1)
    to_all(2)
    rows_along([2, 3], [2], True)
    z_middle(0)
    to_all(1)
    rows_along([0], range(3, Z), True)
    to_all(0)
    rows_along([1], range(3, Z), True)

    for copy in vec_z:
        copy.wait_recv()
    vec_half = r.vec_half
    vec_half[...] = sum((r.vec_z[i - 1] for i in range(1, Z)), vec_sum[...])
    vec_core = push(vec_half, r.gain_sums.at[1], partner)
    own_sums.append(move(vec_half, r.gain_sums.at[0]))
    rows_along([2, 3], range(3, Z), True)
    for k in reversed(range(STAGES)):
        all_here(k)

    vec_core.wait_recv()
    for copy in own_sums:
        copy.wait()
    out_own.wait()
    for copy in out_copies:
        copy.wait_recv()
    own_row.wait()
    for copy in own_pair:
        copy.wait_recv()
    for copy in to_core.values():
        copy.wait_recv()
    assert all(n <= sems.shape[0] for n, sems in zip(counts, (send, recv, local)))
    for copy in sent:
        copy.wait_send()
    for when, copy in sent_if:

        @pl.when(when)
        def _():
            copy.wait_send()


def finish(z, *refs):
    got, gi_got, ff, gain_sums = refs[:4]
    out, gi, grad_first, grad_conv, grad_last, grad_gain, grad_gain1, grad_gain2, *refs = refs[4:]
    first, conv, last, gains, sems = refs
    t = lax.axis_index("tp")
    copies = []

    def move(src, dst):
        copy = pltpu.make_async_copy(src, dst, sems.at[len(copies)])
        copy.start()
        copies.append(copy)

    half = z.R // 2
    for i in range(2):
        move(gi_got.at[pl.ds(i * half, half)], gi.at[pl.ds(i * half, half)])
    move(got, out)

    def summed(start, count):
        return jnp.concatenate(
            [ff[u % z.S, u // z.S].astype(F32) for u in range(start, start + count)], axis=1
        )

    first[...] = summed(0, z.nd)
    move(first, grad_first)
    for k in range(TAPS):
        conv[k] = summed(z.nd + k * z.nh, z.nh)
    move(conv, grad_conv)
    last[...] = summed(z.nd + TAPS * z.nh, z.nd)
    move(last, grad_last)
    sums = gain_sums[0] + gain_sums[1]

    def line(start, count):
        return jnp.concatenate([sums[j : j + 1, :] for j in range(start, start + count)], axis=1)

    def picked(row, width, step):
        return sum(
            jnp.where(t == j, row[:, j * step : j * step + width], 0.0) for j in range(z.T)
        )

    grad_gain[...] = picked(line(0, z.nd), z.Dt, z.Dt)
    grad_gain1[...] = picked(line(z.nd, z.nh), z.Hs, z.Hp)
    grad_gain2[...] = picked(line(z.nd + z.nh, z.nh), z.Hs, z.Hp)
    for copy in copies:
        copy.wait()


def shards(
    mesh,
    inputs,
    starts,
    first_proj,
    dilated_conv,
    last_proj,
    first_norm_gain,
    second_norm_gain,
    third_norm_gain,
    cotangent,
):
    z = Sizes(mesh, inputs, starts, first_proj, cotangent)
    S, T, Z, N, D, E, HP, Hp, NR = z.S, z.T, z.Z, z.N, z.D, z.E, z.HP, z.Hp, z.NR
    more = Hp - z.Hs
    first, last = first_proj.T, last_proj
    conv = dilated_conv.transpose(0, 2, 1)
    if more:
        first, last = (jnp.pad(part, ((0, more), (0, 0))) for part in (first, last))
        conv = jnp.pad(
            conv.reshape(TAPS, z.Hs, T, z.Hs), ((0, 0), (0, more), (0, 0), (0, more))
        ).reshape(TAPS, Hp, HP)
    vm, anywhere = pltpu.VMEM, pl.ANY
    ins = dict(
        x=(inputs, anywhere),
        starts=(starts, vm),
        w1=(first, anywhere),
        wc=(conv, anywhere),
        w3=(last, anywhere),
        g1=(first_norm_gain.reshape(z.nd, LANES), vm),
        g2=(second_norm_gain.reshape(1, z.Hs), vm),
        g3=(third_norm_gain.reshape(1, z.Hs), vm),
        cot=(cotangent.transpose(0, 2, 1), anywhere),
    )
    outs = dict(
        out=((z.R, z.Dt, N), BF16),
        gi=((z.R, N, D), BF16),
        ff=((S, NR, Hp, LANES), BF16),
        gain_sums=((2, 24, LANES), F32),
    )
    near = vm if z.line else jax.ShapeDtypeStruct
    scratch = dict(
        send=pltpu.SemaphoreType.DMA((226 if z.line else 800,)),
        recv=pltpu.SemaphoreType.DMA((222 if z.line else 800,)),
        local=pltpu.SemaphoreType.DMA((13,)),
        xe=vm((E, D), BF16),
        cote=vm((E, D), BF16),
        act0=vm((E, D), BF16),
        slope0=vm((E, D), F32),
        mean0=vm((E, 1), F32),
        scale0=vm((E, 1), F32),
        mask=vm((E, LANES), F32),
        flags_left=vm((z.R, N), jnp.int32),
        flags_right=vm((z.R, N), jnp.int32),
        gslots=vm((T, 8, LANES), F32),
        gains=vm((8, HP), F32),
        wg=vm((S, NR, Z, 2, Hp, LANES), BF16),
        hid=vm((E, HP), F32),
        xhat1=vm((E, HP), F32),
        slope1=vm((E, HP), F32),
        scale1=vm((E, 1), F32),
        xhat2=vm((E, HP), F32),
        slope2=vm((E, HP), F32),
        scale2=vm((E, 1), F32),
        act1=vm((E + 2 * PAD, HP), F32),
        dhid2=vm((E + 2 * PAD, HP), F32),
        taps=vm((E, TAPS * HP), BF16),
        back=vm((N, TAPS * HP), BF16),
        act2=vm((E, HP), BF16),
        dhid1=vm((N, HP), BF16),
        big=vm((N, D), F32),
        gi_own=vm((N, D), BF16),
        acc0=vm((8, D), F32),
        acc1=vm((8, HP), F32),
        acc2=vm((8, HP), F32),
        cot_t=vm((D, N), BF16),
        out_t=vm((D, N), BF16),
        w1_in=vm((Hp, D), BF16),
        wc_in=vm((TAPS, Hp, HP), BF16),
        w3_in=vm((Hp, D), BF16),
        gl=vm((8, LANES), F32),
        g=vm((S, NR, Z, 2, Hp, LANES), BF16),
        rc=vm((S, NR, Z, Hp, LANES), BF16),
        ff_own=vm((NR, Hp, LANES), BF16),
        vec=vm((24, LANES), F32),
        vec_sum=vm((24, LANES), F32),
        vec_plane=vm((S, 24, LANES), F32),
        vec_z=vm((Z, 24, LANES), F32),
        vec_half=vm((24, LANES), F32),
    )
    if z.line:
        scratch.update(rz_end=vm((NR, 3, Hp, LANES), BF16))
        scratch.update(rz_pair=vm((NR, 2, Hp, LANES), BF16), rz_one=vm((NR, Hp, LANES), BF16))
    else:
        scratch.update(rz=vm((Z, NR, Hp, LANES), BF16))
    if z.square:
        scratch.update(rx=vm((2, NR, Z // 2, Hp, LANES), BF16))
        scratch.update(ry=vm((2, NR, Z // 2, Hp, LANES), BF16))
        scratch.update(rx2=vm((NR, Z // 2, Hp, LANES), BF16))
        scratch.update(ry2=vm((NR, Z // 2, Hp, LANES), BF16))
    else:
        scratch.update(rd=vm((S, NR, Z, Hp, LANES), BF16))
    names = [*ins, *outs, *scratch]
    results = pl.pallas_call(
        functools.partial(kernel, z, names),
        out_shape=[near(shape, kind) for shape, kind in outs.values()],
        in_specs=[pl.BlockSpec(memory_space=space) for _, space in ins.values()],
        out_specs=[pl.BlockSpec(memory_space=anywhere)] * len(outs),
        scratch_shapes=list(scratch.values()),
        compiler_params=pltpu.CompilerParams(
            collective_id=0, has_side_effects=True, vmem_limit_bytes=(50 if z.line else 63) * 2**20
        ),
    )(*[array for array, _ in ins.values()])
    if z.line:
        results = [pltpu.with_memory_space_constraint(part, vm) for part in results]
    shape = jax.ShapeDtypeStruct
    out, gi, grad_first, grad_conv, grad_last, grad_gain, grad_gain1, grad_gain2 = pl.pallas_call(
        functools.partial(finish, z),
        out_shape=[
            shape((z.R, z.Dt, N), BF16),
            shape((z.R, N, D), BF16),
            shape((Hp, D), F32),
            shape((TAPS, Hp, HP), F32),
            shape((Hp, D), F32),
            shape((1, z.Dt), F32),
            shape((1, z.Hs), F32),
            shape((1, z.Hs), F32),
        ],
        in_specs=[pl.BlockSpec(memory_space=space) for space in (anywhere, anywhere, vm, vm)],
        out_specs=[pl.BlockSpec(memory_space=space) for space in [anywhere] * 5 + [vm] * 3],
        scratch_shapes=[
            vm((Hp, D), F32),
            vm((TAPS, Hp, HP), F32),
            vm((Hp, D), F32),
            vm((8, LANES), F32),
            pltpu.SemaphoreType.DMA((6,)),
        ],
        compiler_params=pltpu.CompilerParams(vmem_limit_bytes=12 * 2**20),
    )(*results)
    if more:
        grad_first, grad_last = grad_first[: z.Hs], grad_last[: z.Hs]
        grad_conv = grad_conv.reshape(TAPS, Hp, T, Hp)[:, : z.Hs, :, : z.Hs]
        grad_conv = grad_conv.reshape(TAPS, z.Hs, z.H)
    return (
        out.transpose(0, 2, 1),
        gi,
        grad_first.T,
        grad_conv.transpose(0, 2, 1),
        grad_last,
        grad_gain.reshape(-1),
        grad_gain1.reshape(-1),
        grad_gain2.reshape(-1),
    )


def solution(mesh):
    placed = (
        P(None, "seq", None),
        P(None, "seq"),
        P(None, "tp"),
        P(None, None, "tp"),
        P("tp", None),
        P(),
        P("tp"),
        P("tp"),
        P(None, "seq", "tp"),
    )
    return jax.shard_map(
        functools.partial(shards, mesh),
        mesh=mesh,
        in_specs=placed,
        out_specs=(
            P(None, "seq", "tp"),
            P(None, "seq", None),
            P(None, "tp"),
            P(None, None, "tp"),
            P("tp", None),
            P("tp"),
            P("tp"),
            P("tp"),
        ),
        check_vma=False,
    )
```

```python
import functools
from types import SimpleNamespace

import jax
import jax.numpy as jnp
from jax import lax
from jax.experimental import pallas as pl
from jax.experimental.pallas import tpu as pltpu
from jax.sharding import PartitionSpec as P

MESH = pl.DeviceIdType.MESH
F32 = jnp.float32
BF16 = jnp.bfloat16

TAPS = 5
STEP = 2
REACH = 4
EPS = 1e-05
LANES = 128
RIM = 16
PAD = 8
STAGES = 4
REST = STAGES
BLOCK = 64
HALF_ROOT = 0.7071067811865476
PEAK = 0.3989422804014327

NT = (((1,), (1,)), ((), ()))
OFFSETS = [STEP * k - REACH for k in range(TAPS)]


class Sizes:
    def __init__(self, mesh, inputs, starts, first_proj, cotangent):
        self.S = mesh.shape["seq"]
        self.T = mesh.shape["tp"]
        self.Z = self.T // 2
        self.R, self.N, self.D = inputs.shape
        assert self.R == self.T and self.N % LANES == 0
        self.Hs = first_proj.shape[1]
        self.H = self.Hs * self.T
        self.Hp = -(-self.Hs // 16) * 16
        self.HP = self.Hp * self.T
        assert self.HP % LANES == 0 and self.D % LANES == 0
        self.E = self.N + 2 * RIM
        self.nd = self.D // LANES
        self.nh = self.HP // LANES
        self.units = 2 * self.nd + TAPS * self.nh
        one, two = -(-self.nd // self.S), -(-(self.nd + TAPS * self.nh) // self.S)
        whole = self.units // self.S
        self.rest = self.units % self.S if whole > two else 0
        self.NF = whole if self.rest else -(-self.units // self.S)
        self.NR = self.NF + (self.rest > 0)
        self.chunks = [(0, one), (one, (one + two) // 2), ((one + two) // 2, two), (two, self.NF)]
        self.Dt = cotangent.shape[2]
        assert self.Dt % 16 == 0
        self.square = self.S == 4
        self.line = self.Z == 4


def cells(ref, row, count):
    return ref[pl.ds(row, count), :]


def gelu_parts(v):
    whole = 0.5 * (1.0 + lax.erf(v * HALF_ROOT))
    slope = whole + v * (PEAK * jnp.exp(-0.5 * v * v))
    return v * whole, slope


def kernel(z, names, *refs):
    r = SimpleNamespace(**dict(zip(names, refs, strict=True)))
    S, T, Z, N, D, E, H, Hp, HP, NR = z.S, z.T, z.Z, z.N, z.D, z.E, z.H, z.Hp, z.HP, z.NR
    s, t = lax.axis_index("seq"), lax.axis_index("tp")
    core, layer = lax.rem(t, 2), t // 2
    partner = (s, t + 1 - 2 * core)

    send, recv, local = r.send, r.recv, r.local
    counts = [0, 0, 0]
    sent, sent_if, together = [], [], []

    def remote(src, dst, device, arrival=None, sends=None):
        return pltpu.make_async_remote_copy(
            src_ref=src,
            dst_ref=dst,
            send_sem=send.at[sendings() if sends is None else sends],
            recv_sem=recv.at[arrivals(1) if arrival is None else arrival],
            device_id=device,
            device_id_type=MESH,
        )

    def sendings():
        counts[0] += 1
        return counts[0] - 1

    def arrivals(count):
        counts[1] += count
        return counts[1] - count

    def shared(place):
        pair = (arrivals(1), sendings())
        together.append((pair[1], place))
        return pair

    def arrived(arrival, place):
        remote(place, place, partner, arrival, 0).wait_recv()

    def push(src, dst, device, arrival=None, sends=None):
        copy = remote(src, dst, device, arrival, sends)
        copy.start()
        if sends is None:
            sent.append(copy)
        return copy

    def push_if(when, copy):
        @pl.when(when)
        def _():
            copy.start()

        sent_if.append((when, copy))

    def move(src, dst):
        counts[2] += 1
        copy = pltpu.make_async_copy(src, dst, local.at[counts[2] - 1])
        copy.start()
        return copy

    def z_at(i):
        return lax.rem(layer + i + Z, Z)

    def dev_z(i):
        return (s, 2 * z_at(i) + core)

    def seq_at(i):
        return lax.rem(s + i + S, S)

    steps = range(1, Z)
    if z.line:
        upper = layer // 2
        inner = lax.rem((layer + 1) // 2, 2)
        end, middle = 3 * upper, 1 + upper
        first = inner * (3 - layer) + (1 - inner) * middle
        second = inner * end + (1 - inner) * (3 - middle)
        origins = [None, first, second, 3 - end]
        own_to = [(first, 2 - inner), (end, 1)]
        passed = {1: (end, 2), 2: (3 - layer, 3), 3: (end, 3)}
    else:
        origins = [None] + [z_at(-i) for i in steps]
        own_to = [(z_at(i), i) for i in steps]
        passed, inner = {}, 0

    def at_layer(to):
        return (s, 2 * to + core)

    def only(at_end, go):
        if z.line:
            pl.when(inner == 1 - at_end)(go)
        elif at_end:
            go()

    def send_own(base, src, place, later=False):
        copies = [remote(src, place, at_layer(to), base + j) for to, j in own_to]
        if z.line:
            push_if(inner == 1, copies.pop())
        sent.extend(copies)
        later = later and z.line
        for copy in copies:
            if later:
                pl.when(inner == 1)(copy.start)
            else:
                copy.start()
        return (lambda: pl.when(inner == 0)(copies[0].start)) if later else (lambda: None)

    def take(base, j, place, onward, at_end, start=True):
        if base + j not in onwards:
            extra = None
            if j in passed:
                to, then = passed[j]
                extra = remote(place, place, at_layer(to), base + then)
                sent_if.append((inner == 1, extra))
            onwards[base + j] = (extra, onward(j, place))

        def go():
            extra, copies = onwards[base + j]
            arrived(base + j, place)
            if extra is not None and not at_end:
                extra.start()
            if start:
                for copy in copies:
                    copy.start()

        only(at_end, go)

    onwards = {}
    right, left = (seq_at(1), t), (seq_at(-1), t)
    if z.square:
        sx, sy, sd = s ^ 1, s ^ 2, s ^ 3
        x_side, y_side = (sx, t), (sy, t)

    xe, cot, cot_t = r.xe, r.cot, r.cot_t

    def features(who):
        return pl.ds(pl.multiple_of(who * z.Dt, 16), z.Dt)

    weights_in = [move(r.w1, r.w1_in), move(r.wc, r.wc_in), move(r.w3, r.w3_in)]
    row_in = move(r.x.at[t], xe.at[pl.ds(RIM, N)])
    cot_own = move(cot.at[t], cot_t.at[features(t)])

    barrier = pltpu.get_barrier_semaphore()
    for i in range(1, T):
        pl.semaphore_signal(barrier, inc=1, device_id=(s, lax.rem(t + i, T)), device_id_type=MESH)
    for i in range(1, S):
        pl.semaphore_signal(barrier, inc=1, device_id=(seq_at(i), t), device_id_type=MESH)
    pl.semaphore_wait(barrier, T + S - 2)

    rim_r = push(r.x.at[t, pl.ds(N - RIM, RIM)], xe.at[pl.ds(0, RIM)], right)
    rim_l = push(r.x.at[t, pl.ds(0, RIM)], xe.at[pl.ds(RIM + N, RIM)], left)
    flags_r = push(r.starts, r.flags_left, right)
    flags_l = push(r.starts, r.flags_right, left)
    r.gl[0:1, : z.Hs] = r.g2[...]
    r.gl[1:2, : z.Hs] = r.g3[...]
    some_gains = r.gslots.at[pl.ds(0, T - 1)]
    for_gains = shared(some_gains)
    for i in range(1, T):
        push(r.gl, r.gslots.at[t], (s, lax.rem(t + i, T)), *for_gains)
    gain_own = move(r.gl, r.gslots.at[t])

    wg = r.wg
    bases, plane = {}, {}
    plane_x, plane_y, plane_d, plane_any, across = {}, {}, {}, {}, {}

    def unit_in(u):
        if u < z.nd:
            return r.w1_in[:, u * LANES : (u + 1) * LANES]
        u -= z.nd
        if u < TAPS * z.nh:
            return r.wc_in[u // z.nh, :, u % z.nh * LANES : (u % z.nh + 1) * LANES]
        u -= TAPS * z.nh
        if u < z.nd:
            return r.w3_in[:, u * LANES : (u + 1) * LANES]
        return jnp.zeros((Hp, LANES), BF16)

    def rounds(k):
        a, b = z.chunks[k]
        return pl.ds(a, b - a)

    def carried(ref, k, which, c):
        if k == REST:
            return ref.at[pl.ds(0, z.rest), z.NF, which, c]
        return ref.at[s, rounds(k), which, c]

    def every(ref, k, which, c):
        return carried(ref, k, which, c) if k == REST else ref.at[:, rounds(k), which, c]

    every_chip = pl.ds(0, Z)

    def weights_own(k):
        if k == REST:
            for q in range(z.rest):
                wg[q, z.NF, layer, core] = unit_in(z.NF * S + q)
        else:
            for q in range(S):
                for n in range(*z.chunks[k]):
                    wg[q, n, layer, core] = unit_in(n * S + q)
        place = carried(wg, k, layer, core)
        bases[k] = arrivals(Z)
        send_own(bases[k], place, place)
        across[k] = shared(every(wg, k, every_chip, core))
        place = every(wg, k, layer, core)
        push(place, place, partner, *across[k])
        if k != REST:
            copies = S if z.square else S - 1
            plane[k] = sendings()
            together.append(
                (plane[k], wg.at[pl.ds(0, copies - z.square), rounds(k), pl.ds(0, Z - 1), core])
            )

    def weights_along(k, at_end, js=steps, start=True):
        def onward(j, place):
            if k == REST:
                return [remote(place, place, partner, *across[k])]
            if not z.square:
                plane_any[k, j] = [
                    remote(place, place, (seq_at(i), t), None, plane[k]) for i in range(1, S)
                ]
                return plane_any[k, j]
            plane_x[k, j] = remote(place, place, x_side, None, plane[k])
            plane_y[k, j] = remote(place, place, y_side, None, plane[k])
            return [plane_x[k, j], plane_y[k, j]]

        for j in js:
            take(bases[k], j, carried(wg, k, origins[j], core), onward, at_end, start)

    def weights_spread(k, js=steps):
        def go():
            for j in js:
                for copy in onwards[bases[k] + j][1]:
                    copy.start()

        only(False, go)

    def weights_corner(k, at_end):
        if not z.square:
            return
        for j in steps:
            if (k, j) not in plane_d:
                over_y = (k + j) % 2
                place = wg.at[sx if over_y else sy, rounds(k), origins[j], core]
                side = y_side if over_y else x_side
                plane_d[k, j] = remote(place, place, side, None, plane[k])

        def go():
            for j in steps:
                plane_x[k, j].wait_recv()
                plane_y[k, j].wait_recv()
                plane_d[k, j].start()
                for q in (s, sx, sy):
                    place = wg.at[q, rounds(k), origins[j], core]
                    push(place, place, partner, *across[k])

        only(at_end, go)

    def weights_across(k, js=steps):
        for j in js:
            if z.square:
                plane_d[k, j].wait_recv()
                place = wg.at[sd, rounds(k), origins[j], core]
            else:
                for copy in plane_any[k, j]:
                    copy.wait_recv()
                place = wg.at[:, rounds(k), origins[j], core]
            push(place, place, partner, *across[k])

    def weights_ready(k):
        arrived(across[k][0], every(wg, k, every_chip, 1 - core))

    some_cot = cot_t.at[pl.ds(0, (T - 1) * z.Dt)]
    for_cot = shared(some_cot)

    def cotangent_out(at_end):
        def go():
            for i in range(1, T):
                to = lax.rem(t + i, T)
                push(cot.at[to], cot_t.at[features(t)], (s, to), *for_cot)

        only(at_end, go)

    weights_in[0].wait()
    weights_in[1].wait()
    weights_own(0)
    weights_own(1)
    weights_in[2].wait()
    weights_own(2)
    weights_own(3)
    some_rest = [REST] if z.rest else []
    for k in some_rest:
        weights_own(k)
    def unit(ref, u):
        return ref[u % S, u // S].reshape(HP, LANES)

    def weights(first, count):
        return jnp.concatenate([unit(wg, u) for u in range(first, first + count)], axis=1)

    def first_weight():
        return weights(0, z.nd)

    def tap_weight(k):
        return weights(z.nd + k * z.nh, z.nh)

    def last_weight():
        return weights(z.nd + TAPS * z.nh, z.nd)

    row_in.wait()

    gain0 = jnp.concatenate([r.g1[j : j + 1, :] for j in range(z.nd)], axis=1)

    def first_norm(first, count, size):
        def body(i, carry):
            row = pl.multiple_of(first + i * size, 16)
            v = cells(xe, row, size).astype(F32)
            mean = jnp.sum(v, axis=1, keepdims=True) / D
            spread = jnp.sum(v * v, axis=1, keepdims=True) / D - mean * mean
            scale = lax.rsqrt(spread + EPS)
            act, slope = gelu_parts((v - mean) * scale * gain0)
            r.act0[pl.ds(row, size), :] = act.astype(BF16)
            r.slope0[pl.ds(row, size), :] = slope
            r.mean0[pl.ds(row, size), :] = mean
            r.scale0[pl.ds(row, size), :] = scale
            return carry

        lax.fori_loop(0, count, body, 0)

    first_norm(RIM, N // BLOCK, BLOCK)

    for k in range(STAGES):
        weights_along(k, False, steps[:2], k < 2)
        weights_along(k, True, steps[:1])
    for k in some_rest:
        weights_along(k, False, steps[:2])
        weights_along(k, True, steps[:1])
    rim_r.wait_recv()
    rim_l.wait_recv()
    first_norm(0, 1, RIM)
    first_norm(RIM + N, 1, RIM)

    gain_own.wait()
    arrived(for_gains[0], some_gains)
    for j in range(T):
        r.gains[0:2, j * Hp : (j + 1) * Hp] = r.gslots[j, 0:2, :Hp]

    flags_r.wait_recv()
    flags_l.wait_recv()
    here = r.starts[pl.ds(t, 1), :]
    before = r.flags_left[pl.ds(t, 1), :]
    after = r.flags_right[pl.ds(t, 1), :]
    window = jnp.concatenate([before[:, N - LANES :], here, after[:, :LANES]], axis=1).astype(F32)
    window = jnp.broadcast_to(window, (E, N + 2 * LANES))
    at = lax.broadcasted_iota(jnp.int32, window.shape, 1) - LANES
    place = lax.broadcasted_iota(jnp.int32, window.shape, 0) - RIM
    rows = lax.broadcasted_iota(jnp.int32, (E, 1), 0) - RIM + s * N
    for k, offset in enumerate(OFFSETS):
        low, high = min(offset, 0), max(offset, 0)
        begun = jnp.sum(
            jnp.where((at > place + low) & (at <= place + high), window, 0.0), axis=1, keepdims=True
        )
        moved = rows + offset
        inside = (begun == 0.0) & (moved >= 0) & (moved < S * N)
        r.mask[:, k : k + 1] = inside.astype(F32)

    third = steps[2:]
    weights_along(0, False, third)
    weights_along(0, True, [2])
    weights_along(1, False, third)
    weights_along(1, True, [2])
    weights_along(2, False, third, False)
    weights_along(2, True, [2])
    weights_along(3, False, third, False)
    for k in some_rest:
        weights_along(k, False, third)
    weights_corner(0, False)
    weights_spread(2)
    weights_along(0, True, third)
    weights_along(1, True, third)
    weights_along(3, True, [2])
    weights_along(2, True, third)
    cotangent_out(True)
    weights_corner(0, True)
    weights_corner(1, False)
    weights_along(3, True, third)
    for k in some_rest:
        weights_along(k, True, steps[1:])
    weights_corner(1, True)
    weights_spread(3)
    weights_across(0, steps[:1])
    cotangent_out(False)
    weights_across(0, steps[1:])

    weights_ready(0)
    r.hid[...] = lax.dot_general(r.act0[...], first_weight(), NT, preferred_element_type=F32)
    weights_corner(2, False)
    weights_corner(2, True)
    weights_across(1)

    def inner_norm(which, act_store, first, count, size):
        gain = r.gains[which : which + 1, :]
        xhat_ref, slope_ref, scale_ref = (
            (r.xhat1, r.slope1, r.scale1),
            (r.xhat2, r.slope2, r.scale2),
        )[which]

        def body(i, carry):
            row = pl.multiple_of(first + i * size, 16)
            v = cells(r.hid, row, size)
            mean = jnp.sum(v, axis=1, keepdims=True) / H
            spread = jnp.sum(v * v, axis=1, keepdims=True) / H - mean * mean
            scale = lax.rsqrt(spread + EPS)
            xhat = (v - mean) * scale
            act, slope = gelu_parts(xhat * gain)
            act_store(row, act)
            xhat_ref[pl.ds(row, size), :] = xhat
            slope_ref[pl.ds(row, size), :] = slope
            scale_ref[pl.ds(row, size), :] = scale
            return carry

        lax.fori_loop(0, count, body, 0)

    act1, taps = r.act1, r.taps
    act1[0:PAD, :] = jnp.zeros((PAD, HP), F32)
    act1[PAD + E :, :] = jnp.zeros((PAD, HP), F32)

    def keep_act1(row, act):
        act1[pl.ds(pl.multiple_of(row + PAD, 8), act.shape[0]), :] = act.astype(BF16).astype(F32)

    inner_norm(0, keep_act1, RIM, N // BLOCK, BLOCK)
    inner_norm(0, keep_act1, 0, 1, RIM)
    inner_norm(0, keep_act1, RIM + N, 1, RIM)
    for k, offset in enumerate(OFFSETS):
        taps[:, k * HP : (k + 1) * HP] = (
            act1[PAD + offset : PAD + offset + E, :] * r.mask[:, k : k + 1]
        ).astype(BF16)


    def tap_term(k):
        return lax.dot_general(
            taps[:, k * HP : (k + 1) * HP], tap_weight(k), NT, preferred_element_type=F32
        )

    weights_ready(1)
    total = tap_term(0) + tap_term(1)
    weights_corner(3, False)
    weights_corner(3, True)
    weights_across(2)
    weights_ready(2)
    for k in range(2, TAPS):
        total = total + tap_term(k)
    r.hid[...] = total
    weights_across(3)

    cot_own.wait()
    arrived(for_cot[0], some_cot)
    cote = r.cote
    cote[RIM : RIM + N, :] = cot_t[...].T
    edge_r = push(cote.at[pl.ds(N, RIM)], cote.at[pl.ds(0, RIM)], right)
    edge_l = push(cote.at[pl.ds(RIM, RIM)], cote.at[pl.ds(RIM + N, RIM)], left)

    act2 = r.act2

    def keep_act2(row, act):
        act2[pl.ds(row, act.shape[0]), :] = act.astype(BF16)

    inner_norm(1, keep_act2, RIM, N // BLOCK, BLOCK)

    for k in [3, *some_rest]:
        weights_ready(k)
    big, out_t = r.big, r.out_t
    some_out = r.out.at[pl.ds(0, T - 1)]
    for_out = shared(some_out)
    half_units = z.nd // 2
    own_half = layer // (Z // 2)
    for n in range(2):
        half = own_half if n == 0 else 1 - own_half
        units = [z.nd + TAPS * z.nh + half * half_units + j for j in range(half_units)]
        span = pl.ds(pl.multiple_of(half * half_units * LANES, LANES), half_units * LANES)
        rows = jnp.dot(
            act2[RIM : RIM + N, :],
            jnp.concatenate([unit(wg, u) for u in units], axis=1),
            preferred_element_type=F32,
        )
        rows = rows + xe[RIM : RIM + N, span].astype(F32)
        out_t[span, :] = rows.astype(BF16).T
        for i in range(T // 2):
            to = half * (T // 2) + lax.rem(t + i, T // 2)

            @pl.when(to != t)
            def _():
                push(out_t.at[features(to)], r.out.at[t], (s, to), *for_out)

    out_own = move(out_t.at[features(t)], r.out.at[t])

    g = r.g

    def grad_units(first, lhs, rhs, count):
        for j in range(0, count, 2):
            width = min(2, count - j)
            block = jnp.dot(
                lhs, rhs(j * LANES, width * LANES), preferred_element_type=F32
            ).astype(BF16)
            for i in range(width):
                u = first + j + i
                g[u % S, u // S] = block[:, i * LANES : (i + 1) * LANES].reshape(Z, 2, Hp, LANES)

    rc = r.rc
    swaps, plane1, plane2, along_back = {}, {}, {}, {}
    some_sums = r.ff.at[pl.ds(0, S - 1), pl.ds(0, z.NF)]
    spread_out = shared(some_sums)
    beside, over, own_sums = {}, {}, []

    def swap(k):
        place = every(g, k, every_chip, 1 - core)
        to = rc.at[pl.ds(0, z.rest), z.NF] if k == REST else rc.at[:, rounds(k)]
        swaps[k] = push(place, to, partner)

    def add_swapped(k):
        swaps[k].wait_recv()
        at_ = [(q, z.NF) for q in range(z.rest)]
        if k != REST:
            at_ = [(q, n) for q in range(S) for n in range(*z.chunks[k])]
        for q, n in at_:
            g[q, n, :, core] = (g[q, n, :, core].astype(F32) + rc[q, n].astype(F32)).astype(BF16)

    near, far = pl.ds(0, Z // 2), pl.ds(Z // 2, Z // 2)

    def to_plane(k):
        a, b = z.chunks[k]
        span = pl.ds(a, b - a)
        add_swapped(k)
        if z.square:
            over_x, over_y = shared(r.rx.at[:, span]), shared(r.ry.at[:, span])
            push(g.at[sx, span, near, core], r.rx.at[0, span], x_side, *over_x)
            push(g.at[sd, span, near, core], r.rx.at[1, span], x_side, *over_x)
            push(g.at[sy, span, far, core], r.ry.at[0, span], y_side, *over_y)
            push(g.at[sd, span, far, core], r.ry.at[1, span], y_side, *over_y)
            plane1[k] = [(over_x[0], r.rx.at[:, span]), (over_y[0], r.ry.at[:, span])]
        else:
            others = r.rd.at[pl.ds(1, S - 1), span]
            over = shared(others)
            for i in range(1, S):
                push(g.at[seq_at(i), span, :, core], r.rd.at[i, span], (seq_at(i), t), *over)
            plane1[k] = [(over[0], others)]

    def add_into(q, n, where, other):
        g[q, n, where, core] = (g[q, n, where, core].astype(F32) + other.astype(F32)).astype(BF16)

    def turn_plane(k):
        a, b = z.chunks[k]
        span = pl.ds(a, b - a)
        for arrival, place in plane1[k]:
            arrived(arrival, place)
        if not z.square:
            return
        for n in range(a, b):
            add_into(sy, n, near, r.rx[1, n])
            add_into(sx, n, far, r.ry[1, n])
        plane2[k] = [
            push(g.at[sy, span, near, core], r.ry2.at[span], y_side),
            push(g.at[sx, span, far, core], r.rx2.at[span], x_side),
        ]
        for n in range(a, b):
            add_into(s, n, near, r.rx[0, n])
            add_into(s, n, far, r.ry[0, n])

    def to_z(k):
        a, b = z.chunks[k]
        span = pl.ds(a, b - a)
        if z.square:
            for copy in plane2[k]:
                copy.wait_recv()
            for n in range(a, b):
                add_into(s, n, near, r.ry2[n])
                add_into(s, n, far, r.rx2[n])
        else:
            for n in range(a, b):
                sums = g[s, n, :, core].astype(F32)
                for i in range(1, S):
                    sums = sums + r.rd[i, n].astype(F32)
                g[s, n, :, core] = sums.astype(BF16)

    def sums_of(k):
        if k == REST:
            return [(q, z.NF, z.NF + q) for q in range(z.rest)]
        return [(s, n, n) for n in range(*z.chunks[k])]

    def rows_of(k):
        return pl.ds(z.NF, z.rest) if k == REST else rounds(k)

    def z_start(k):
        if z.line:
            beside[k] = arrivals(1)
            copy = remote(
                carried(g, k, pl.ds(1 - upper, 3), core),
                r.rz_end.at[rows_of(k)],
                at_layer(middle),
                beside[k],
            )
            push_if(inner == 0, copy)
        else:
            along_back[k] = [
                push(carried(g, k, z_at(i), core), r.rz.at[i, rows_of(k)], dev_z(i)) for i in steps
            ]

    def z_over(k):
        if z.line:
            over[k] = arrivals(1)
            pair = pl.ds(2 - 2 * upper, 2)
            copy = remote(
                carried(g, k, pair, core), r.rz_pair.at[rows_of(k)], at_layer(3 - layer), over[k]
            )
            sent_if.append((inner == 1, copy))

            @pl.when(inner == 1)
            def _():
                arrived(beside[k], r.rz_end.at[rows_of(k)])
                for q, n, b in sums_of(k):
                    add_into(q, n, pair, r.rz_end[b, pl.ds(1 - upper, 2)])
                copy.start()

    def z_middle(k):
        if z.line:
            along_back[k] = remote(
                carried(g, k, end, core), r.rz_one.at[rows_of(k)], at_layer(end)
            )
            sent_if.append((inner == 1, along_back[k]))

            @pl.when(inner == 1)
            def _():
                arrived(over[k], r.rz_pair.at[rows_of(k)])
                for q, n, b in sums_of(k):
                    add_into(q, n, pl.ds(2 * upper, 2), r.rz_pair[b])
                along_back[k].start()
                for q, n, b in sums_of(k):
                    sums = g[q, n, layer, core].astype(F32) + r.rz_end[b, 2 * upper].astype(F32)
                    r.ff_own[b] = sums.astype(BF16)

    def to_all(k):
        if z.line:

            @pl.when(inner == 0)
            def _():
                along_back[k].wait_recv()
                for q, n, b in sums_of(k):
                    sums = g[q, n, layer, core].astype(F32) + r.rz_one[b].astype(F32)
                    r.ff_own[b] = sums.astype(BF16)
        else:
            for copy in along_back[k]:
                copy.wait_recv()
            for q, n, b in sums_of(k):
                sums = g[q, n, layer, core].astype(F32)
                for i in steps:
                    sums = sums + r.rz[i, b].astype(F32)
                r.ff_own[b] = sums.astype(BF16)
        place = r.ff_own.at[rows_of(k)]
        for i in range(1, S):
            if k == REST:
                push(place, r.others.at[i], (seq_at(i), t), *for_others)
            else:
                push(place, r.ff.at[s, rounds(k)], (seq_at(i), t), *spread_out)
        if k != REST:
            own_sums.append(move(place, r.ff.at[s, rounds(k)]))

    def rest_end():
        arrived(for_others[0], some_others)
        for q in range(z.rest):
            sums = r.ff_own[z.NF + q].astype(F32)
            for i in range(1, S):
                sums = sums + r.others[i, q].astype(F32)
            r.rest_sum[q] = sums.astype(BF16)
        own_sums.append(move(r.rest_sum, r.ff.at[pl.ds(0, z.rest), z.NF]))

    if z.rest:
        some_others = r.others.at[pl.ds(1, S - 1)]
        for_others = shared(some_others)
    for u in [] if z.rest else range(z.units, S * NR):
        g[u % S, u // S] = jnp.zeros((Z, 2, Hp, LANES), BF16)
    own = slice(RIM, RIM + N)
    act2_t = act2[own, :].astype(F32).T.astype(BF16)
    grad_units(z.nd + TAPS * z.nh, act2_t, lambda c, w: cote[own, c : c + w], z.nd)
    swap(3)
    for k in some_rest:
        swap(k)
    inner_norm(1, keep_act2, 0, 1, RIM)
    inner_norm(1, keep_act2, RIM + N, 1, RIM)

    edge_r.wait_recv()
    edge_l.wait_recv()
    r.hid[...] = lax.dot_general(cote[...], last_weight(), NT, preferred_element_type=F32)
    r.acc1[...] = jnp.zeros_like(r.acc1)
    r.acc2[...] = jnp.zeros_like(r.acc2)
    r.acc0[...] = jnp.zeros_like(r.acc0)

    def inner_norm_back(which, first, count, size, grad_store, acc_ref=None):
        gain = r.gains[which : which + 1, :]
        xhat_ref, slope_ref, scale_ref = (
            (r.xhat1, r.slope1, r.scale1),
            (r.xhat2, r.slope2, r.scale2),
        )[which]

        def body(i, carry):
            row = pl.multiple_of(first + i * size, 16)
            xhat = cells(xhat_ref, row, size)
            dpre = cells(r.hid, row, size) * cells(slope_ref, row, size)
            if acc_ref is not None:
                dgain = dpre * xhat
                acc_ref[...] += sum(dgain[n : n + 8] for n in range(0, size, 8))
            dx = dpre * gain
            plain = jnp.sum(dx, axis=1, keepdims=True) / H
            cross = jnp.sum(dx * xhat, axis=1, keepdims=True) / H
            grad_store(row, cells(scale_ref, row, size) * (dx - plain - xhat * cross))
            return carry

        lax.fori_loop(0, count, body, 0)

    dhid2 = r.dhid2
    dhid2[0:PAD, :] = jnp.zeros((PAD, HP), F32)
    dhid2[PAD + E :, :] = jnp.zeros((PAD, HP), F32)

    def keep_dhid2(row, grad):
        dhid2[pl.ds(pl.multiple_of(row + PAD, 8), grad.shape[0]), :] = grad.astype(BF16).astype(F32)

    inner_norm_back(1, 0, 1, RIM, keep_dhid2)
    inner_norm_back(1, RIM, N // BLOCK, BLOCK, keep_dhid2, r.acc2)
    inner_norm_back(1, RIM + N, 1, RIM, keep_dhid2)

    to_plane(3)
    for k in some_rest:
        add_swapped(k)
        z_start(k)

    dhid2_t = dhid2[PAD + RIM : PAD + RIM + N, :].T.astype(BF16)
    grad_units(z.nd, dhid2_t, lambda c, w: taps[own, c : c + w], TAPS * z.nh)
    swap(2)
    swap(1)

    back = r.back
    for j, offset in enumerate(OFFSETS):
        first = PAD + RIM + offset
        back[:, j * HP : (j + 1) * HP] = (
            dhid2[first : first + N, :] * r.mask[RIM : RIM + N, j : j + 1]
        ).astype(BF16)
    total = None
    for j in range(TAPS):
        term = jnp.dot(
            back[:, j * HP : (j + 1) * HP], tap_weight(TAPS - 1 - j), preferred_element_type=F32
        )
        total = term if total is None else total + term
    r.hid[RIM : RIM + N, :] = total

    to_plane(2)
    dhid1 = r.dhid1

    def keep_dhid1(row, grad):
        dhid1[pl.ds(pl.multiple_of(row - RIM, 16), grad.shape[0]), :] = grad.astype(BF16)

    inner_norm_back(0, RIM, N // BLOCK, BLOCK, keep_dhid1, r.acc1)

    big[...] = jnp.dot(dhid1[...], first_weight(), preferred_element_type=F32)

    def first_norm_back(i, carry):
        row = pl.multiple_of(i * BLOCK, BLOCK)
        wide = pl.multiple_of(row + RIM, 16)
        scale = cells(r.scale0, wide, BLOCK)
        xhat = (cells(xe, wide, BLOCK).astype(F32) - cells(r.mean0, wide, BLOCK)) * scale
        dpre = cells(big, row, BLOCK) * cells(r.slope0, wide, BLOCK)
        dgain = dpre * xhat
        r.acc0[...] += sum(dgain[n : n + 8] for n in range(0, BLOCK, 8))
        dx = dpre * gain0
        plain = jnp.sum(dx, axis=1, keepdims=True) / D
        cross = jnp.sum(dx * xhat, axis=1, keepdims=True) / D
        grad = scale * (dx - plain - xhat * cross)
        r.gi_own[pl.ds(row, BLOCK), :] = (cells(cote, wide, BLOCK).astype(F32) + grad).astype(BF16)
        return carry

    gi, gi_own = r.gi, r.gi_own
    parts = 4
    part = N // parts
    per_part = part // min(part, BLOCK)
    row_bases = {}
    core_rows = gi.at[pl.ds(0, Z)]
    for_rows = shared(core_rows)

    def rows_along(qs, js, at_end):
        def onward(j, place):
            return [remote(place, place, partner, *for_rows)]

        for j in js:
            for q in qs:
                span = pl.ds(q * part, part)
                place = gi.at[2 * origins[j] + core, span]
                take(row_bases[q], j, place, onward, at_end)

    def rows_own(q):
        span = pl.ds(q * part, part)
        return send_own(row_bases[q], gi_own.at[span], gi.at[t, span], q >= 2)

    later = []
    for q in range(parts):
        lax.fori_loop(q * per_part, (q + 1) * per_part, first_norm_back, 0)
        span = pl.ds(q * part, part)
        row_bases[q] = arrivals(Z)
        later.append(rows_own(q))
        push(gi_own.at[span], gi.at[t, span], partner, *for_rows)
    own_row = move(gi_own, gi.at[t])
    turn_plane(3)

    vec = r.vec
    sum0 = jnp.sum(r.acc0[...], axis=0, keepdims=True)
    sum1 = jnp.sum(r.acc1[...], axis=0, keepdims=True)
    sum2 = jnp.sum(r.acc2[...], axis=0, keepdims=True)
    vec[...] = jnp.zeros_like(vec)
    for j in range(z.nd):
        vec[j : j + 1, :] = sum0[:, j * LANES : (j + 1) * LANES]
    for j in range(z.nh):
        vec[z.nd + j : z.nd + j + 1, :] = sum1[:, j * LANES : (j + 1) * LANES]
        vec[z.nd + z.nh + j : z.nd + z.nh + j + 1, :] = sum2[:, j * LANES : (j + 1) * LANES]
    vec_plane = shared(r.vec_plane.at[pl.ds(1, S - 1)])
    for i in range(1, S):
        push(vec, r.vec_plane.at[i], (seq_at(i), t), *vec_plane)

    dhid1_t = dhid1[...].astype(F32).T.astype(BF16)
    grad_units(0, dhid1_t, lambda c, w: r.act0[own, c : c + w], z.nd)
    swap(0)
    to_plane(1)
    turn_plane(2)
    to_plane(0)
    to_z(3)
    z_start(3)
    later[2]()
    rows_along([0, 1], [1], False)
    for k in some_rest:
        z_over(k)
    z_over(3)
    turn_plane(1)
    to_z(2)
    z_start(2)
    later[3]()
    rows_along([0], [2], False)
    rows_along([2], [1], False)
    rows_along([1], [2], False)

    arrived(vec_plane[0], r.vec_plane.at[pl.ds(1, S - 1)])
    vec_sum = r.vec_sum
    vec_sum[...] = sum((r.vec_plane[i] for i in range(1, S)), vec[...])
    vec_z = shared(r.vec_z.at[pl.ds(0, Z - 1)])
    for i in range(1, Z):
        push(vec_sum, r.vec_z.at[i - 1], dev_z(i), *vec_z)

    turn_plane(0)
    z_over(2)
    rows_along([2], [2], False)
    for k in some_rest:
        z_middle(k)
    z_middle(3)
    rows_along([3], [1], False)
    to_z(1)
    z_start(1)
    rows_along([0], [3], False)
    to_z(0)
    z_start(0)
    z_over(1)
    z_middle(2)
    rows_along([1], [3], False)
    for k in some_rest:
        to_all(k)
    to_all(3)
    z_over(0)
    rows_along([3], [2], False)
    z_middle(1)
    rows_along([2], [3], False)
    rows_along([0, 1, 2, 3], [1], True)
    rows_along([0, 1], [2], True)
    z_middle(0)
    to_all(2)
    to_all(1)
    to_all(0)
    rows_along([3], [3], False)
    rows_along([2, 3], [2], True)
    rows_along([0, 1], range(3, Z), True)

    arrived(vec_z[0], r.vec_z.at[pl.ds(0, Z - 1)])
    vec_half = r.vec_half
    vec_half[...] = sum((r.vec_z[i - 1] for i in range(1, Z)), vec_sum[...])
    vec_core = push(vec_half, r.gain_sums.at[1], partner)
    own_sums.append(move(vec_half, r.gain_sums.at[0]))
    rows_along([2, 3], range(3, Z), True)
    arrived(spread_out[0], some_sums)

    vec_core.wait_recv()
    if z.rest:
        rest_end()
    for copy in own_sums:
        copy.wait()
    out_own.wait()
    arrived(for_out[0], some_out)
    own_row.wait()
    arrived(for_rows[0], core_rows)
    assert all(n <= sems.shape[0] for n, sems in zip(counts, (send, recv, local)))
    for copy in sent:
        copy.wait_send()
    for sends, place in together:
        remote(place, place, partner, 0, sends).wait_send()
    for when, copy in sent_if:

        @pl.when(when)
        def _():
            copy.wait_send()


def finish(z, *refs):
    got, gi_got, ff, gain_sums = refs[:4]
    out, gi, grad_first, grad_conv, grad_last, grad_gain, grad_gain1, grad_gain2, *refs = refs[4:]
    first, conv, last, gains, sems = refs
    t = lax.axis_index("tp")
    copies = []

    def move(src, dst):
        copy = pltpu.make_async_copy(src, dst, sems.at[len(copies)])
        copy.start()
        copies.append(copy)

    for i in range(z.R):
        move(gi_got.at[i], gi.at[i])
    move(got, out)

    def summed(start, count):
        return jnp.concatenate(
            [ff[u % z.S, u // z.S].astype(F32) for u in range(start, start + count)], axis=1
        )

    first[...] = summed(0, z.nd)
    move(first, grad_first)
    for k in range(TAPS):
        conv[k] = summed(z.nd + k * z.nh, z.nh)
    move(conv, grad_conv)
    last[...] = summed(z.nd + TAPS * z.nh, z.nd)
    move(last, grad_last)
    sums = gain_sums[0] + gain_sums[1]

    def line(start, count):
        return jnp.concatenate([sums[j : j + 1, :] for j in range(start, start + count)], axis=1)

    def picked(row, width, step):
        return sum(
            jnp.where(t == j, row[:, j * step : j * step + width], 0.0) for j in range(z.T)
        )

    grad_gain[...] = picked(line(0, z.nd), z.Dt, z.Dt)
    grad_gain1[...] = picked(line(z.nd, z.nh), z.Hs, z.Hp)
    grad_gain2[...] = picked(line(z.nd + z.nh, z.nh), z.Hs, z.Hp)
    for copy in copies:
        copy.wait()


def shards(
    mesh,
    inputs,
    starts,
    first_proj,
    dilated_conv,
    last_proj,
    first_norm_gain,
    second_norm_gain,
    third_norm_gain,
    cotangent,
):
    z = Sizes(mesh, inputs, starts, first_proj, cotangent)
    S, T, Z, N, D, E, HP, Hp, NR = z.S, z.T, z.Z, z.N, z.D, z.E, z.HP, z.Hp, z.NR
    more = Hp - z.Hs
    first, last = first_proj.T, last_proj
    conv = dilated_conv.transpose(0, 2, 1)
    if more:
        first, last = (jnp.pad(part, ((0, more), (0, 0))) for part in (first, last))
        conv = jnp.pad(
            conv.reshape(TAPS, z.Hs, T, z.Hs), ((0, 0), (0, more), (0, 0), (0, more))
        ).reshape(TAPS, Hp, HP)
    vm, anywhere = pltpu.VMEM, pl.ANY
    ins = dict(
        x=(inputs, anywhere),
        starts=(starts, vm),
        w1=(first, anywhere),
        wc=(conv, anywhere),
        w3=(last, anywhere),
        g1=(first_norm_gain.reshape(z.nd, LANES), vm),
        g2=(second_norm_gain.reshape(1, z.Hs), vm),
        g3=(third_norm_gain.reshape(1, z.Hs), vm),
        cot=(cotangent.transpose(0, 2, 1), anywhere),
    )
    outs = dict(
        out=((z.R, z.Dt, N), BF16),
        gi=((z.R, N, D), BF16),
        ff=((S, NR, Hp, LANES), BF16),
        gain_sums=((2, 24, LANES), F32),
    )
    NB = z.NF + z.rest
    near = vm if z.line else jax.ShapeDtypeStruct
    scratch = dict(
        send=pltpu.SemaphoreType.DMA((105 if z.line else 800,)),
        recv=pltpu.SemaphoreType.DMA((128 if z.line else 800,)),
        local=pltpu.SemaphoreType.DMA((14,)),
        xe=vm((E, D), BF16),
        cote=vm((E, D), BF16),
        act0=vm((E, D), BF16),
        slope0=vm((E, D), F32),
        mean0=vm((E, 1), F32),
        scale0=vm((E, 1), F32),
        mask=vm((E, LANES), F32),
        flags_left=vm((z.R, N), jnp.int32),
        flags_right=vm((z.R, N), jnp.int32),
        gslots=vm((T, 8, LANES), F32),
        gains=vm((8, HP), F32),
        wg=vm((S, NR, Z, 2, Hp, LANES), BF16),
        hid=vm((E, HP), F32),
        xhat1=vm((E, HP), F32),
        slope1=vm((E, HP), F32),
        scale1=vm((E, 1), F32),
        xhat2=vm((E, HP), F32),
        slope2=vm((E, HP), F32),
        scale2=vm((E, 1), F32),
        act1=vm((E + 2 * PAD, HP), F32),
        dhid2=vm((E + 2 * PAD, HP), F32),
        taps=vm((E, TAPS * HP), BF16),
        back=vm((N, TAPS * HP), BF16),
        act2=vm((E, HP), BF16),
        dhid1=vm((N, HP), BF16),
        big=vm((N, D), F32),
        gi_own=vm((N, D), BF16),
        acc0=vm((8, D), F32),
        acc1=vm((8, HP), F32),
        acc2=vm((8, HP), F32),
        cot_t=vm((D, N), BF16),
        out_t=vm((D, N), BF16),
        w1_in=vm((Hp, D), BF16),
        wc_in=vm((TAPS, Hp, HP), BF16),
        w3_in=vm((Hp, D), BF16),
        gl=vm((8, LANES), F32),
        g=vm((S, NR, Z, 2, Hp, LANES), BF16),
        rc=vm((S, NR, Z, Hp, LANES), BF16),
        ff_own=vm((NB, Hp, LANES), BF16),
        vec=vm((24, LANES), F32),
        vec_sum=vm((24, LANES), F32),
        vec_plane=vm((S, 24, LANES), F32),
        vec_z=vm((Z, 24, LANES), F32),
        vec_half=vm((24, LANES), F32),
    )
    if z.line:
        scratch.update(rz_end=vm((NB, 3, Hp, LANES), BF16))
        scratch.update(rz_pair=vm((NB, 2, Hp, LANES), BF16), rz_one=vm((NB, Hp, LANES), BF16))
    if z.rest:
        scratch.update(others=vm((S, z.rest, Hp, LANES), BF16))
        scratch.update(rest_sum=vm((z.rest, Hp, LANES), BF16))
    else:
        scratch.update(rz=vm((Z, NB, Hp, LANES), BF16))
    if z.square:
        scratch.update(rx=vm((2, NR, Z // 2, Hp, LANES), BF16))
        scratch.update(ry=vm((2, NR, Z // 2, Hp, LANES), BF16))
        scratch.update(rx2=vm((NR, Z // 2, Hp, LANES), BF16))
        scratch.update(ry2=vm((NR, Z // 2, Hp, LANES), BF16))
    else:
        scratch.update(rd=vm((S, NR, Z, Hp, LANES), BF16))
    names = [*ins, *outs, *scratch]
    results = pl.pallas_call(
        functools.partial(kernel, z, names),
        out_shape=[near(shape, kind) for shape, kind in outs.values()],
        in_specs=[pl.BlockSpec(memory_space=space) for _, space in ins.values()],
        out_specs=[pl.BlockSpec(memory_space=anywhere)] * len(outs),
        scratch_shapes=list(scratch.values()),
        compiler_params=pltpu.CompilerParams(
            collective_id=0, has_side_effects=True, vmem_limit_bytes=(50 if z.line else 63) * 2**20
        ),
    )(*[array for array, _ in ins.values()])
    if z.line:
        results = [pltpu.with_memory_space_constraint(part, vm) for part in results]
    shape = jax.ShapeDtypeStruct
    out, gi, grad_first, grad_conv, grad_last, grad_gain, grad_gain1, grad_gain2 = pl.pallas_call(
        functools.partial(finish, z),
        out_shape=[
            shape((z.R, z.Dt, N), BF16),
            shape((z.R, N, D), BF16),
            shape((Hp, D), F32),
            shape((TAPS, Hp, HP), F32),
            shape((Hp, D), F32),
            shape((1, z.Dt), F32),
            shape((1, z.Hs), F32),
            shape((1, z.Hs), F32),
        ],
        in_specs=[pl.BlockSpec(memory_space=space) for space in (anywhere, anywhere, vm, vm)],
        out_specs=[pl.BlockSpec(memory_space=space) for space in [anywhere] * 5 + [vm] * 3],
        scratch_shapes=[
            vm((Hp, D), F32),
            vm((TAPS, Hp, HP), F32),
            vm((Hp, D), F32),
            vm((8, LANES), F32),
            pltpu.SemaphoreType.DMA((z.R + 4,)),
        ],
        compiler_params=pltpu.CompilerParams(vmem_limit_bytes=12 * 2**20),
    )(*results)
    if more:
        grad_first, grad_last = grad_first[: z.Hs], grad_last[: z.Hs]
        grad_conv = grad_conv.reshape(TAPS, Hp, T, Hp)[:, : z.Hs, :, : z.Hs]
        grad_conv = grad_conv.reshape(TAPS, z.Hs, z.H)
    return (
        out.transpose(0, 2, 1),
        gi,
        grad_first.T,
        grad_conv.transpose(0, 2, 1),
        grad_last,
        grad_gain.reshape(-1),
        grad_gain1.reshape(-1),
        grad_gain2.reshape(-1),
    )


def solution(mesh):
    placed = (
        P(None, "seq", None),
        P(None, "seq"),
        P(None, "tp"),
        P(None, None, "tp"),
        P("tp", None),
        P(),
        P("tp"),
        P("tp"),
        P(None, "seq", "tp"),
    )
    return jax.shard_map(
        functools.partial(shards, mesh),
        mesh=mesh,
        in_specs=placed,
        out_specs=(
            P(None, "seq", "tp"),
            P(None, "seq", None),
            P(None, "tp"),
            P(None, None, "tp"),
            P("tp", None),
            P("tp"),
            P("tp"),
            P("tp"),
        ),
        check_vma=False,
    )
```

```python
import functools
from types import SimpleNamespace

import jax
import jax.numpy as jnp
from jax import lax
from jax.experimental import pallas as pl
from jax.experimental.pallas import tpu as pltpu
from jax.sharding import PartitionSpec as P

MESH = pl.DeviceIdType.MESH
F32 = jnp.float32
BF16 = jnp.bfloat16

TAPS = 5
STEP = 2
REACH = 4
EPS = 1e-05
LANES = 128
RIM = 16
PAD = 8
STAGES = 4
REST, FULL = STAGES, STAGES + 1
BLOCK = 64
HALF_ROOT = 0.7071067811865476
PEAK = 0.3989422804014327

NT = (((1,), (1,)), ((), ()))
OFFSETS = [STEP * k - REACH for k in range(TAPS)]


class Sizes:
    def __init__(self, mesh, inputs, starts, first_proj, cotangent):
        self.S = mesh.shape["seq"]
        self.T = mesh.shape["tp"]
        self.Z = self.T // 2
        self.R, self.N, self.D = inputs.shape
        assert self.R == self.T and self.N % LANES == 0
        self.Hs = first_proj.shape[1]
        self.H = self.Hs * self.T
        self.Hp = -(-self.Hs // 16) * 16
        self.HP = self.Hp * self.T
        assert self.HP % LANES == 0 and self.D % LANES == 0
        self.E = self.N + 2 * RIM
        self.nd = self.D // LANES
        self.nh = self.HP // LANES
        self.units = 2 * self.nd + TAPS * self.nh
        one, two = -(-self.nd // self.S), -(-(self.nd + TAPS * self.nh) // self.S)
        whole = self.units // self.S
        self.rest = self.units % self.S if whole > two else 0
        self.NF = whole if self.rest else -(-self.units // self.S)
        self.NR = self.NF + (self.rest > 0)
        self.chunks = [(0, one), (one, (one + two) // 2), ((one + two) // 2, two), (two, self.NF)]
        self.Dt = cotangent.shape[2]
        assert self.Dt % 16 == 0
        self.full = self.NF - 1 if self.rest and self.NF - 1 > two else None
        self.ahead = list(self.chunks)
        if self.full is not None:
            self.ahead[3] = (two, self.full)
        self.square = self.S == 4
        self.line = self.Z == 4


def cells(ref, row, count):
    return ref[pl.ds(row, count), :]


def gelu_parts(v):
    whole = 0.5 * (1.0 + lax.erf(v * HALF_ROOT))
    slope = whole + v * (PEAK * jnp.exp(-0.5 * v * v))
    return v * whole, slope


def kernel(z, names, *refs):
    r = SimpleNamespace(**dict(zip(names, refs, strict=True)))
    S, T, Z, N, D, E, H, Hp, HP, NR = z.S, z.T, z.Z, z.N, z.D, z.E, z.H, z.Hp, z.HP, z.NR
    s, t = lax.axis_index("seq"), lax.axis_index("tp")
    core, layer = lax.rem(t, 2), t // 2
    partner = (s, t + 1 - 2 * core)

    send, recv, local = r.send, r.recv, r.local
    counts = [0, 0, 0]
    sent, sent_if, together, together_if = [], [], [], []

    def remote(src, dst, device, arrival=None, sends=None):
        return pltpu.make_async_remote_copy(
            src_ref=src,
            dst_ref=dst,
            send_sem=send.at[sendings() if sends is None else sends],
            recv_sem=recv.at[arrivals(1) if arrival is None else arrival],
            device_id=device,
            device_id_type=MESH,
        )

    def sendings():
        counts[0] += 1
        return counts[0] - 1

    def arrivals(count):
        counts[1] += count
        return counts[1] - count

    def shared(place):
        pair = (arrivals(1), sendings())
        together.append((pair[1], place))
        return pair

    def arrived(arrival, place):
        remote(place, place, partner, arrival, 0).wait_recv()

    def push(src, dst, device, arrival=None, sends=None):
        copy = remote(src, dst, device, arrival, sends)
        copy.start()
        if sends is None:
            sent.append(copy)
        return copy

    def push_if(when, copy):
        @pl.when(when)
        def _():
            copy.start()

        sent_if.append((when, copy))

    def move(src, dst):
        counts[2] += 1
        copy = pltpu.make_async_copy(src, dst, local.at[counts[2] - 1])
        copy.start()
        return copy

    def z_at(i):
        return lax.rem(layer + i + Z, Z)

    def dev_z(i):
        return (s, 2 * z_at(i) + core)

    def seq_at(i):
        return lax.rem(s + i + S, S)

    steps = range(1, Z)
    if z.line:
        upper = layer // 2
        inner = lax.rem((layer + 1) // 2, 2)
        end, middle = 3 * upper, 1 + upper
        first = inner * (3 - layer) + (1 - inner) * middle
        second = inner * end + (1 - inner) * (3 - middle)
        origins = [None, first, second, 3 - end]
        own_to = [(first, 2 - inner), (end, 1)]
        passed = {1: (end, 2), 2: (3 - layer, 3), 3: (end, 3)}
    else:
        origins = [None] + [z_at(-i) for i in steps]
        own_to = [(z_at(i), i) for i in steps]
        passed, inner = {}, 0

    def at_layer(to):
        return (s, 2 * to + core)

    def only(at_end, go):
        if z.line:
            pl.when(inner == 1 - at_end)(go)
        elif at_end:
            go()

    def send_own(base, src, place, later=False):
        copies = [remote(src, place, at_layer(to), base + j - 1, streams[base]) for to, j in own_to]
        if z.line:
            pl.when(inner == 1)(copies.pop().start)
        later = later and z.line
        for copy in copies:
            if later:
                pl.when(inner == 1)(copy.start)
            else:
                copy.start()
        return (lambda: pl.when(inner == 0)(copies[0].start)) if later else (lambda: None)

    def take(base, j, place, onward, at_end, start=True):
        if base + j not in onwards:
            extra = None
            if j in passed:
                to, then = passed[j]
                extra = remote(place, place, at_layer(to), base + then - 1, streams[base])
            onwards[base + j] = (extra, onward(j, place))

        def go():
            extra, copies = onwards[base + j]
            arrived(base + j - 1, place)
            if extra is not None and not at_end:
                extra.start()
            if start:
                for copy in copies:
                    copy.start()

        only(at_end, go)

    onwards, streams = {}, {}

    def stream(one, most):
        base = arrivals(Z - 1)
        streams[base] = sendings()
        if z.line:
            together_if.append((inner == 0, streams[base], one))
            together_if.append((inner == 1, streams[base], most))
        else:
            together.append((streams[base], most))
        return base

    right, left = (seq_at(1), t), (seq_at(-1), t)
    if z.square:
        sx, sy, sd = s ^ 1, s ^ 2, s ^ 3
        x_side, y_side = (sx, t), (sy, t)

    xe, cot, cot_t = r.xe, r.cot, r.cot_t

    def features(who):
        return pl.ds(pl.multiple_of(who * z.Dt, 16), z.Dt)

    weights_in = [move(r.w1, r.w1_in), move(r.wc, r.wc_in), move(r.w3, r.w3_in)]
    row_in = move(r.x.at[t], xe.at[pl.ds(RIM, N)])
    cot_own = move(cot.at[t], cot_t.at[features(t)])

    barrier = pltpu.get_barrier_semaphore()
    for i in range(1, T):
        pl.semaphore_signal(barrier, inc=1, device_id=(s, lax.rem(t + i, T)), device_id_type=MESH)
    for i in range(1, S):
        pl.semaphore_signal(barrier, inc=1, device_id=(seq_at(i), t), device_id_type=MESH)
    pl.semaphore_wait(barrier, T + S - 2)

    rim_r = push(r.x.at[t, pl.ds(N - RIM, RIM)], xe.at[pl.ds(0, RIM)], right)
    rim_l = push(r.x.at[t, pl.ds(0, RIM)], xe.at[pl.ds(RIM + N, RIM)], left)
    flags_r = push(r.starts, r.flags_left, right)
    flags_l = push(r.starts, r.flags_right, left)
    r.gl[0:1, : z.Hs] = r.g2[...]
    r.gl[1:2, : z.Hs] = r.g3[...]
    some_gains = r.gslots.at[pl.ds(0, T - 1)]
    for_gains = shared(some_gains)
    for i in range(1, T):
        push(r.gl, r.gslots.at[t], (s, lax.rem(t + i, T)), *for_gains)
    gain_own = move(r.gl, r.gslots.at[t])

    wg = r.wg
    bases, plane, corner = {}, {}, {}
    plane_x, plane_y, plane_d, plane_any, across = {}, {}, {}, {}, {}

    def unit_in(u):
        if u < z.nd:
            return r.w1_in[:, u * LANES : (u + 1) * LANES]
        u -= z.nd
        if u < TAPS * z.nh:
            return r.wc_in[u // z.nh, :, u % z.nh * LANES : (u % z.nh + 1) * LANES]
        u -= TAPS * z.nh
        if u < z.nd:
            return r.w3_in[:, u * LANES : (u + 1) * LANES]
        return jnp.zeros((Hp, LANES), BF16)

    cuts = list(z.ahead)

    def rounds(k):
        a, b = cuts[k]
        return pl.ds(a, b - a)

    def carried(ref, k, which, c):
        if k == REST:
            return ref.at[pl.ds(0, z.rest), z.NF, which, c]
        if k == FULL:
            return ref.at[:, z.full, which, c]
        return ref.at[s, rounds(k), which, c]

    def every(ref, k, which, c):
        return carried(ref, k, which, c) if k >= REST else ref.at[:, rounds(k), which, c]

    every_chip = pl.ds(0, Z)

    def weights_own(k):
        if k == REST:
            for q in range(z.rest):
                wg[q, z.NF, layer, core] = unit_in(z.NF * S + q)
        elif k == FULL:
            for q in range(S):
                wg[q, z.full, layer, core] = unit_in(z.full * S + q)
        else:
            for q in range(S):
                for n in range(*cuts[k]):
                    wg[q, n, layer, core] = unit_in(n * S + q)
        place = carried(wg, k, layer, core)
        count = place.shape[0]
        if z.line:
            most = wg.at[pl.ds(0, count), pl.ds(0, Z + 1), 0, 0]
        else:
            most = wg.at[0, pl.ds(0, count), pl.ds(0, Z - 1), 0]
        bases[k] = stream(place, most)
        send_own(bases[k], place, place)
        across[k] = shared(every(wg, k, every_chip, core))
        place = every(wg, k, layer, core)
        push(place, place, partner, *across[k])
        if k < REST:
            copies = S if z.square else S - 1
            plane[k] = sendings()
            together.append(
                (plane[k], wg.at[pl.ds(0, copies - z.square), rounds(k), pl.ds(0, Z - 1), core])
            )

    def weights_along(k, at_end, js=steps, start=True):
        def onward(j, place):
            if k >= REST:
                return [remote(place, place, partner, *across[k])]
            if not z.square:
                plane_any[k, j] = [
                    remote(place, place, (seq_at(i), t), None, plane[k]) for i in range(1, S)
                ]
                return plane_any[k, j]
            plane_x[k, j] = remote(place, place, x_side, None, plane[k])
            plane_y[k, j] = remote(place, place, y_side, None, plane[k])
            return [plane_x[k, j], plane_y[k, j]]

        for j in js:
            take(bases[k], j, carried(wg, k, origins[j], core), onward, at_end, start)

    def weights_spread(k, js=steps):
        def go():
            for j in js:
                for copy in onwards[bases[k] + j][1]:
                    copy.start()

        only(False, go)

    def weights_corner(k, at_end):
        if not z.square:
            return
        if k not in corner:
            corner[k] = arrivals(1)
        for j in steps:
            if (k, j) not in plane_d:
                over_y = (k + j) % 2
                place = wg.at[sx if over_y else sy, rounds(k), origins[j], core]
                side = y_side if over_y else x_side
                plane_d[k, j] = remote(place, place, side, corner[k], plane[k])

        def go():
            for j in steps:
                plane_x[k, j].wait_recv()
                plane_y[k, j].wait_recv()
                plane_d[k, j].start()
                for q in (s, sx, sy):
                    place = wg.at[q, rounds(k), origins[j], core]
                    push(place, place, partner, *across[k])

        only(at_end, go)

    def weights_across(k):
        if z.square:
            arrived(corner[k], wg.at[0, rounds(k), pl.ds(0, Z - 1), core])
        for j in steps:
            place = wg.at[sd if z.square else pl.ds(0, S), rounds(k), origins[j], core]
            if not z.square:
                for copy in plane_any[k, j]:
                    copy.wait_recv()
            push(place, place, partner, *across[k])

    def weights_ready(k):
        arrived(across[k][0], every(wg, k, every_chip, 1 - core))

    some_cot = cot_t.at[pl.ds(0, (T - 1) * z.Dt)]
    for_cot = shared(some_cot)

    def cotangent_out(at_end, to_end):
        def go():
            for i in range(1, T):
                to = lax.rem(t + i, T)

                def one():
                    push(cot.at[to], cot_t.at[features(t)], (s, to), *for_cot)

                if z.line:
                    pl.when(lax.rem((to // 2 + 1) // 2, 2) == 1 - to_end)(one)
                elif to_end:
                    one()

        only(at_end, go)

    weights_in[0].wait()
    weights_in[1].wait()
    weights_own(0)
    weights_own(1)
    weights_in[2].wait()
    weights_own(2)
    weights_own(3)
    some_rest = [REST] if z.rest else []
    by_all = some_rest if z.full is None else [FULL, REST]
    def unit(ref, u):
        return ref[u % S, u // S].reshape(HP, LANES)

    def weights(first, count):
        return jnp.concatenate([unit(wg, u) for u in range(first, first + count)], axis=1)

    def first_weight():
        return weights(0, z.nd)

    def tap_weight(k):
        return weights(z.nd + k * z.nh, z.nh)

    def last_weight():
        return weights(z.nd + TAPS * z.nh, z.nd)

    row_in.wait()

    gain0 = jnp.concatenate([r.g1[j : j + 1, :] for j in range(z.nd)], axis=1)

    def first_norm(first, count, size):
        def body(i, carry):
            row = pl.multiple_of(first + i * size, 16)
            v = cells(xe, row, size).astype(F32)
            mean = jnp.sum(v, axis=1, keepdims=True) / D
            spread = jnp.sum(v * v, axis=1, keepdims=True) / D - mean * mean
            scale = lax.rsqrt(spread + EPS)
            act, slope = gelu_parts((v - mean) * scale * gain0)
            r.act0[pl.ds(row, size), :] = act.astype(BF16)
            r.slope0[pl.ds(row, size), :] = slope
            r.mean0[pl.ds(row, size), :] = mean
            r.scale0[pl.ds(row, size), :] = scale
            return carry

        lax.fori_loop(0, count, body, 0)

    first_norm(RIM, N // BLOCK, BLOCK)

    for k in range(STAGES):
        weights_along(k, False, steps[:2], k < 2)
        weights_along(k, True, steps[:1])
    for k in by_all:
        weights_own(k)
    rim_r.wait_recv()
    rim_l.wait_recv()
    first_norm(0, 1, RIM)
    first_norm(RIM + N, 1, RIM)

    gain_own.wait()
    arrived(for_gains[0], some_gains)
    for j in range(T):
        r.gains[0:2, j * Hp : (j + 1) * Hp] = r.gslots[j, 0:2, :Hp]

    flags_r.wait_recv()
    flags_l.wait_recv()
    here = r.starts[pl.ds(t, 1), :]
    before = r.flags_left[pl.ds(t, 1), :]
    after = r.flags_right[pl.ds(t, 1), :]
    window = jnp.concatenate([before[:, N - LANES :], here, after[:, :LANES]], axis=1).astype(F32)
    window = jnp.broadcast_to(window, (E, N + 2 * LANES))
    at = lax.broadcasted_iota(jnp.int32, window.shape, 1) - LANES
    place = lax.broadcasted_iota(jnp.int32, window.shape, 0) - RIM
    rows = lax.broadcasted_iota(jnp.int32, (E, 1), 0) - RIM + s * N
    for k, offset in enumerate(OFFSETS):
        low, high = min(offset, 0), max(offset, 0)
        begun = jnp.sum(
            jnp.where((at > place + low) & (at <= place + high), window, 0.0), axis=1, keepdims=True
        )
        moved = rows + offset
        inside = (begun == 0.0) & (moved >= 0) & (moved < S * N)
        r.mask[:, k : k + 1] = inside.astype(F32)

    third = steps[2:]
    weights_along(0, False, third)
    weights_along(0, True, [2])
    weights_along(1, False, third)
    cotangent_out(False, False)
    weights_along(1, True, [2])
    weights_along(2, False, third, False)
    weights_along(2, True, [2])
    weights_along(3, False, third, False)
    weights_corner(0, False)
    weights_spread(2)
    weights_along(0, True, third)
    cotangent_out(True, False)
    weights_along(1, True, third)
    weights_along(3, True, [2])
    weights_along(2, True, third)
    weights_corner(0, True)
    weights_corner(1, False)
    weights_along(3, True, third)
    weights_corner(1, True)
    weights_spread(3)
    weights_corner(2, True)
    cotangent_out(True, True)
    for k in by_all:
        weights_along(k, False, steps[:2])
    weights_across(0)
    cotangent_out(False, True)

    weights_ready(0)
    r.hid[...] = lax.dot_general(r.act0[...], first_weight(), NT, preferred_element_type=F32)
    weights_corner(2, False)
    weights_corner(3, True)
    weights_across(1)

    def inner_norm(which, act_store, first, count, size):
        gain = r.gains[which : which + 1, :]
        xhat_ref, slope_ref, scale_ref = (
            (r.xhat1, r.slope1, r.scale1),
            (r.xhat2, r.slope2, r.scale2),
        )[which]

        def body(i, carry):
            row = pl.multiple_of(first + i * size, 16)
            v = cells(r.hid, row, size)
            mean = jnp.sum(v, axis=1, keepdims=True) / H
            spread = jnp.sum(v * v, axis=1, keepdims=True) / H - mean * mean
            scale = lax.rsqrt(spread + EPS)
            xhat = (v - mean) * scale
            act, slope = gelu_parts(xhat * gain)
            act_store(row, act)
            xhat_ref[pl.ds(row, size), :] = xhat
            slope_ref[pl.ds(row, size), :] = slope
            scale_ref[pl.ds(row, size), :] = scale
            return carry

        lax.fori_loop(0, count, body, 0)

    act1, taps = r.act1, r.taps
    act1[0:PAD, :] = jnp.zeros((PAD, HP), F32)
    act1[PAD + E :, :] = jnp.zeros((PAD, HP), F32)

    def keep_act1(row, act):
        act1[pl.ds(pl.multiple_of(row + PAD, 8), act.shape[0]), :] = act.astype(BF16).astype(F32)

    inner_norm(0, keep_act1, RIM, N // BLOCK, BLOCK)
    inner_norm(0, keep_act1, 0, 1, RIM)
    inner_norm(0, keep_act1, RIM + N, 1, RIM)
    for k, offset in enumerate(OFFSETS):
        taps[:, k * HP : (k + 1) * HP] = (
            act1[PAD + offset : PAD + offset + E, :] * r.mask[:, k : k + 1]
        ).astype(BF16)


    def tap_term(k):
        return lax.dot_general(
            taps[:, k * HP : (k + 1) * HP], tap_weight(k), NT, preferred_element_type=F32
        )

    cote = r.cote
    edge_r = remote(cote.at[pl.ds(N, RIM)], cote.at[pl.ds(0, RIM)], right)
    edge_l = remote(cote.at[pl.ds(RIM, RIM)], cote.at[pl.ds(RIM + N, RIM)], left)
    sent.extend([edge_r, edge_l])

    def cotangent_in(at_end):
        def go():
            cot_own.wait()
            arrived(for_cot[0], some_cot)
            cote[RIM : RIM + N, :] = cot_t[...].T
            edge_r.start()
            edge_l.start()

        only(at_end, go)

    cotangent_in(False)
    weights_ready(1)
    total = tap_term(0) + tap_term(1)
    weights_corner(3, False)
    for k in by_all:
        weights_along(k, False, third)
    weights_across(2)
    weights_ready(2)
    for k in range(2, TAPS):
        total = total + tap_term(k)
    r.hid[...] = total
    for k in by_all:
        weights_along(k, True)
    weights_across(3)

    cotangent_in(True)

    act2 = r.act2

    def keep_act2(row, act):
        act2[pl.ds(row, act.shape[0]), :] = act.astype(BF16)

    inner_norm(1, keep_act2, RIM, N // BLOCK, BLOCK)

    for k in [3, *by_all]:
        weights_ready(k)
    big, out_t = r.big, r.out_t
    some_out = r.out.at[pl.ds(0, T - 1)]
    for_out = shared(some_out)
    half_units = z.nd // 2
    own_half = layer // (Z // 2)
    for n in range(2):
        half = own_half if n == 0 else 1 - own_half
        units = [z.nd + TAPS * z.nh + half * half_units + j for j in range(half_units)]
        span = pl.ds(pl.multiple_of(half * half_units * LANES, LANES), half_units * LANES)
        rows = jnp.dot(
            act2[RIM : RIM + N, :],
            jnp.concatenate([unit(wg, u) for u in units], axis=1),
            preferred_element_type=F32,
        )
        rows = rows + xe[RIM : RIM + N, span].astype(F32)
        out_t[span, :] = rows.astype(BF16).T
        for i in range(T // 2):
            to = half * (T // 2) + lax.rem(t + i, T // 2)

            @pl.when(to != t)
            def _():
                push(out_t.at[features(to)], r.out.at[t], (s, to), *for_out)

    out_own = move(out_t.at[features(t)], r.out.at[t])

    cuts[:] = z.chunks

    g = r.g

    def grad_units(first, lhs, rhs, count):
        for j in range(0, count, 2):
            width = min(2, count - j)
            block = jnp.dot(
                lhs, rhs(j * LANES, width * LANES), preferred_element_type=F32
            ).astype(BF16)
            for i in range(width):
                u = first + j + i
                g[u % S, u // S] = block[:, i * LANES : (i + 1) * LANES].reshape(Z, 2, Hp, LANES)

    rc = r.rc
    swaps, plane1, plane2, along_back, first_copies = {}, {}, {}, {}, {}
    some_sums = r.ff.at[pl.ds(0, S - 1), pl.ds(0, z.NF)]
    spread_out = shared(some_sums)
    beside, over, own_sums = {}, {}, []

    for k in [3, *some_rest, 2, 1, 0]:
        place = every(g, k, every_chip, 1 - core)
        to = rc.at[pl.ds(0, z.rest), z.NF] if k == REST else rc.at[:, rounds(k)]
        swaps[k] = remote(place, to, partner)
        sent.append(swaps[k])

    def add_swapped(k):
        swaps[k].wait_recv()
        at_ = [(q, z.NF) for q in range(z.rest)]
        if k != REST:
            at_ = [(q, n) for q in range(S) for n in range(*cuts[k])]
        for q, n in at_:
            g[q, n, :, core] = (g[q, n, :, core].astype(F32) + rc[q, n].astype(F32)).astype(BF16)

    near, far = pl.ds(0, Z // 2), pl.ds(Z // 2, Z // 2)

    def to_plane(k, at_end=None):
        span = rounds(k)
        if k not in plane1:
            if z.square:
                over_x, over_y = shared(r.rx.at[:, span]), shared(r.ry.at[:, span])
                plane1[k] = [(over_x[0], r.rx.at[:, span]), (over_y[0], r.ry.at[:, span])]
                first_copies[k] = [
                    remote(g.at[sx, span, near, core], r.rx.at[0, span], x_side, *over_x),
                    remote(g.at[sd, span, near, core], r.rx.at[1, span], x_side, *over_x),
                    remote(g.at[sy, span, far, core], r.ry.at[0, span], y_side, *over_y),
                    remote(g.at[sd, span, far, core], r.ry.at[1, span], y_side, *over_y),
                ]
            else:
                others = r.rd.at[pl.ds(1, S - 1), span]
                over = shared(others)
                plane1[k] = [(over[0], others)]
                first_copies[k] = [
                    remote(g.at[seq_at(i), span, :, core], r.rd.at[i, span], (seq_at(i), t), *over)
                    for i in range(1, S)
                ]

        def go():
            add_swapped(k)
            for copy in first_copies[k]:
                copy.start()

        go() if at_end is None else only(at_end, go)

    def add_into(q, n, where, other):
        g[q, n, where, core] = (g[q, n, where, core].astype(F32) + other.astype(F32)).astype(BF16)

    def turn_plane(k):
        a, b = cuts[k]
        span = pl.ds(a, b - a)
        for arrival, place in plane1[k]:
            arrived(arrival, place)
        if not z.square:
            return
        for n in range(a, b):
            add_into(sy, n, near, r.rx[1, n])
            add_into(sx, n, far, r.ry[1, n])
        plane2[k] = [
            push(g.at[sy, span, near, core], r.ry2.at[span], y_side),
            push(g.at[sx, span, far, core], r.rx2.at[span], x_side),
        ]
        for n in range(a, b):
            add_into(s, n, near, r.rx[0, n])
            add_into(s, n, far, r.ry[0, n])

    def to_z(k):
        a, b = cuts[k]
        span = pl.ds(a, b - a)
        if z.square:
            for copy in plane2[k]:
                copy.wait_recv()
            for n in range(a, b):
                add_into(s, n, near, r.ry2[n])
                add_into(s, n, far, r.rx2[n])
        else:
            for n in range(a, b):
                sums = g[s, n, :, core].astype(F32)
                for i in range(1, S):
                    sums = sums + r.rd[i, n].astype(F32)
                g[s, n, :, core] = sums.astype(BF16)

    def sums_of(k):
        if k == REST:
            return [(q, z.NF, z.NF + q) for q in range(z.rest)]
        return [(s, n, n) for n in range(*cuts[k])]

    def rows_of(k):
        return pl.ds(z.NF, z.rest) if k == REST else rounds(k)

    def z_start(k):
        if z.line:
            beside[k] = arrivals(1)
            copy = remote(
                carried(g, k, pl.ds(1 - upper, 3), core),
                r.rz_end.at[rows_of(k)],
                at_layer(middle),
                beside[k],
            )
            push_if(inner == 0, copy)
        else:
            along_back[k] = [
                push(carried(g, k, z_at(i), core), r.rz.at[i, rows_of(k)], dev_z(i)) for i in steps
            ]

    def z_over(k):
        if z.line:
            over[k] = arrivals(1)
            pair = pl.ds(2 - 2 * upper, 2)
            copy = remote(
                carried(g, k, pair, core), r.rz_pair.at[rows_of(k)], at_layer(3 - layer), over[k]
            )
            sent_if.append((inner == 1, copy))

            @pl.when(inner == 1)
            def _():
                arrived(beside[k], r.rz_end.at[rows_of(k)])
                for q, n, b in sums_of(k):
                    add_into(q, n, pair, r.rz_end[b, pl.ds(1 - upper, 2)])
                copy.start()

    def z_middle(k):
        if z.line:
            along_back[k] = remote(
                carried(g, k, end, core), r.rz_one.at[rows_of(k)], at_layer(end)
            )
            sent_if.append((inner == 1, along_back[k]))

            @pl.when(inner == 1)
            def _():
                arrived(over[k], r.rz_pair.at[rows_of(k)])
                for q, n, b in sums_of(k):
                    add_into(q, n, pl.ds(2 * upper, 2), r.rz_pair[b])
                along_back[k].start()
                for q, n, b in sums_of(k):
                    sums = g[q, n, layer, core].astype(F32) + r.rz_end[b, 2 * upper].astype(F32)
                    r.ff_own[b] = sums.astype(BF16)

    def to_all(k):
        if z.line:

            @pl.when(inner == 0)
            def _():
                along_back[k].wait_recv()
                for q, n, b in sums_of(k):
                    sums = g[q, n, layer, core].astype(F32) + r.rz_one[b].astype(F32)
                    r.ff_own[b] = sums.astype(BF16)
        else:
            for copy in along_back[k]:
                copy.wait_recv()
            for q, n, b in sums_of(k):
                sums = g[q, n, layer, core].astype(F32)
                for i in steps:
                    sums = sums + r.rz[i, b].astype(F32)
                r.ff_own[b] = sums.astype(BF16)
        place = r.ff_own.at[rows_of(k)]
        for i in range(1, S):
            if k == REST:
                push(place, r.others.at[i], (seq_at(i), t), *for_others)
            else:
                push(place, r.ff.at[s, rounds(k)], (seq_at(i), t), *spread_out)
        if k != REST:
            own_sums.append(move(place, r.ff.at[s, rounds(k)]))

    def rest_end():
        arrived(for_others[0], some_others)
        for q in range(z.rest):
            sums = r.ff_own[z.NF + q].astype(F32)
            for i in range(1, S):
                sums = sums + r.others[i, q].astype(F32)
            r.rest_sum[q] = sums.astype(BF16)
        own_sums.append(move(r.rest_sum, r.ff.at[pl.ds(0, z.rest), z.NF]))

    if z.rest:
        some_others = r.others.at[pl.ds(1, S - 1)]
        for_others = shared(some_others)
    for u in [] if z.rest else range(z.units, S * NR):
        g[u % S, u // S] = jnp.zeros((Z, 2, Hp, LANES), BF16)
    own = slice(RIM, RIM + N)

    def last_gradients(at_end):
        def go():
            act2_t = act2[own, :].astype(F32).T.astype(BF16)
            grad_units(z.nd + TAPS * z.nh, act2_t, lambda c, w: cote[own, c : c + w], z.nd)
            for k in [3, *some_rest]:
                swaps[k].start()

        only(at_end, go)

    def conv_gradients(at_end):
        def go():
            dhid2_t = dhid2[PAD + RIM : PAD + RIM + N, :].T.astype(BF16)
            grad_units(z.nd, dhid2_t, lambda c, w: taps[own, c : c + w], TAPS * z.nh)
            for k in (2, 1):
                swaps[k].start()

        only(at_end, go)

    def add_rest(at_end):
        for k in some_rest:
            only(at_end, functools.partial(add_swapped, k))

    last_gradients(True)
    inner_norm(1, keep_act2, 0, 1, RIM)
    inner_norm(1, keep_act2, RIM + N, 1, RIM)

    edge_r.wait_recv()
    edge_l.wait_recv()
    r.hid[...] = lax.dot_general(cote[...], last_weight(), NT, preferred_element_type=F32)
    r.acc1[...] = jnp.zeros_like(r.acc1)
    r.acc2[...] = jnp.zeros_like(r.acc2)
    r.acc0[...] = jnp.zeros_like(r.acc0)

    def inner_norm_back(which, first, count, size, grad_store, acc_ref=None):
        gain = r.gains[which : which + 1, :]
        xhat_ref, slope_ref, scale_ref = (
            (r.xhat1, r.slope1, r.scale1),
            (r.xhat2, r.slope2, r.scale2),
        )[which]

        def body(i, carry):
            row = pl.multiple_of(first + i * size, 16)
            xhat = cells(xhat_ref, row, size)
            dpre = cells(r.hid, row, size) * cells(slope_ref, row, size)
            if acc_ref is not None:
                dgain = dpre * xhat
                acc_ref[...] += sum(dgain[n : n + 8] for n in range(0, size, 8))
            dx = dpre * gain
            plain = jnp.sum(dx, axis=1, keepdims=True) / H
            cross = jnp.sum(dx * xhat, axis=1, keepdims=True) / H
            grad_store(row, cells(scale_ref, row, size) * (dx - plain - xhat * cross))
            return carry

        lax.fori_loop(0, count, body, 0)

    dhid2 = r.dhid2
    dhid2[0:PAD, :] = jnp.zeros((PAD, HP), F32)
    dhid2[PAD + E :, :] = jnp.zeros((PAD, HP), F32)

    def keep_dhid2(row, grad):
        dhid2[pl.ds(pl.multiple_of(row + PAD, 8), grad.shape[0]), :] = grad.astype(BF16).astype(F32)

    inner_norm_back(1, 0, 1, RIM, keep_dhid2)
    inner_norm_back(1, RIM, N // BLOCK, BLOCK, keep_dhid2, r.acc2)
    inner_norm_back(1, RIM + N, 1, RIM, keep_dhid2)

    to_plane(3, True)
    add_rest(True)
    for k in some_rest:
        z_start(k)
    conv_gradients(True)

    back = r.back
    for j, offset in enumerate(OFFSETS):
        first = PAD + RIM + offset
        back[:, j * HP : (j + 1) * HP] = (
            dhid2[first : first + N, :] * r.mask[RIM : RIM + N, j : j + 1]
        ).astype(BF16)
    total = None
    for j in range(TAPS):
        term = jnp.dot(
            back[:, j * HP : (j + 1) * HP], tap_weight(TAPS - 1 - j), preferred_element_type=F32
        )
        total = term if total is None else total + term
    r.hid[RIM : RIM + N, :] = total

    to_plane(2, True)
    dhid1 = r.dhid1

    def keep_dhid1(row, grad):
        dhid1[pl.ds(pl.multiple_of(row - RIM, 16), grad.shape[0]), :] = grad.astype(BF16)

    inner_norm_back(0, RIM, N // BLOCK, BLOCK, keep_dhid1, r.acc1)

    big[...] = jnp.dot(dhid1[...], first_weight(), preferred_element_type=F32)

    def first_norm_back(row, size):
        wide = row + RIM
        scale = cells(r.scale0, wide, size)
        xhat = (cells(xe, wide, size).astype(F32) - cells(r.mean0, wide, size)) * scale
        dpre = cells(big, row, size) * cells(r.slope0, wide, size)
        dgain = dpre * xhat
        r.acc0[...] += sum(dgain[n : n + 8] for n in range(0, size, 8))
        dx = dpre * gain0
        plain = jnp.sum(dx, axis=1, keepdims=True) / D
        cross = jnp.sum(dx * xhat, axis=1, keepdims=True) / D
        grad = scale * (dx - plain - xhat * cross)
        r.gi_own[pl.ds(row, size), :] = (cells(cote, wide, size).astype(F32) + grad).astype(BF16)

    gi, gi_own = r.gi, r.gi_own
    marks = [0, N // 4, N // 2, 3 * N // 4, 7 * N // 8, N]
    parts = len(marks) - 1

    def part_span(q):
        return pl.ds(marks[q], marks[q + 1] - marks[q])

    row_bases = {}
    core_rows = gi.at[pl.ds(0, Z)]
    for_rows = shared(core_rows)

    def rows_along(qs, js, at_end):
        def onward(j, place):
            return [remote(place, place, partner, *for_rows)]

        for j in js:
            for q in qs:
                span = part_span(q)
                place = gi.at[2 * origins[j] + core, span]
                take(row_bases[q], j, place, onward, at_end)

    def rows_own(q):
        span = part_span(q)
        return send_own(row_bases[q], gi_own.at[span], gi.at[t, span], q >= 2)

    later = []
    for q in range(parts):
        first_norm_back(marks[q], marks[q + 1] - marks[q])
        span = part_span(q)
        some = gi.at[pl.ds(0, Z + 1 if z.line else Z - 1), span]
        row_bases[q] = stream(gi_own.at[span], some)
        later.append(rows_own(q))
        push(gi_own.at[span], gi.at[t, span], partner, *for_rows)
    own_row = move(gi_own, gi.at[t])
    last_gradients(False)
    conv_gradients(False)

    vec = r.vec
    sum0 = jnp.sum(r.acc0[...], axis=0, keepdims=True)
    sum1 = jnp.sum(r.acc1[...], axis=0, keepdims=True)
    sum2 = jnp.sum(r.acc2[...], axis=0, keepdims=True)
    vec[...] = jnp.zeros_like(vec)
    for j in range(z.nd):
        vec[j : j + 1, :] = sum0[:, j * LANES : (j + 1) * LANES]
    for j in range(z.nh):
        vec[z.nd + j : z.nd + j + 1, :] = sum1[:, j * LANES : (j + 1) * LANES]
        vec[z.nd + z.nh + j : z.nd + z.nh + j + 1, :] = sum2[:, j * LANES : (j + 1) * LANES]
    vec_plane = shared(r.vec_plane.at[pl.ds(1, S - 1)])
    for i in range(1, S):
        push(vec, r.vec_plane.at[i], (seq_at(i), t), *vec_plane)

    dhid1_t = dhid1[...].astype(F32).T.astype(BF16)
    grad_units(0, dhid1_t, lambda c, w: r.act0[own, c : c + w], z.nd)
    swaps[0].start()
    to_plane(3, False)
    add_rest(False)
    to_plane(2, False)
    turn_plane(3)
    to_plane(1)
    turn_plane(2)
    to_plane(0)
    to_z(3)
    z_start(3)
    later[2]()
    rows_along([0, 1], [1], False)
    for k in some_rest:
        z_over(k)
    z_over(3)
    turn_plane(1)
    to_z(2)
    z_start(2)
    later[3]()
    later[4]()
    rows_along([0], [2], False)
    rows_along([2], [1], False)
    rows_along([1], [2], False)

    arrived(vec_plane[0], r.vec_plane.at[pl.ds(1, S - 1)])
    vec_sum = r.vec_sum
    vec_sum[...] = sum((r.vec_plane[i] for i in range(1, S)), vec[...])
    vec_z = shared(r.vec_z.at[pl.ds(0, Z - 1)])
    for i in range(1, Z):
        push(vec_sum, r.vec_z.at[i - 1], dev_z(i), *vec_z)

    turn_plane(0)
    rows_along([3], [1], False)
    z_over(2)
    rows_along([2], [2], False)
    for k in some_rest:
        z_middle(k)
    z_middle(3)
    rows_along([4], [1], False)
    to_z(1)
    z_start(1)
    rows_along([0], [3], False)
    to_z(0)
    z_start(0)
    rows_along([1], [3], False)
    z_over(1)
    z_middle(2)
    z_over(0)
    rows_along([3, 4], [2], False)
    for k in some_rest:
        to_all(k)
    to_all(3)
    rows_along([2], [3], False)
    z_middle(1)
    rows_along([0, 1, 2, 3, 4], [1], True)
    rows_along([0, 1], [2], True)
    z_middle(0)
    to_all(2)
    to_all(1)
    to_all(0)
    rows_along([3, 4], [3], False)
    rows_along([2, 3, 4], [2], True)
    rows_along([0, 1], range(3, Z), True)

    arrived(vec_z[0], r.vec_z.at[pl.ds(0, Z - 1)])
    vec_half = r.vec_half
    vec_half[...] = sum((r.vec_z[i - 1] for i in range(1, Z)), vec_sum[...])
    vec_core = push(vec_half, r.gain_sums.at[1], partner)
    own_sums.append(move(vec_half, r.gain_sums.at[0]))
    rows_along([2, 3, 4], range(3, Z), True)
    arrived(spread_out[0], some_sums)

    vec_core.wait_recv()
    if z.rest:
        rest_end()
    for copy in own_sums:
        copy.wait()
    out_own.wait()
    arrived(for_out[0], some_out)
    own_row.wait()
    arrived(for_rows[0], core_rows)
    assert all(n <= sems.shape[0] for n, sems in zip(counts, (send, recv, local)))
    for copy in sent:
        copy.wait_send()
    for sends, place in together:
        remote(place, place, partner, 0, sends).wait_send()
    for when, sends, place in together_if:
        pl.when(when)(remote(place, place, partner, 0, sends).wait_send)
    for when, copy in sent_if:

        @pl.when(when)
        def _():
            copy.wait_send()


def finish(z, *refs):
    got, gi_got, ff, gain_sums = refs[:4]
    out, gi, grad_first, grad_conv, grad_last, grad_gain, grad_gain1, grad_gain2, *refs = refs[4:]
    first, conv, last, gain, gain1, gain2, sems = refs
    t = lax.axis_index("tp")
    copies = []

    def move(src, dst):
        copy = pltpu.make_async_copy(src, dst, sems.at[len(copies)])
        copy.start()
        copies.append(copy)

    for i in range(z.R):
        move(gi_got.at[i], gi.at[i])
    move(got, out)

    def summed(start, count):
        return jnp.concatenate(
            [ff[u % z.S, u // z.S].astype(F32) for u in range(start, start + count)], axis=1
        )

    first[...] = summed(0, z.nd)
    move(first, grad_first)
    for k in range(TAPS):
        conv[k] = summed(z.nd + k * z.nh, z.nh)
    move(conv, grad_conv)
    last[...] = summed(z.nd + TAPS * z.nh, z.nd)
    move(last, grad_last)
    sums = gain_sums[0] + gain_sums[1]

    def line(start, count):
        return jnp.concatenate([sums[j : j + 1, :] for j in range(start, start + count)], axis=1)

    def picked(row, width, step):
        return sum(
            jnp.where(t == j, row[:, j * step : j * step + width], 0.0) for j in range(z.T)
        )

    gain[...] = picked(line(0, z.nd), z.Dt, z.Dt)
    move(gain, grad_gain)
    gain1[...] = picked(line(z.nd, z.nh), z.Hs, z.Hp)
    move(gain1, grad_gain1)
    gain2[...] = picked(line(z.nd + z.nh, z.nh), z.Hs, z.Hp)
    move(gain2, grad_gain2)
    for copy in copies:
        copy.wait()


def shards(
    mesh,
    inputs,
    starts,
    first_proj,
    dilated_conv,
    last_proj,
    first_norm_gain,
    second_norm_gain,
    third_norm_gain,
    cotangent,
):
    z = Sizes(mesh, inputs, starts, first_proj, cotangent)
    S, T, Z, N, D, E, HP, Hp, NR = z.S, z.T, z.Z, z.N, z.D, z.E, z.HP, z.Hp, z.NR
    more = Hp - z.Hs
    first, last = first_proj.T, last_proj
    conv = dilated_conv.transpose(0, 2, 1)
    if more:
        first, last = (jnp.pad(part, ((0, more), (0, 0))) for part in (first, last))
        conv = jnp.pad(
            conv.reshape(TAPS, z.Hs, T, z.Hs), ((0, 0), (0, more), (0, 0), (0, more))
        ).reshape(TAPS, Hp, HP)
    vm, anywhere = pltpu.VMEM, pl.ANY
    ins = dict(
        x=(inputs, anywhere),
        starts=(starts, vm),
        w1=(first, anywhere),
        wc=(conv, anywhere),
        w3=(last, anywhere),
        g1=(first_norm_gain.reshape(z.nd, LANES), vm),
        g2=(second_norm_gain.reshape(1, z.Hs), vm),
        g3=(third_norm_gain.reshape(1, z.Hs), vm),
        cot=(cotangent.transpose(0, 2, 1), anywhere),
    )
    outs = dict(
        out=((z.R, z.Dt, N), BF16),
        gi=((z.R, N, D), BF16),
        ff=((S, NR, Hp, LANES), BF16),
        gain_sums=((2, 24, LANES), F32),
    )
    NB = z.NF + z.rest
    near = vm if z.line else jax.ShapeDtypeStruct
    scratch = dict(
        send=pltpu.SemaphoreType.DMA((72 if z.line else 800,)),
        recv=pltpu.SemaphoreType.DMA((118 if z.line else 800,)),
        local=pltpu.SemaphoreType.DMA((14,)),
        xe=vm((E, D), BF16),
        cote=vm((E, D), BF16),
        act0=vm((E, D), BF16),
        slope0=vm((E, D), F32),
        mean0=vm((E, 1), F32),
        scale0=vm((E, 1), F32),
        mask=vm((E, LANES), F32),
        flags_left=vm((z.R, N), jnp.int32),
        flags_right=vm((z.R, N), jnp.int32),
        gslots=vm((T, 8, LANES), F32),
        gains=vm((8, HP), F32),
        wg=vm((S, NR, Z, 2, Hp, LANES), BF16),
        hid=vm((E, HP), F32),
        xhat1=vm((E, HP), F32),
        slope1=vm((E, HP), F32),
        scale1=vm((E, 1), F32),
        xhat2=vm((E, HP), F32),
        slope2=vm((E, HP), F32),
        scale2=vm((E, 1), F32),
        act1=vm((E + 2 * PAD, HP), F32),
        dhid2=vm((E + 2 * PAD, HP), F32),
        taps=vm((E, TAPS * HP), BF16),
        back=vm((N, TAPS * HP), BF16),
        act2=vm((E, HP), BF16),
        dhid1=vm((N, HP), BF16),
        big=vm((N, D), F32),
        gi_own=vm((N, D), BF16),
        acc0=vm((8, D), F32),
        acc1=vm((8, HP), F32),
        acc2=vm((8, HP), F32),
        cot_t=vm((D, N), BF16),
        out_t=vm((D, N), BF16),
        w1_in=vm((Hp, D), BF16),
        wc_in=vm((TAPS, Hp, HP), BF16),
        w3_in=vm((Hp, D), BF16),
        gl=vm((8, LANES), F32),
        g=vm((S, NR, Z, 2, Hp, LANES), BF16),
        rc=vm((S, NR, Z, Hp, LANES), BF16),
        ff_own=vm((NB, Hp, LANES), BF16),
        vec=vm((24, LANES), F32),
        vec_sum=vm((24, LANES), F32),
        vec_plane=vm((S, 24, LANES), F32),
        vec_z=vm((Z, 24, LANES), F32),
        vec_half=vm((24, LANES), F32),
    )
    if z.line:
        scratch.update(rz_end=vm((NB, 3, Hp, LANES), BF16))
        scratch.update(rz_pair=vm((NB, 2, Hp, LANES), BF16), rz_one=vm((NB, Hp, LANES), BF16))
    if z.rest:
        scratch.update(others=vm((S, z.rest, Hp, LANES), BF16))
        scratch.update(rest_sum=vm((z.rest, Hp, LANES), BF16))
    else:
        scratch.update(rz=vm((Z, NB, Hp, LANES), BF16))
    if z.square:
        scratch.update(rx=vm((2, NR, Z // 2, Hp, LANES), BF16))
        scratch.update(ry=vm((2, NR, Z // 2, Hp, LANES), BF16))
        scratch.update(rx2=vm((NR, Z // 2, Hp, LANES), BF16))
        scratch.update(ry2=vm((NR, Z // 2, Hp, LANES), BF16))
    else:
        scratch.update(rd=vm((S, NR, Z, Hp, LANES), BF16))
    names = [*ins, *outs, *scratch]
    results = pl.pallas_call(
        functools.partial(kernel, z, names),
        out_shape=[near(shape, kind) for shape, kind in outs.values()],
        in_specs=[pl.BlockSpec(memory_space=space) for _, space in ins.values()],
        out_specs=[pl.BlockSpec(memory_space=anywhere)] * len(outs),
        scratch_shapes=list(scratch.values()),
        compiler_params=pltpu.CompilerParams(
            collective_id=0, has_side_effects=True, vmem_limit_bytes=(50 if z.line else 63) * 2**20
        ),
    )(*[array for array, _ in ins.values()])
    if z.line:
        results = [pltpu.with_memory_space_constraint(part, vm) for part in results]
    shape = jax.ShapeDtypeStruct
    out, gi, grad_first, grad_conv, grad_last, grad_gain, grad_gain1, grad_gain2 = pl.pallas_call(
        functools.partial(finish, z),
        out_shape=[
            shape((z.R, z.Dt, N), BF16),
            shape((z.R, N, D), BF16),
            shape((Hp, D), F32),
            shape((TAPS, Hp, HP), F32),
            shape((Hp, D), F32),
            shape((1, z.Dt), F32),
            shape((1, z.Hs), F32),
            shape((1, z.Hs), F32),
        ],
        in_specs=[pl.BlockSpec(memory_space=space) for space in (anywhere, anywhere, vm, vm)],
        out_specs=[pl.BlockSpec(memory_space=space) for space in [anywhere] * 8],
        scratch_shapes=[
            vm((Hp, D), F32),
            vm((TAPS, Hp, HP), F32),
            vm((Hp, D), F32),
            vm((1, z.Dt), F32),
            vm((1, z.Hs), F32),
            vm((1, z.Hs), F32),
            pltpu.SemaphoreType.DMA((z.R + 7,)),
        ],
        compiler_params=pltpu.CompilerParams(vmem_limit_bytes=12 * 2**20),
    )(*results)
    if more:
        grad_first, grad_last = grad_first[: z.Hs], grad_last[: z.Hs]
        grad_conv = grad_conv.reshape(TAPS, Hp, T, Hp)[:, : z.Hs, :, : z.Hs]
        grad_conv = grad_conv.reshape(TAPS, z.Hs, z.H)
    return (
        out.transpose(0, 2, 1),
        gi,
        grad_first.T,
        grad_conv.transpose(0, 2, 1),
        grad_last,
        grad_gain.reshape(-1),
        grad_gain1.reshape(-1),
        grad_gain2.reshape(-1),
    )


def solution(mesh):
    placed = (
        P(None, "seq", None),
        P(None, "seq"),
        P(None, "tp"),
        P(None, None, "tp"),
        P("tp", None),
        P(),
        P("tp"),
        P("tp"),
        P(None, "seq", "tp"),
    )
    return jax.shard_map(
        functools.partial(shards, mesh),
        mesh=mesh,
        in_specs=placed,
        out_specs=(
            P(None, "seq", "tp"),
            P(None, "seq", None),
            P(None, "tp"),
            P(None, None, "tp"),
            P("tp", None),
            P("tp"),
            P("tp"),
            P("tp"),
        ),
        check_vma=False,
    )
```

```python
import functools
from types import SimpleNamespace

import jax
import jax.numpy as jnp
from jax import lax
from jax.experimental import pallas as pl
from jax.experimental.pallas import tpu as pltpu
from jax.sharding import PartitionSpec as P

MESH = pl.DeviceIdType.MESH
F32 = jnp.float32
BF16 = jnp.bfloat16

TAPS = 5
STEP = 2
REACH = 4
EPS = 1e-05
LANES = 128
RIM = 16
PAD = 8
STAGES = 4
REST, FULL = STAGES, STAGES + 1
BLOCK = 64
HALF_ROOT = 0.7071067811865476
PEAK = 0.3989422804014327

NT = (((1,), (1,)), ((), ()))
OFFSETS = [STEP * k - REACH for k in range(TAPS)]


class Sizes:
    def __init__(self, mesh, inputs, starts, first_proj, cotangent):
        self.S = mesh.shape["seq"]
        self.T = mesh.shape["tp"]
        self.Z = self.T // 2
        self.R, self.N, self.D = inputs.shape
        assert self.R == self.T and self.N % LANES == 0
        self.Hs = first_proj.shape[1]
        self.H = self.Hs * self.T
        self.Hp = -(-self.Hs // 16) * 16
        self.HP = self.Hp * self.T
        assert self.HP % LANES == 0 and self.D % LANES == 0
        self.E = self.N + 2 * RIM
        self.nd = self.D // LANES
        self.nh = self.HP // LANES
        self.units = 2 * self.nd + TAPS * self.nh
        one, two = -(-self.nd // self.S), -(-(self.nd + TAPS * self.nh) // self.S)
        whole = self.units // self.S
        self.rest = self.units % self.S if whole > two else 0
        self.NF = whole if self.rest else -(-self.units // self.S)
        self.NR = self.NF + (self.rest > 0)
        self.chunks = [(0, one), (one, (one + two) // 2), ((one + two) // 2, two), (two, self.NF)]
        self.Dt = cotangent.shape[2]
        assert self.Dt % 16 == 0
        self.full = self.NF - 1 if self.rest and self.NF - 1 > two else None
        self.ahead = list(self.chunks)
        if self.full is not None:
            self.ahead[3] = (two, self.full)
        self.square = self.S == 4
        self.line = self.Z == 4


def cells(ref, row, count):
    return ref[pl.ds(row, count), :]


def gelu_parts(v):
    whole = 0.5 * (1.0 + lax.erf(v * HALF_ROOT))
    slope = whole + v * (PEAK * jnp.exp(-0.5 * v * v))
    return v * whole, slope


def kernel(z, names, *refs):
    r = SimpleNamespace(**dict(zip(names, refs, strict=True)))
    S, T, Z, N, D, E, H, Hp, HP, NR = z.S, z.T, z.Z, z.N, z.D, z.E, z.H, z.Hp, z.HP, z.NR
    s, t = lax.axis_index("seq"), lax.axis_index("tp")
    core, layer = lax.rem(t, 2), t // 2
    partner = (s, t + 1 - 2 * core)

    send, recv, local = r.send, r.recv, r.local
    counts = [0, 0, 0]
    sent, sent_if, together, together_if = [], [], [], []

    def remote(src, dst, device, arrival=None, sends=None):
        return pltpu.make_async_remote_copy(
            src_ref=src,
            dst_ref=dst,
            send_sem=send.at[sendings() if sends is None else sends],
            recv_sem=recv.at[arrivals(1) if arrival is None else arrival],
            device_id=device,
            device_id_type=MESH,
        )

    def sendings():
        counts[0] += 1
        return counts[0] - 1

    def arrivals(count):
        counts[1] += count
        return counts[1] - count

    def shared(place):
        pair = (arrivals(1), sendings())
        together.append((pair[1], place))
        return pair

    def arrived(arrival, place):
        remote(place, place, partner, arrival, 0).wait_recv()

    def push(src, dst, device, arrival=None, sends=None):
        copy = remote(src, dst, device, arrival, sends)
        copy.start()
        if sends is None:
            sent.append(copy)
        return copy

    def push_if(when, copy):
        @pl.when(when)
        def _():
            copy.start()

        sent_if.append((when, copy))

    def move(src, dst):
        counts[2] += 1
        copy = pltpu.make_async_copy(src, dst, local.at[counts[2] - 1])
        copy.start()
        return copy

    def z_at(i):
        return lax.rem(layer + i + Z, Z)

    def dev_z(i):
        return (s, 2 * z_at(i) + core)

    def seq_at(i):
        return lax.rem(s + i + S, S)

    steps = range(1, Z)
    if z.line:
        upper = layer // 2
        inner = lax.rem((layer + 1) // 2, 2)
        end, middle = 3 * upper, 1 + upper
        first = inner * (3 - layer) + (1 - inner) * middle
        second = inner * end + (1 - inner) * (3 - middle)
        origins = [None, first, second, 3 - end]
        own_to = [(first, 2 - inner), (end, 1)]
        passed = {1: (end, 2), 2: (3 - layer, 3), 3: (end, 3)}
    else:
        origins = [None] + [z_at(-i) for i in steps]
        own_to = [(z_at(i), i) for i in steps]
        passed, inner = {}, 0

    def at_layer(to):
        return (s, 2 * to + core)

    def only(at_end, go):
        if z.line:
            pl.when(inner == 1 - at_end)(go)
        elif at_end:
            go()

    def send_own(base, src, place, later=False):
        copies = [remote(src, place, at_layer(to), base + j - 1, streams[base]) for to, j in own_to]
        if z.line:
            pl.when(inner == 1)(copies.pop().start)
        later = later and z.line
        for copy in copies:
            if later:
                pl.when(inner == 1)(copy.start)
            else:
                copy.start()
        return (lambda: pl.when(inner == 0)(copies[0].start)) if later else (lambda: None)

    def take(base, j, place, onward, at_end, start=True):
        if base + j not in onwards:
            extra = None
            if j in passed:
                to, then = passed[j]
                extra = remote(place, place, at_layer(to), base + then - 1, streams[base])
            onwards[base + j] = (extra, onward(j, place))

        def go():
            extra, copies = onwards[base + j]
            arrived(base + j - 1, place)
            if extra is not None and not at_end:
                extra.start()
            if start:
                for copy in copies:
                    copy.start()

        only(at_end, go)

    onwards, streams = {}, {}

    def stream(one, most):
        base = arrivals(Z - 1)
        streams[base] = sendings()
        if z.line:
            together_if.append((inner == 0, streams[base], one))
            together_if.append((inner == 1, streams[base], most))
        else:
            together.append((streams[base], most))
        return base

    right, left = (seq_at(1), t), (seq_at(-1), t)
    if z.square:
        sx, sy, sd = s ^ 1, s ^ 2, s ^ 3
        x_side, y_side = (sx, t), (sy, t)

    xe, cot, cot_t = r.xe, r.cot, r.cot_t

    def features(who):
        return pl.ds(pl.multiple_of(who * z.Dt, 16), z.Dt)

    weights_in = [move(r.w1, r.w1_in), move(r.wc, r.wc_in), move(r.w3, r.w3_in)]
    row_in = move(r.x.at[t], xe.at[pl.ds(RIM, N)])
    cot_own = move(cot.at[t], cot_t.at[features(t)])

    barrier = pltpu.get_barrier_semaphore()
    for i in range(1, T):
        pl.semaphore_signal(barrier, inc=1, device_id=(s, lax.rem(t + i, T)), device_id_type=MESH)
    for i in range(1, S):
        pl.semaphore_signal(barrier, inc=1, device_id=(seq_at(i), t), device_id_type=MESH)
    pl.semaphore_wait(barrier, T + S - 2)

    rim_r = push(r.x.at[t, pl.ds(N - RIM, RIM)], xe.at[pl.ds(0, RIM)], right)
    rim_l = push(r.x.at[t, pl.ds(0, RIM)], xe.at[pl.ds(RIM + N, RIM)], left)
    flags_r = push(r.starts, r.flags_left, right)
    flags_l = push(r.starts, r.flags_right, left)
    r.gl[0:1, : z.Hs] = r.g2[...]
    r.gl[1:2, : z.Hs] = r.g3[...]
    some_gains = r.gslots.at[pl.ds(0, T - 1)]
    for_gains = shared(some_gains)
    for i in range(1, T):
        push(r.gl, r.gslots.at[t], (s, lax.rem(t + i, T)), *for_gains)
    gain_own = move(r.gl, r.gslots.at[t])

    wg = r.wg
    bases, plane, corner = {}, {}, {}
    plane_x, plane_y, plane_d, plane_any, across = {}, {}, {}, {}, {}

    def unit_in(u):
        if u < z.nd:
            return r.w1_in[:, u * LANES : (u + 1) * LANES]
        u -= z.nd
        if u < TAPS * z.nh:
            return r.wc_in[u // z.nh, :, u % z.nh * LANES : (u % z.nh + 1) * LANES]
        u -= TAPS * z.nh
        if u < z.nd:
            return r.w3_in[:, u * LANES : (u + 1) * LANES]
        return jnp.zeros((Hp, LANES), BF16)

    cuts = list(z.ahead)

    def rounds(k):
        a, b = cuts[k]
        return pl.ds(a, b - a)

    def carried(ref, k, which, c):
        if k == REST:
            return ref.at[pl.ds(0, z.rest), z.NF, which, c]
        if k == FULL:
            return ref.at[:, z.full, which, c]
        return ref.at[s, rounds(k), which, c]

    def every(ref, k, which, c):
        return carried(ref, k, which, c) if k >= REST else ref.at[:, rounds(k), which, c]

    every_chip = pl.ds(0, Z)

    def weights_own(k):
        if k == REST:
            for q in range(z.rest):
                wg[q, z.NF, layer, core] = unit_in(z.NF * S + q)
        elif k == FULL:
            for q in range(S):
                wg[q, z.full, layer, core] = unit_in(z.full * S + q)
        else:
            for q in range(S):
                for n in range(*cuts[k]):
                    wg[q, n, layer, core] = unit_in(n * S + q)
        place = carried(wg, k, layer, core)
        count = place.shape[0]
        if z.line:
            most = wg.at[pl.ds(0, count), pl.ds(0, Z + 1), 0, 0]
        else:
            most = wg.at[0, pl.ds(0, count), pl.ds(0, Z - 1), 0]
        bases[k] = stream(place, most)
        send_own(bases[k], place, place)
        across[k] = shared(every(wg, k, every_chip, core))
        place = every(wg, k, layer, core)
        push(place, place, partner, *across[k])
        if k < REST:
            copies = S if z.square else S - 1
            plane[k] = sendings()
            together.append(
                (plane[k], wg.at[pl.ds(0, copies - z.square), rounds(k), pl.ds(0, Z - 1), core])
            )

    def weights_along(k, at_end, js=steps, start=True):
        def onward(j, place):
            if k >= REST:
                return [remote(place, place, partner, *across[k])]
            if not z.square:
                plane_any[k, j] = [
                    remote(place, place, (seq_at(i), t), None, plane[k]) for i in range(1, S)
                ]
                return plane_any[k, j]
            plane_x[k, j] = remote(place, place, x_side, None, plane[k])
            plane_y[k, j] = remote(place, place, y_side, None, plane[k])
            return [plane_x[k, j], plane_y[k, j]]

        for j in js:
            take(bases[k], j, carried(wg, k, origins[j], core), onward, at_end, start)

    def weights_spread(k, js=steps):
        def go():
            for j in js:
                for copy in onwards[bases[k] + j][1]:
                    copy.start()

        only(False, go)

    def weights_corner(k, at_end):
        if not z.square:
            return
        if k not in corner:
            corner[k] = arrivals(1)
        for j in steps:
            if (k, j) not in plane_d:
                over_y = (k + j) % 2
                place = wg.at[sx if over_y else sy, rounds(k), origins[j], core]
                side = y_side if over_y else x_side
                plane_d[k, j] = remote(place, place, side, corner[k], plane[k])

        def go():
            for j in steps:
                plane_x[k, j].wait_recv()
                plane_y[k, j].wait_recv()
                plane_d[k, j].start()
                for q in (s, sx, sy):
                    place = wg.at[q, rounds(k), origins[j], core]
                    push(place, place, partner, *across[k])

        only(at_end, go)

    def weights_across(k, at_end=None):
        def go():
            if z.square:
                arrived(corner[k], wg.at[0, rounds(k), pl.ds(0, Z - 1), core])
            for j in steps:
                place = wg.at[sd if z.square else pl.ds(0, S), rounds(k), origins[j], core]
                if not z.square:
                    for copy in plane_any[k, j]:
                        copy.wait_recv()
                push(place, place, partner, *across[k])

        go() if at_end is None else only(at_end, go)

    def weights_ready(k):
        arrived(across[k][0], every(wg, k, every_chip, 1 - core))

    some_cot = cot_t.at[pl.ds(0, (T - 1) * z.Dt)]
    for_cot = shared(some_cot)

    def cotangent_out(at_end, to_end):
        def go():
            for i in range(1, T):
                to = lax.rem(t + i, T)

                def one():
                    push(cot.at[to], cot_t.at[features(t)], (s, to), *for_cot)

                if z.line:
                    pl.when(lax.rem((to // 2 + 1) // 2, 2) == 1 - to_end)(one)
                elif to_end:
                    one()

        only(at_end, go)

    weights_in[0].wait()
    weights_in[1].wait()
    weights_own(0)
    weights_own(1)
    weights_in[2].wait()
    weights_own(2)
    weights_own(3)
    some_rest = [REST] if z.rest else []
    by_all = some_rest if z.full is None else [FULL, REST]
    def unit(ref, u):
        return ref[u % S, u // S].reshape(HP, LANES)

    def weights(first, count):
        return jnp.concatenate([unit(wg, u) for u in range(first, first + count)], axis=1)

    def first_weight():
        return weights(0, z.nd)

    def tap_weight(k):
        return weights(z.nd + k * z.nh, z.nh)

    def last_weight():
        return weights(z.nd + TAPS * z.nh, z.nd)

    row_in.wait()

    gain0 = jnp.concatenate([r.g1[j : j + 1, :] for j in range(z.nd)], axis=1)

    def first_norm(first, count, size):
        def body(i, carry):
            row = pl.multiple_of(first + i * size, 16)
            v = cells(xe, row, size).astype(F32)
            mean = jnp.sum(v, axis=1, keepdims=True) / D
            spread = jnp.sum(v * v, axis=1, keepdims=True) / D - mean * mean
            scale = lax.rsqrt(spread + EPS)
            act, slope = gelu_parts((v - mean) * scale * gain0)
            r.act0[pl.ds(row, size), :] = act.astype(BF16)
            r.slope0[pl.ds(row, size), :] = slope
            r.mean0[pl.ds(row, size), :] = mean
            r.scale0[pl.ds(row, size), :] = scale
            return carry

        lax.fori_loop(0, count, body, 0)

    first_norm(RIM, N // BLOCK, BLOCK)

    for k in range(STAGES):
        weights_along(k, False, steps[:2], k < 2)
        weights_along(k, True, steps[:1])
    for k in by_all:
        weights_own(k)
    rim_r.wait_recv()
    rim_l.wait_recv()
    first_norm(0, 1, RIM)
    first_norm(RIM + N, 1, RIM)

    gain_own.wait()
    arrived(for_gains[0], some_gains)
    for j in range(T):
        r.gains[0:2, j * Hp : (j + 1) * Hp] = r.gslots[j, 0:2, :Hp]

    flags_r.wait_recv()
    flags_l.wait_recv()
    here = r.starts[pl.ds(t, 1), :]
    before = r.flags_left[pl.ds(t, 1), :]
    after = r.flags_right[pl.ds(t, 1), :]
    window = jnp.concatenate([before[:, N - LANES :], here, after[:, :LANES]], axis=1).astype(F32)
    window = jnp.broadcast_to(window, (E, N + 2 * LANES))
    at = lax.broadcasted_iota(jnp.int32, window.shape, 1) - LANES
    place = lax.broadcasted_iota(jnp.int32, window.shape, 0) - RIM
    rows = lax.broadcasted_iota(jnp.int32, (E, 1), 0) - RIM + s * N
    for k, offset in enumerate(OFFSETS):
        low, high = min(offset, 0), max(offset, 0)
        begun = jnp.sum(
            jnp.where((at > place + low) & (at <= place + high), window, 0.0), axis=1, keepdims=True
        )
        moved = rows + offset
        inside = (begun == 0.0) & (moved >= 0) & (moved < S * N)
        r.mask[:, k : k + 1] = inside.astype(F32)

    third = steps[2:]
    weights_along(0, False, third)
    weights_along(0, True, [2])
    weights_along(1, False, third)
    cotangent_out(False, False)
    weights_along(1, True, [2])
    weights_along(2, False, third, False)
    weights_along(2, True, [2])
    weights_along(3, False, third, False)
    weights_corner(0, False)
    weights_spread(2)
    weights_along(0, True, third)
    cotangent_out(True, False)
    weights_along(1, True, third)
    weights_along(3, True, [2])
    weights_along(2, True, third)
    weights_corner(0, True)
    weights_corner(1, False)
    weights_along(3, True, third)
    weights_corner(1, True)
    weights_spread(3)
    weights_corner(2, True)
    cotangent_out(True, True)
    for k in by_all:
        weights_along(k, False, steps[:2])
    weights_across(0)
    cotangent_out(False, True)

    weights_ready(0)
    r.hid[...] = lax.dot_general(r.act0[...], first_weight(), NT, preferred_element_type=F32)

    weights_corner(3, True)
    weights_across(1, True)

    def inner_norm(which, act_store, first, count, size):
        gain = r.gains[which : which + 1, :]
        xhat_ref, slope_ref, scale_ref = (
            (r.xhat1, r.slope1, r.scale1),
            (r.xhat2, r.slope2, r.scale2),
        )[which]

        def body(i, carry):
            row = pl.multiple_of(first + i * size, 16)
            v = cells(r.hid, row, size)
            mean = jnp.sum(v, axis=1, keepdims=True) / H
            spread = jnp.sum(v * v, axis=1, keepdims=True) / H - mean * mean
            scale = lax.rsqrt(spread + EPS)
            xhat = (v - mean) * scale
            act, slope = gelu_parts(xhat * gain)
            act_store(row, act)
            xhat_ref[pl.ds(row, size), :] = xhat
            slope_ref[pl.ds(row, size), :] = slope
            scale_ref[pl.ds(row, size), :] = scale
            return carry

        lax.fori_loop(0, count, body, 0)

    act1, taps = r.act1, r.taps
    act1[0:PAD, :] = jnp.zeros((PAD, HP), F32)
    act1[PAD + E :, :] = jnp.zeros((PAD, HP), F32)

    def keep_act1(row, act):
        act1[pl.ds(pl.multiple_of(row + PAD, 8), act.shape[0]), :] = act.astype(BF16).astype(F32)

    inner_norm(0, keep_act1, RIM, N // BLOCK, BLOCK)
    inner_norm(0, keep_act1, 0, 1, RIM)
    inner_norm(0, keep_act1, RIM + N, 1, RIM)
    for k, offset in enumerate(OFFSETS):
        taps[:, k * HP : (k + 1) * HP] = (
            act1[PAD + offset : PAD + offset + E, :] * r.mask[:, k : k + 1]
        ).astype(BF16)
    weights_corner(2, False)
    weights_corner(3, False)
    weights_across(1, False)

    def tap_term(k):
        return lax.dot_general(
            taps[:, k * HP : (k + 1) * HP], tap_weight(k), NT, preferred_element_type=F32
        )

    cote = r.cote
    edge_r = remote(cote.at[pl.ds(N, RIM)], cote.at[pl.ds(0, RIM)], right)
    edge_l = remote(cote.at[pl.ds(RIM, RIM)], cote.at[pl.ds(RIM + N, RIM)], left)
    sent.extend([edge_r, edge_l])

    def cotangent_in(at_end):
        def go():
            cot_own.wait()
            arrived(for_cot[0], some_cot)
            cote[RIM : RIM + N, :] = cot_t[...].T
            edge_r.start()
            edge_l.start()

        only(at_end, go)

    cotangent_in(False)
    weights_across(2, True)
    weights_ready(1)
    total = tap_term(0) + tap_term(1)
    for k in by_all:
        weights_along(k, False, third)
    cotangent_in(True)
    weights_across(2, False)
    weights_ready(2)
    for k in range(2, TAPS):
        total = total + tap_term(k)
        if k == 3:
            weights_across(3)
    r.hid[...] = total
    for k in by_all:
        weights_along(k, True)


    act2 = r.act2

    def keep_act2(row, act):
        act2[pl.ds(row, act.shape[0]), :] = act.astype(BF16)

    inner_norm(1, keep_act2, RIM, N // BLOCK, BLOCK)

    for k in [3, *by_all]:
        weights_ready(k)
    big, out_t = r.big, r.out_t
    some_out = r.out.at[pl.ds(0, T - 1)]
    for_out = shared(some_out)
    half_units = z.nd // 2
    own_half = layer // (Z // 2)
    for n in range(2):
        half = own_half if n == 0 else 1 - own_half
        units = [z.nd + TAPS * z.nh + half * half_units + j for j in range(half_units)]
        span = pl.ds(pl.multiple_of(half * half_units * LANES, LANES), half_units * LANES)
        rows = jnp.dot(
            act2[RIM : RIM + N, :],
            jnp.concatenate([unit(wg, u) for u in units], axis=1),
            preferred_element_type=F32,
        )
        rows = rows + xe[RIM : RIM + N, span].astype(F32)
        out_t[span, :] = rows.astype(BF16).T
        for i in range(T // 2):
            to = half * (T // 2) + lax.rem(t + i, T // 2)

            @pl.when(to != t)
            def _():
                push(out_t.at[features(to)], r.out.at[t], (s, to), *for_out)

    out_own = move(out_t.at[features(t)], r.out.at[t])

    cuts[:] = z.chunks

    g = r.g

    def grad_units(first, lhs, rhs, count):
        for j in range(0, count, 2):
            width = min(2, count - j)
            block = jnp.dot(
                lhs, rhs(j * LANES, width * LANES), preferred_element_type=F32
            ).astype(BF16)
            for i in range(width):
                u = first + j + i
                g[u % S, u // S] = block[:, i * LANES : (i + 1) * LANES].reshape(Z, 2, Hp, LANES)

    rc = r.rc
    swaps, plane1, plane2, along_back, first_copies = {}, {}, {}, {}, {}
    some_sums = r.ff.at[pl.ds(0, S - 1), pl.ds(0, z.NF)]
    spread_out = shared(some_sums)
    beside, over, z_sends, own_sums = {}, {}, {}, []

    plane_sends = {}
    for k in [3, *some_rest, 2, 1, 0]:
        place = every(g, k, every_chip, 1 - core)
        to = rc.at[pl.ds(0, z.rest), z.NF] if k == REST else rc.at[:, rounds(k)]
        if z.square and z.line and k != REST:
            a, b = cuts[k]
            plane_sends[k] = sendings()
            together.append((plane_sends[k], wg.at[pl.ds(0, b - a), pl.ds(0, 7), :, 0]))
        swaps[k] = remote(place, to, partner, None, plane_sends.get(k))
        if k not in plane_sends:
            sent.append(swaps[k])

    def add_swapped(k):
        swaps[k].wait_recv()
        at_ = [(q, z.NF) for q in range(z.rest)]
        if k != REST:
            at_ = [(q, n) for q in range(S) for n in range(*cuts[k])]
        for q, n in at_:
            g[q, n, :, core] = (g[q, n, :, core].astype(F32) + rc[q, n].astype(F32)).astype(BF16)

    near, far = pl.ds(0, Z // 2), pl.ds(Z // 2, Z // 2)

    def to_plane(k, at_end=None):
        span = rounds(k)
        if k not in plane1:
            if z.square:
                if k in plane_sends:
                    over_x, over_y = ((arrivals(1), plane_sends[k]) for _ in range(2))
                else:
                    over_x, over_y = shared(r.rx.at[:, span]), shared(r.ry.at[:, span])
                plane1[k] = [(over_x[0], r.rx.at[:, span]), (over_y[0], r.ry.at[:, span])]
                first_copies[k] = [
                    remote(g.at[sx, span, near, core], r.rx.at[0, span], x_side, *over_x),
                    remote(g.at[sd, span, near, core], r.rx.at[1, span], x_side, *over_x),
                    remote(g.at[sy, span, far, core], r.ry.at[0, span], y_side, *over_y),
                    remote(g.at[sd, span, far, core], r.ry.at[1, span], y_side, *over_y),
                ]
            else:
                others = r.rd.at[pl.ds(1, S - 1), span]
                over = shared(others)
                plane1[k] = [(over[0], others)]
                first_copies[k] = [
                    remote(g.at[seq_at(i), span, :, core], r.rd.at[i, span], (seq_at(i), t), *over)
                    for i in range(1, S)
                ]

        def go():
            add_swapped(k)
            for copy in first_copies[k]:
                copy.start()

        go() if at_end is None else only(at_end, go)

    def add_into(q, n, where, other):
        g[q, n, where, core] = (g[q, n, where, core].astype(F32) + other.astype(F32)).astype(BF16)

    def turn_plane(k):
        a, b = cuts[k]
        span = pl.ds(a, b - a)
        for arrival, place in plane1[k]:
            arrived(arrival, place)
        if not z.square:
            return
        for n in range(a, b):
            add_into(sy, n, near, r.rx[1, n])
            add_into(sx, n, far, r.ry[1, n])
        plane2[k] = [
            push(g.at[sy, span, near, core], r.ry2.at[span], y_side, None, plane_sends.get(k)),
            push(g.at[sx, span, far, core], r.rx2.at[span], x_side, None, plane_sends.get(k)),
        ]
        for n in range(a, b):
            add_into(s, n, near, r.rx[0, n])
            add_into(s, n, far, r.ry[0, n])

    def to_z(k):
        a, b = cuts[k]
        span = pl.ds(a, b - a)
        if z.square:
            for copy in plane2[k]:
                copy.wait_recv()
            for n in range(a, b):
                add_into(s, n, near, r.ry2[n])
                add_into(s, n, far, r.rx2[n])
        else:
            for n in range(a, b):
                sums = g[s, n, :, core].astype(F32)
                for i in range(1, S):
                    sums = sums + r.rd[i, n].astype(F32)
                g[s, n, :, core] = sums.astype(BF16)

    def sums_of(k):
        if k == REST:
            return [(q, z.NF, z.NF + q) for q in range(z.rest)]
        return [(s, n, n) for n in range(*cuts[k])]

    def rows_of(k):
        return pl.ds(z.NF, z.rest) if k == REST else rounds(k)

    def z_start(k):
        if z.line:
            beside[k] = arrivals(2)
            z_sends[k] = sendings()
            blocks = len(sums_of(k))
            together.append((z_sends[k], wg.at[pl.ds(0, blocks), pl.ds(0, 3), 0, 0]))
            for n, (which, to) in enumerate(
                [(pl.ds(2 - 2 * upper, 2), pl.ds(1 - upper, 2)), (middle, 2 * upper)]
            ):
                copy = remote(
                    carried(g, k, which, core),
                    r.rz_end.at[rows_of(k), to],
                    at_layer(middle),
                    beside[k] + n,
                    z_sends[k],
                )
                only(True, copy.start)
        else:
            along_back[k] = [
                push(carried(g, k, z_at(i), core), r.rz.at[i, rows_of(k)], dev_z(i)) for i in steps
            ]

    def z_over(k):
        if z.line:
            over[k] = arrivals(1)
            pair = pl.ds(2 - 2 * upper, 2)
            copy = remote(
                carried(g, k, pair, core), r.rz_pair.at[rows_of(k)], at_layer(3 - layer), over[k], z_sends[k]
            )

            @pl.when(inner == 1)
            def _():
                arrived(beside[k], r.rz_end.at[rows_of(k), pl.ds(1 - upper, 2)])
                for q, n, b in sums_of(k):
                    add_into(q, n, pair, r.rz_end[b, pl.ds(1 - upper, 2)])
                copy.start()

    def z_middle(k):
        if z.line:
            along_back[k] = remote(
                carried(g, k, end, core), r.rz_one.at[rows_of(k)], at_layer(end), None, z_sends[k]
            )

            @pl.when(inner == 1)
            def _():
                arrived(over[k], r.rz_pair.at[rows_of(k)])
                for q, n, b in sums_of(k):
                    add_into(q, n, pl.ds(2 * upper, 2), r.rz_pair[b])
                along_back[k].start()
                arrived(beside[k] + 1, r.rz_end.at[rows_of(k), 2 * upper])
                for q, n, b in sums_of(k):
                    sums = g[q, n, layer, core].astype(F32) + r.rz_end[b, 2 * upper].astype(F32)
                    r.ff_own[b] = sums.astype(BF16)

    own_copies = {}

    def to_all(k, at_end):
        place = r.ff_own.at[rows_of(k)]
        if k != REST and k not in own_copies:
            counts[2] += 1
            own_copies[k] = pltpu.make_async_copy(
                place, r.ff.at[s, rounds(k)], local.at[counts[2] - 1]
            )
            own_sums.append(own_copies[k])

        def go():
            if not z.line:
                for copy in along_back[k]:
                    copy.wait_recv()
                for q, n, b in sums_of(k):
                    sums = g[q, n, layer, core].astype(F32)
                    for i in steps:
                        sums = sums + r.rz[i, b].astype(F32)
                    r.ff_own[b] = sums.astype(BF16)
            elif at_end:
                along_back[k].wait_recv()
                for q, n, b in sums_of(k):
                    sums = g[q, n, layer, core].astype(F32) + r.rz_one[b].astype(F32)
                    r.ff_own[b] = sums.astype(BF16)
            for i in range(1, S):
                if k == REST:
                    push(place, r.others.at[i], (seq_at(i), t), *for_others)
                else:
                    push(place, r.ff.at[s, rounds(k)], (seq_at(i), t), *spread_out)
            if k != REST:
                own_copies[k].start()

        only(at_end, go)

    def rest_end():
        arrived(for_others[0], some_others)
        for q in range(z.rest):
            sums = r.ff_own[z.NF + q].astype(F32)
            for i in range(1, S):
                sums = sums + r.others[i, q].astype(F32)
            r.rest_sum[q] = sums.astype(BF16)
        own_sums.append(move(r.rest_sum, r.ff.at[pl.ds(0, z.rest), z.NF]))

    if z.rest:
        some_others = r.others.at[pl.ds(1, S - 1)]
        for_others = shared(some_others)
    for u in [] if z.rest else range(z.units, S * NR):
        g[u % S, u // S] = jnp.zeros((Z, 2, Hp, LANES), BF16)
    own = slice(RIM, RIM + N)

    def last_gradients(at_end):
        def go():
            act2_t = act2[own, :].astype(F32).T.astype(BF16)
            grad_units(z.nd + TAPS * z.nh, act2_t, lambda c, w: cote[own, c : c + w], z.nd)
            for k in [3, *some_rest]:
                swaps[k].start()

        only(at_end, go)

    def conv_gradients(at_end):
        def go():
            dhid2_t = dhid2[PAD + RIM : PAD + RIM + N, :].T.astype(BF16)
            grad_units(z.nd, dhid2_t, lambda c, w: taps[own, c : c + w], TAPS * z.nh)
            for k in (2, 1):
                swaps[k].start()

        only(at_end, go)

    def add_rest(at_end):
        for k in some_rest:
            only(at_end, functools.partial(add_swapped, k))

    last_gradients(True)
    inner_norm(1, keep_act2, 0, 1, RIM)
    inner_norm(1, keep_act2, RIM + N, 1, RIM)

    edge_r.wait_recv()
    edge_l.wait_recv()
    r.hid[...] = lax.dot_general(cote[...], last_weight(), NT, preferred_element_type=F32)
    r.acc1[...] = jnp.zeros_like(r.acc1)
    r.acc2[...] = jnp.zeros_like(r.acc2)
    r.acc0[...] = jnp.zeros_like(r.acc0)

    def inner_norm_back(which, first, count, size, grad_store, acc_ref=None):
        gain = r.gains[which : which + 1, :]
        xhat_ref, slope_ref, scale_ref = (
            (r.xhat1, r.slope1, r.scale1),
            (r.xhat2, r.slope2, r.scale2),
        )[which]

        def body(i, carry):
            row = pl.multiple_of(first + i * size, 16)
            xhat = cells(xhat_ref, row, size)
            dpre = cells(r.hid, row, size) * cells(slope_ref, row, size)
            if acc_ref is not None:
                dgain = dpre * xhat
                acc_ref[...] += sum(dgain[n : n + 8] for n in range(0, size, 8))
            dx = dpre * gain
            plain = jnp.sum(dx, axis=1, keepdims=True) / H
            cross = jnp.sum(dx * xhat, axis=1, keepdims=True) / H
            grad_store(row, cells(scale_ref, row, size) * (dx - plain - xhat * cross))
            return carry

        lax.fori_loop(0, count, body, 0)

    dhid2 = r.dhid2
    dhid2[0:PAD, :] = jnp.zeros((PAD, HP), F32)
    dhid2[PAD + E :, :] = jnp.zeros((PAD, HP), F32)

    def keep_dhid2(row, grad):
        dhid2[pl.ds(pl.multiple_of(row + PAD, 8), grad.shape[0]), :] = grad.astype(BF16).astype(F32)

    inner_norm_back(1, 0, 1, RIM, keep_dhid2)
    inner_norm_back(1, RIM, N // BLOCK, BLOCK, keep_dhid2, r.acc2)
    inner_norm_back(1, RIM + N, 1, RIM, keep_dhid2)

    to_plane(3, True)
    add_rest(True)
    for k in some_rest:
        z_start(k)
    conv_gradients(True)
    to_plane(2, True)

    back = r.back
    for j, offset in enumerate(OFFSETS):
        first = PAD + RIM + offset
        back[:, j * HP : (j + 1) * HP] = (
            dhid2[first : first + N, :] * r.mask[RIM : RIM + N, j : j + 1]
        ).astype(BF16)
    total = None
    for j in range(TAPS):
        term = jnp.dot(
            back[:, j * HP : (j + 1) * HP], tap_weight(TAPS - 1 - j), preferred_element_type=F32
        )
        total = term if total is None else total + term
    r.hid[RIM : RIM + N, :] = total

    dhid1 = r.dhid1

    def keep_dhid1(row, grad):
        dhid1[pl.ds(pl.multiple_of(row - RIM, 16), grad.shape[0]), :] = grad.astype(BF16)

    inner_norm_back(0, RIM, N // BLOCK, BLOCK, keep_dhid1, r.acc1)

    big[...] = jnp.dot(dhid1[...], first_weight(), preferred_element_type=F32)

    def first_norm_back(row, size):
        wide = row + RIM
        scale = cells(r.scale0, wide, size)
        xhat = (cells(xe, wide, size).astype(F32) - cells(r.mean0, wide, size)) * scale
        dpre = cells(big, row, size) * cells(r.slope0, wide, size)
        dgain = dpre * xhat
        r.acc0[...] += sum(dgain[n : n + 8] for n in range(0, size, 8))
        dx = dpre * gain0
        plain = jnp.sum(dx, axis=1, keepdims=True) / D
        cross = jnp.sum(dx * xhat, axis=1, keepdims=True) / D
        grad = scale * (dx - plain - xhat * cross)
        r.gi_own[pl.ds(row, size), :] = (cells(cote, wide, size).astype(F32) + grad).astype(BF16)

    gi, gi_own = r.gi, r.gi_own
    marks = [0, N // 4, N // 2, 3 * N // 4, 7 * N // 8, N]
    parts = len(marks) - 1

    def part_span(q):
        return pl.ds(marks[q], marks[q + 1] - marks[q])

    row_bases = {}
    core_rows = gi.at[pl.ds(0, Z)]
    for_rows = shared(core_rows)

    def rows_along(qs, js, at_end):
        def onward(j, place):
            return [remote(place, place, partner, *for_rows)]

        for j in js:
            for q in qs:
                span = part_span(q)
                place = gi.at[2 * origins[j] + core, span]
                take(row_bases[q], j, place, onward, at_end)

    def rows_own(q):
        span = part_span(q)
        return send_own(row_bases[q], gi_own.at[span], gi.at[t, span], q >= 2)

    later = []
    for q in range(parts):
        first_norm_back(marks[q], marks[q + 1] - marks[q])
        span = part_span(q)
        some = gi.at[pl.ds(0, Z + 1 if z.line else Z - 1), span]
        row_bases[q] = stream(gi_own.at[span], some)
        later.append(rows_own(q))
        push(gi_own.at[span], gi.at[t, span], partner, *for_rows)
    own_row = move(gi_own, gi.at[t])
    last_gradients(False)
    conv_gradients(False)

    vec = r.vec
    sum0 = jnp.sum(r.acc0[...], axis=0, keepdims=True)
    sum1 = jnp.sum(r.acc1[...], axis=0, keepdims=True)
    sum2 = jnp.sum(r.acc2[...], axis=0, keepdims=True)
    vec[...] = jnp.zeros_like(vec)
    for j in range(z.nd):
        vec[j : j + 1, :] = sum0[:, j * LANES : (j + 1) * LANES]
    for j in range(z.nh):
        vec[z.nd + j : z.nd + j + 1, :] = sum1[:, j * LANES : (j + 1) * LANES]
        vec[z.nd + z.nh + j : z.nd + z.nh + j + 1, :] = sum2[:, j * LANES : (j + 1) * LANES]
    vec_plane = shared(r.vec_plane.at[pl.ds(1, S - 1)])
    for i in range(1, S):
        push(vec, r.vec_plane.at[i], (seq_at(i), t), *vec_plane)

    dhid1_t = dhid1[...].astype(F32).T.astype(BF16)
    grad_units(0, dhid1_t, lambda c, w: r.act0[own, c : c + w], z.nd)
    swaps[0].start()
    to_plane(3, False)
    add_rest(False)
    to_plane(2, False)
    turn_plane(3)
    to_plane(1)
    turn_plane(2)
    to_plane(0)
    to_z(3)
    z_start(3)
    later[2]()
    rows_along([0, 1], [1], False)
    for k in some_rest:
        z_over(k)
    z_over(3)
    turn_plane(1)
    to_z(2)
    z_start(2)
    later[3]()
    later[4]()
    rows_along([0], [2], False)
    rows_along([2, 3, 4], [1], False)
    rows_along([1], [2], False)

    arrived(vec_plane[0], r.vec_plane.at[pl.ds(1, S - 1)])
    vec_sum = r.vec_sum
    vec_sum[...] = sum((r.vec_plane[i] for i in range(1, S)), vec[...])
    vec_z = shared(r.vec_z.at[pl.ds(0, Z - 1)])
    for i in range(1, Z):
        push(vec_sum, r.vec_z.at[i - 1], dev_z(i), *vec_z)

    turn_plane(0)
    z_over(2)
    rows_along([2], [2], False)
    for k in [*some_rest, 3]:
        z_middle(k)
        to_all(k, False)
    to_z(1)
    z_start(1)
    rows_along([0], [3], False)
    to_z(0)
    z_start(0)
    rows_along([1], [3], False)
    z_over(1)
    z_middle(2)
    to_all(2, False)
    z_over(0)
    rows_along([3, 4], [2], False)
    for k in some_rest:
        to_all(k, True)
    to_all(3, True)
    rows_along([2], [3], False)
    z_middle(1)
    to_all(1, False)
    rows_along([0, 1, 2, 3, 4], [1], True)
    rows_along([0, 1], [2], True)
    z_middle(0)
    to_all(0, False)
    for k in (2, 1, 0):
        to_all(k, True)
    rows_along([3, 4], [3], False)
    rows_along([2, 3, 4], [2], True)
    rows_along([0, 1], range(3, Z), True)

    arrived(vec_z[0], r.vec_z.at[pl.ds(0, Z - 1)])
    vec_half = r.vec_half
    vec_half[...] = sum((r.vec_z[i - 1] for i in range(1, Z)), vec_sum[...])
    vec_core = push(vec_half, r.gain_sums.at[1], partner)
    own_sums.append(move(vec_half, r.gain_sums.at[0]))
    rows_along([2, 3, 4], range(3, Z), True)
    arrived(spread_out[0], some_sums)

    vec_core.wait_recv()
    if z.rest:
        rest_end()
    for copy in own_sums:
        copy.wait()
    out_own.wait()
    arrived(for_out[0], some_out)
    own_row.wait()
    arrived(for_rows[0], core_rows)
    assert all(n <= sems.shape[0] for n, sems in zip(counts, (send, recv, local)))
    for copy in sent:
        copy.wait_send()
    for sends, place in together:
        remote(place, place, partner, 0, sends).wait_send()
    for when, sends, place in together_if:
        pl.when(when)(remote(place, place, partner, 0, sends).wait_send)
    for when, copy in sent_if:

        @pl.when(when)
        def _():
            copy.wait_send()


def finish(z, *refs):
    got, gi_got, ff, gain_sums = refs[:4]
    out, gi, grad_first, grad_conv, grad_last, grad_gain, grad_gain1, grad_gain2, *refs = refs[4:]
    first, conv, last, gain, gain1, gain2, sems = refs
    t = lax.axis_index("tp")
    copies = []

    def move(src, dst):
        copy = pltpu.make_async_copy(src, dst, sems.at[len(copies)])
        copy.start()
        copies.append(copy)

    for i in range(z.R):
        move(gi_got.at[i], gi.at[i])
    move(got, out)

    def summed(start, count):
        return jnp.concatenate(
            [ff[u % z.S, u // z.S].astype(F32) for u in range(start, start + count)], axis=1
        )

    first[...] = summed(0, z.nd)
    move(first, grad_first)
    for k in range(TAPS):
        conv[k] = summed(z.nd + k * z.nh, z.nh)
    move(conv, grad_conv)
    last[...] = summed(z.nd + TAPS * z.nh, z.nd)
    move(last, grad_last)
    sums = gain_sums[0] + gain_sums[1]

    def line(start, count):
        return jnp.concatenate([sums[j : j + 1, :] for j in range(start, start + count)], axis=1)

    def picked(row, width, step):
        return sum(
            jnp.where(t == j, row[:, j * step : j * step + width], 0.0) for j in range(z.T)
        )

    gain[...] = picked(line(0, z.nd), z.Dt, z.Dt)
    move(gain, grad_gain)
    gain1[...] = picked(line(z.nd, z.nh), z.Hs, z.Hp)
    move(gain1, grad_gain1)
    gain2[...] = picked(line(z.nd + z.nh, z.nh), z.Hs, z.Hp)
    move(gain2, grad_gain2)
    for copy in copies:
        copy.wait()


def shards(
    mesh,
    inputs,
    starts,
    first_proj,
    dilated_conv,
    last_proj,
    first_norm_gain,
    second_norm_gain,
    third_norm_gain,
    cotangent,
):
    z = Sizes(mesh, inputs, starts, first_proj, cotangent)
    S, T, Z, N, D, E, HP, Hp, NR = z.S, z.T, z.Z, z.N, z.D, z.E, z.HP, z.Hp, z.NR
    more = Hp - z.Hs
    first, last = first_proj.T, last_proj
    conv = dilated_conv.transpose(0, 2, 1)
    if more:
        first, last = (jnp.pad(part, ((0, more), (0, 0))) for part in (first, last))
        conv = jnp.pad(
            conv.reshape(TAPS, z.Hs, T, z.Hs), ((0, 0), (0, more), (0, 0), (0, more))
        ).reshape(TAPS, Hp, HP)
    vm, anywhere = pltpu.VMEM, pl.ANY
    ins = dict(
        x=(inputs, anywhere),
        starts=(starts, vm),
        w1=(first, anywhere),
        wc=(conv, anywhere),
        w3=(last, anywhere),
        g1=(first_norm_gain.reshape(z.nd, LANES), vm),
        g2=(second_norm_gain.reshape(1, z.Hs), vm),
        g3=(third_norm_gain.reshape(1, z.Hs), vm),
        cot=(cotangent.transpose(0, 2, 1), anywhere),
    )
    outs = dict(
        out=((z.R, z.Dt, N), BF16),
        gi=((z.R, N, D), BF16),
        ff=((S, NR, Hp, LANES), BF16),
        gain_sums=((2, 24, LANES), F32),
    )
    NB = z.NF + z.rest
    near = vm if z.line else jax.ShapeDtypeStruct
    scratch = dict(
        send=pltpu.SemaphoreType.DMA((46 if z.line else 800,)),
        recv=pltpu.SemaphoreType.DMA((123 if z.line else 800,)),
        local=pltpu.SemaphoreType.DMA((14,)),
        xe=vm((E, D), BF16),
        cote=vm((E, D), BF16),
        act0=vm((E, D), BF16),
        slope0=vm((E, D), F32),
        mean0=vm((E, 1), F32),
        scale0=vm((E, 1), F32),
        mask=vm((E, LANES), F32),
        flags_left=vm((z.R, N), jnp.int32),
        flags_right=vm((z.R, N), jnp.int32),
        gslots=vm((T, 8, LANES), F32),
        gains=vm((8, HP), F32),
        wg=vm((S, NR, Z, 2, Hp, LANES), BF16),
        hid=vm((E, HP), F32),
        xhat1=vm((E, HP), F32),
        slope1=vm((E, HP), F32),
        scale1=vm((E, 1), F32),
        xhat2=vm((E, HP), F32),
        slope2=vm((E, HP), F32),
        scale2=vm((E, 1), F32),
        act1=vm((E + 2 * PAD, HP), F32),
        dhid2=vm((E + 2 * PAD, HP), F32),
        taps=vm((E, TAPS * HP), BF16),
        back=vm((N, TAPS * HP), BF16),
        act2=vm((E, HP), BF16),
        dhid1=vm((N, HP), BF16),
        big=vm((N, D), F32),
        gi_own=vm((N, D), BF16),
        acc0=vm((8, D), F32),
        acc1=vm((8, HP), F32),
        acc2=vm((8, HP), F32),
        cot_t=vm((D, N), BF16),
        out_t=vm((D, N), BF16),
        w1_in=vm((Hp, D), BF16),
        wc_in=vm((TAPS, Hp, HP), BF16),
        w3_in=vm((Hp, D), BF16),
        gl=vm((8, LANES), F32),
        g=vm((S, NR, Z, 2, Hp, LANES), BF16),
        rc=vm((S, NR, Z, Hp, LANES), BF16),
        ff_own=vm((NB, Hp, LANES), BF16),
        vec=vm((24, LANES), F32),
        vec_sum=vm((24, LANES), F32),
        vec_plane=vm((S, 24, LANES), F32),
        vec_z=vm((Z, 24, LANES), F32),
        vec_half=vm((24, LANES), F32),
    )
    if z.line:
        scratch.update(rz_end=vm((NB, 3, Hp, LANES), BF16))
        scratch.update(rz_pair=vm((NB, 2, Hp, LANES), BF16), rz_one=vm((NB, Hp, LANES), BF16))
    if z.rest:
        scratch.update(others=vm((S, z.rest, Hp, LANES), BF16))
        scratch.update(rest_sum=vm((z.rest, Hp, LANES), BF16))
    else:
        scratch.update(rz=vm((Z, NB, Hp, LANES), BF16))
    if z.square:
        scratch.update(rx=vm((2, NR, Z // 2, Hp, LANES), BF16))
        scratch.update(ry=vm((2, NR, Z // 2, Hp, LANES), BF16))
        scratch.update(rx2=vm((NR, Z // 2, Hp, LANES), BF16))
        scratch.update(ry2=vm((NR, Z // 2, Hp, LANES), BF16))
    else:
        scratch.update(rd=vm((S, NR, Z, Hp, LANES), BF16))
    names = [*ins, *outs, *scratch]
    results = pl.pallas_call(
        functools.partial(kernel, z, names),
        out_shape=[near(shape, kind) for shape, kind in outs.values()],
        in_specs=[pl.BlockSpec(memory_space=space) for _, space in ins.values()],
        out_specs=[pl.BlockSpec(memory_space=anywhere)] * len(outs),
        scratch_shapes=list(scratch.values()),
        compiler_params=pltpu.CompilerParams(
            collective_id=0, has_side_effects=True, vmem_limit_bytes=(50 if z.line else 63) * 2**20
        ),
    )(*[array for array, _ in ins.values()])
    if z.line:
        results = [pltpu.with_memory_space_constraint(part, vm) for part in results]
    shape = jax.ShapeDtypeStruct
    out, gi, grad_first, grad_conv, grad_last, grad_gain, grad_gain1, grad_gain2 = pl.pallas_call(
        functools.partial(finish, z),
        out_shape=[
            shape((z.R, z.Dt, N), BF16),
            shape((z.R, N, D), BF16),
            shape((Hp, D), F32),
            shape((TAPS, Hp, HP), F32),
            shape((Hp, D), F32),
            shape((1, z.Dt), F32),
            shape((1, z.Hs), F32),
            shape((1, z.Hs), F32),
        ],
        in_specs=[pl.BlockSpec(memory_space=space) for space in (anywhere, anywhere, vm, vm)],
        out_specs=[pl.BlockSpec(memory_space=space) for space in [anywhere] * 8],
        scratch_shapes=[
            vm((Hp, D), F32),
            vm((TAPS, Hp, HP), F32),
            vm((Hp, D), F32),
            vm((1, z.Dt), F32),
            vm((1, z.Hs), F32),
            vm((1, z.Hs), F32),
            pltpu.SemaphoreType.DMA((z.R + 7,)),
        ],
        compiler_params=pltpu.CompilerParams(vmem_limit_bytes=12 * 2**20),
    )(*results)
    if more:
        grad_first, grad_last = grad_first[: z.Hs], grad_last[: z.Hs]
        grad_conv = grad_conv.reshape(TAPS, Hp, T, Hp)[:, : z.Hs, :, : z.Hs]
        grad_conv = grad_conv.reshape(TAPS, z.Hs, z.H)
    return (
        out.transpose(0, 2, 1),
        gi,
        grad_first.T,
        grad_conv.transpose(0, 2, 1),
        grad_last,
        grad_gain.reshape(-1),
        grad_gain1.reshape(-1),
        grad_gain2.reshape(-1),
    )


def solution(mesh):
    placed = (
        P(None, "seq", None),
        P(None, "seq"),
        P(None, "tp"),
        P(None, None, "tp"),
        P("tp", None),
        P(),
        P("tp"),
        P("tp"),
        P(None, "seq", "tp"),
    )
    return jax.shard_map(
        functools.partial(shards, mesh),
        mesh=mesh,
        in_specs=placed,
        out_specs=(
            P(None, "seq", "tp"),
            P(None, "seq", None),
            P(None, "tp"),
            P(None, None, "tp"),
            P("tp", None),
            P("tp"),
            P("tp"),
            P("tp"),
        ),
        check_vma=False,
    )
```

```python
import functools
from types import SimpleNamespace

import jax
import jax.numpy as jnp
from jax import lax
from jax.experimental import pallas as pl
from jax.experimental.pallas import tpu as pltpu
from jax.sharding import PartitionSpec as P

MESH = pl.DeviceIdType.MESH
F32 = jnp.float32
BF16 = jnp.bfloat16

TAPS = 5
STEP = 2
REACH = 4
EPS = 1e-05
LANES = 128
RIM = 16
PAD = 8
STAGES = 4
REST, FULL = STAGES, STAGES + 1
BLOCK = 64
HALF_ROOT = 0.7071067811865476
PEAK = 0.3989422804014327

NT = (((1,), (1,)), ((), ()))
OFFSETS = [STEP * k - REACH for k in range(TAPS)]


class Sizes:
    def __init__(self, mesh, inputs, starts, first_proj, cotangent):
        self.S = mesh.shape["seq"]
        self.T = mesh.shape["tp"]
        self.Z = self.T // 2
        self.R, self.N, self.D = inputs.shape
        assert self.R == self.T and self.N % LANES == 0
        self.Hs = first_proj.shape[1]
        self.H = self.Hs * self.T
        self.Hp = -(-self.Hs // 16) * 16
        self.HP = self.Hp * self.T
        assert self.HP % LANES == 0 and self.D % LANES == 0
        self.E = self.N + 2 * RIM
        self.nd = self.D // LANES
        self.nh = self.HP // LANES
        self.units = 2 * self.nd + TAPS * self.nh
        one, two = -(-self.nd // self.S), -(-(self.nd + TAPS * self.nh) // self.S)
        whole = self.units // self.S
        self.rest = self.units % self.S if whole > two else 0
        self.NF = whole if self.rest else -(-self.units // self.S)
        self.NR = self.NF + (self.rest > 0)
        self.chunks = [(0, one), (one, (one + two) // 2), ((one + two) // 2, two), (two, self.NF)]
        self.Dt = cotangent.shape[2]
        assert self.Dt % 16 == 0
        self.full = self.NF - 1 if self.rest and self.NF - 1 > two else None
        self.ahead = list(self.chunks)
        if self.full is not None:
            self.ahead[3] = (two, self.full)
        self.square = self.S == 4
        self.line = self.Z == 4


def cells(ref, row, count):
    return ref[pl.ds(row, count), :]


def gelu_parts(v):
    whole = 0.5 * (1.0 + lax.erf(v * HALF_ROOT))
    slope = whole + v * (PEAK * jnp.exp(-0.5 * v * v))
    return v * whole, slope


def kernel(z, names, *refs):
    r = SimpleNamespace(**dict(zip(names, refs, strict=True)))
    S, T, Z, N, D, E, H, Hp, HP, NR = z.S, z.T, z.Z, z.N, z.D, z.E, z.H, z.Hp, z.HP, z.NR
    s, t = lax.axis_index("seq"), lax.axis_index("tp")
    core, layer = lax.rem(t, 2), t // 2
    partner = (s, t + 1 - 2 * core)

    send, recv, local = r.send, r.recv, r.local
    counts = [0, 0, 0]
    sent, sent_if, together, together_if = [], [], [], []

    def remote(src, dst, device, arrival=None, sends=None):
        return pltpu.make_async_remote_copy(
            src_ref=src,
            dst_ref=dst,
            send_sem=send.at[sendings() if sends is None else sends],
            recv_sem=recv.at[arrivals(1) if arrival is None else arrival],
            device_id=device,
            device_id_type=MESH,
        )

    def sendings():
        counts[0] += 1
        return counts[0] - 1

    def arrivals(count):
        counts[1] += count
        return counts[1] - count

    def shared(place):
        pair = (arrivals(1), sendings())
        together.append((pair[1], place))
        return pair

    def arrived(arrival, place):
        remote(place, place, partner, arrival, 0).wait_recv()

    def push(src, dst, device, arrival=None, sends=None):
        copy = remote(src, dst, device, arrival, sends)
        copy.start()
        if sends is None:
            sent.append(copy)
        return copy

    def push_if(when, copy):
        @pl.when(when)
        def _():
            copy.start()

        sent_if.append((when, copy))

    def move(src, dst):
        counts[2] += 1
        copy = pltpu.make_async_copy(src, dst, local.at[counts[2] - 1])
        copy.start()
        return copy

    def z_at(i):
        return lax.rem(layer + i + Z, Z)

    def dev_z(i):
        return (s, 2 * z_at(i) + core)

    def seq_at(i):
        return lax.rem(s + i + S, S)

    steps = range(1, Z)
    if z.line:
        upper = layer // 2
        inner = lax.rem((layer + 1) // 2, 2)
        end, middle = 3 * upper, 1 + upper
        first = inner * (3 - layer) + (1 - inner) * middle
        second = inner * end + (1 - inner) * (3 - middle)
        origins = [None, first, second, 3 - end]
        own_to = [(first, 2 - inner), (end, 1)]
        passed = {1: (end, 2), 2: (3 - layer, 3), 3: (end, 3)}
    else:
        origins = [None] + [z_at(-i) for i in steps]
        own_to = [(z_at(i), i) for i in steps]
        passed, inner = {}, 0

    def at_layer(to):
        return (s, 2 * to + core)

    def only(at_end, go):
        if z.line:
            pl.when(inner == 1 - at_end)(go)
        elif at_end:
            go()

    def send_own(base, src, place, later=False):
        copies = [remote(src, place, at_layer(to), base + j - 1, streams[base]) for to, j in own_to]
        if z.line:
            pl.when(inner == 1)(copies.pop().start)
        later = later and z.line
        for copy in copies:
            if later:
                pl.when(inner == 1)(copy.start)
            else:
                copy.start()
        return (lambda: pl.when(inner == 0)(copies[0].start)) if later else (lambda: None)

    def take(base, j, place, onward, at_end, start=True):
        if base + j not in onwards:
            extra = None
            if j in passed:
                to, then = passed[j]
                extra = remote(place, place, at_layer(to), base + then - 1, streams[base])
            onwards[base + j] = (extra, onward(j, place))

        def go():
            extra, copies = onwards[base + j]
            arrived(base + j - 1, place)
            if extra is not None and not at_end:
                extra.start()
            if start:
                for copy in copies:
                    copy.start()

        only(at_end, go)

    onwards, streams = {}, {}

    def stream(one, most):
        base = arrivals(Z - 1)
        streams[base] = sendings()
        if z.line:
            together_if.append((inner == 0, streams[base], one))
            together_if.append((inner == 1, streams[base], most))
        else:
            together.append((streams[base], most))
        return base

    right, left = (seq_at(1), t), (seq_at(-1), t)
    if z.square:
        sx, sy, sd = s ^ 1, s ^ 2, s ^ 3
        x_side, y_side = (sx, t), (sy, t)

    xe, cot, cot_t = r.xe, r.cot, r.cot_t

    def features(who):
        return pl.ds(pl.multiple_of(who * z.Dt, 16), z.Dt)

    weights_in = [move(r.w1, r.w1_in), move(r.wc, r.wc_in), move(r.w3, r.w3_in)]
    row_in = move(r.x.at[t], xe.at[pl.ds(RIM, N)])
    cot_own = move(cot.at[t], cot_t.at[features(t)])

    barrier = pltpu.get_barrier_semaphore()
    for i in range(1, T):
        pl.semaphore_signal(barrier, inc=1, device_id=(s, lax.rem(t + i, T)), device_id_type=MESH)
    for i in range(1, S):
        pl.semaphore_signal(barrier, inc=1, device_id=(seq_at(i), t), device_id_type=MESH)
    pl.semaphore_wait(barrier, T + S - 2)

    rim_r = push(r.x.at[t, pl.ds(N - RIM, RIM)], xe.at[pl.ds(0, RIM)], right)
    rim_l = push(r.x.at[t, pl.ds(0, RIM)], xe.at[pl.ds(RIM + N, RIM)], left)
    flags_r = push(r.starts, r.flags_left, right)
    flags_l = push(r.starts, r.flags_right, left)
    r.gl[0:1, : z.Hs] = r.g2[...]
    r.gl[1:2, : z.Hs] = r.g3[...]
    some_gains = r.gslots.at[pl.ds(0, T - 1)]
    for_gains = shared(some_gains)
    for i in range(1, T):
        push(r.gl, r.gslots.at[t], (s, lax.rem(t + i, T)), *for_gains)
    gain_own = move(r.gl, r.gslots.at[t])

    wg = r.wg
    bases, plane, corner = {}, {}, {}
    plane_x, plane_y, plane_d, plane_any, across = {}, {}, {}, {}, {}

    def unit_in(u):
        if u < z.nd:
            return r.w1_in[:, u * LANES : (u + 1) * LANES]
        u -= z.nd
        if u < TAPS * z.nh:
            return r.wc_in[u // z.nh, :, u % z.nh * LANES : (u % z.nh + 1) * LANES]
        u -= TAPS * z.nh
        if u < z.nd:
            return r.w3_in[:, u * LANES : (u + 1) * LANES]
        return jnp.zeros((Hp, LANES), BF16)

    cuts = list(z.ahead)

    def rounds(k):
        a, b = cuts[k]
        return pl.ds(a, b - a)

    def carried(ref, k, which, c):
        if k == REST:
            return ref.at[pl.ds(0, z.rest), z.NF, which, c]
        if k == FULL:
            return ref.at[:, z.full, which, c]
        return ref.at[s, rounds(k), which, c]

    def every(ref, k, which, c):
        return carried(ref, k, which, c) if k >= REST else ref.at[:, rounds(k), which, c]

    every_chip = pl.ds(0, Z)

    def weights_own(k):
        if k == REST:
            for q in range(z.rest):
                wg[q, z.NF, layer, core] = unit_in(z.NF * S + q)
        elif k == FULL:
            for q in range(S):
                wg[q, z.full, layer, core] = unit_in(z.full * S + q)
        else:
            for q in range(S):
                for n in range(*cuts[k]):
                    wg[q, n, layer, core] = unit_in(n * S + q)
        place = carried(wg, k, layer, core)
        count = place.shape[0]
        if z.line:
            most = wg.at[pl.ds(0, count), pl.ds(0, Z + 1), 0, 0]
        else:
            most = wg.at[0, pl.ds(0, count), pl.ds(0, Z - 1), 0]
        bases[k] = stream(place, most)
        send_own(bases[k], place, place)
        across[k] = shared(every(wg, k, every_chip, core))
        place = every(wg, k, layer, core)
        push(place, place, partner, *across[k])
        if k < REST:
            copies = S if z.square else S - 1
            plane[k] = sendings()
            together.append(
                (plane[k], wg.at[pl.ds(0, copies - z.square), rounds(k), pl.ds(0, Z - 1), core])
            )

    def weights_along(k, at_end, js=steps, start=True):
        def onward(j, place):
            if k >= REST:
                return [remote(place, place, partner, *across[k])]
            if not z.square:
                plane_any[k, j] = [
                    remote(place, place, (seq_at(i), t), None, plane[k]) for i in range(1, S)
                ]
                return plane_any[k, j]
            plane_x[k, j] = remote(place, place, x_side, None, plane[k])
            plane_y[k, j] = remote(place, place, y_side, None, plane[k])
            return [plane_x[k, j], plane_y[k, j]]

        for j in js:
            take(bases[k], j, carried(wg, k, origins[j], core), onward, at_end, start)

    def weights_spread(k, js=steps):
        def go():
            for j in js:
                for copy in onwards[bases[k] + j][1]:
                    copy.start()

        only(False, go)

    def weights_corner(k, at_end):
        if not z.square:
            return
        if k not in corner:
            corner[k] = arrivals(1)
        for j in steps:
            if (k, j) not in plane_d:
                over_y = (k + j) % 2
                place = wg.at[sx if over_y else sy, rounds(k), origins[j], core]
                side = y_side if over_y else x_side
                plane_d[k, j] = remote(place, place, side, corner[k], plane[k])

        def go():
            for j in steps:
                plane_x[k, j].wait_recv()
                plane_y[k, j].wait_recv()
                plane_d[k, j].start()
                for q in (s, sx, sy):
                    place = wg.at[q, rounds(k), origins[j], core]
                    push(place, place, partner, *across[k])

        only(at_end, go)

    def weights_across(k, at_end=None):
        def go():
            if z.square:
                arrived(corner[k], wg.at[0, rounds(k), pl.ds(0, Z - 1), core])
            for j in steps:
                place = wg.at[sd if z.square else pl.ds(0, S), rounds(k), origins[j], core]
                if not z.square:
                    for copy in plane_any[k, j]:
                        copy.wait_recv()
                push(place, place, partner, *across[k])

        go() if at_end is None else only(at_end, go)

    def weights_ready(k):
        arrived(across[k][0], every(wg, k, every_chip, 1 - core))

    some_cot = cot_t.at[pl.ds(0, (T - 1) * z.Dt)]
    for_cot = shared(some_cot)

    def cotangent_out(at_end, to_end):
        def go():
            for i in range(1, T):
                to = lax.rem(t + i, T)

                def one():
                    push(cot.at[to], cot_t.at[features(t)], (s, to), *for_cot)

                if z.line:
                    pl.when(lax.rem((to // 2 + 1) // 2, 2) == 1 - to_end)(one)
                elif to_end:
                    one()

        only(at_end, go)

    weights_in[0].wait()
    weights_in[1].wait()
    weights_own(0)
    weights_own(1)
    weights_in[2].wait()
    weights_own(2)
    weights_own(3)
    some_rest = [REST] if z.rest else []
    by_all = some_rest if z.full is None else [FULL, REST]
    def unit(ref, u):
        return ref[u % S, u // S].reshape(HP, LANES)

    def weights(first, count):
        return jnp.concatenate([unit(wg, u) for u in range(first, first + count)], axis=1)

    def first_weight():
        return weights(0, z.nd)

    def tap_weight(k):
        return weights(z.nd + k * z.nh, z.nh)

    def last_weight():
        return weights(z.nd + TAPS * z.nh, z.nd)

    row_in.wait()

    gain0 = jnp.concatenate([r.g1[j : j + 1, :] for j in range(z.nd)], axis=1)

    def first_norm(first, count, size):
        def body(i, carry):
            row = pl.multiple_of(first + i * size, 16)
            v = cells(xe, row, size).astype(F32)
            mean = jnp.sum(v, axis=1, keepdims=True) / D
            spread = jnp.sum(v * v, axis=1, keepdims=True) / D - mean * mean
            scale = lax.rsqrt(spread + EPS)
            act, slope = gelu_parts((v - mean) * scale * gain0)
            r.act0[pl.ds(row, size), :] = act.astype(BF16)
            r.slope0[pl.ds(row, size), :] = slope
            r.mean0[pl.ds(row, size), :] = mean
            r.scale0[pl.ds(row, size), :] = scale
            return carry

        lax.fori_loop(0, count, body, 0)

    first_norm(RIM, N // BLOCK, BLOCK)

    for k in range(STAGES):
        weights_along(k, False, steps[:2], k < 2)
        weights_along(k, True, steps[:1])
    for k in by_all:
        weights_own(k)
    rim_r.wait_recv()
    rim_l.wait_recv()
    first_norm(0, 1, RIM)
    first_norm(RIM + N, 1, RIM)

    gain_own.wait()
    arrived(for_gains[0], some_gains)
    for j in range(T):
        r.gains[0:2, j * Hp : (j + 1) * Hp] = r.gslots[j, 0:2, :Hp]

    flags_r.wait_recv()
    flags_l.wait_recv()
    here = r.starts[pl.ds(t, 1), :]
    before = r.flags_left[pl.ds(t, 1), :]
    after = r.flags_right[pl.ds(t, 1), :]
    window = jnp.concatenate([before[:, N - LANES :], here, after[:, :LANES]], axis=1).astype(F32)
    window = jnp.broadcast_to(window, (E, N + 2 * LANES))
    at = lax.broadcasted_iota(jnp.int32, window.shape, 1) - LANES
    place = lax.broadcasted_iota(jnp.int32, window.shape, 0) - RIM
    rows = lax.broadcasted_iota(jnp.int32, (E, 1), 0) - RIM + s * N
    for k, offset in enumerate(OFFSETS):
        low, high = min(offset, 0), max(offset, 0)
        begun = jnp.sum(
            jnp.where((at > place + low) & (at <= place + high), window, 0.0), axis=1, keepdims=True
        )
        moved = rows + offset
        inside = (begun == 0.0) & (moved >= 0) & (moved < S * N)
        r.mask[:, k : k + 1] = inside.astype(F32)

    third = steps[2:]
    weights_along(0, False, third)
    weights_along(0, True, [2])
    weights_along(1, False, third)
    cotangent_out(False, False)
    weights_along(1, True, [2])
    weights_along(2, False, third, False)
    weights_along(2, True, [2])
    weights_along(3, False, third, False)
    weights_corner(0, False)
    weights_spread(2)
    weights_along(0, True, third)
    cotangent_out(True, False)
    weights_along(1, True, third)
    weights_along(3, True, [2])
    weights_along(2, True, third)
    weights_corner(0, True)
    weights_corner(1, False)
    weights_along(3, True, third)
    weights_corner(1, True)
    weights_spread(3)
    weights_corner(2, True)
    cotangent_out(True, True)
    for k in by_all:
        weights_along(k, False, steps[:2])
    weights_across(0)
    cotangent_out(False, True)

    weights_ready(0)
    r.hid[...] = lax.dot_general(r.act0[...], first_weight(), NT, preferred_element_type=F32)

    weights_corner(3, True)
    weights_across(1, True)

    def inner_norm(which, act_store, first, count, size):
        gain = r.gains[which : which + 1, :]
        xhat_ref, slope_ref, scale_ref = (
            (r.xhat1, r.slope1, r.scale1),
            (r.xhat2, r.slope2, r.scale2),
        )[which]

        def body(i, carry):
            row = pl.multiple_of(first + i * size, 16)
            v = cells(r.hid, row, size)
            mean = jnp.sum(v, axis=1, keepdims=True) / H
            spread = jnp.sum(v * v, axis=1, keepdims=True) / H - mean * mean
            scale = lax.rsqrt(spread + EPS)
            xhat = (v - mean) * scale
            act, slope = gelu_parts(xhat * gain)
            act_store(row, act)
            xhat_ref[pl.ds(row, size), :] = xhat
            slope_ref[pl.ds(row, size), :] = slope
            scale_ref[pl.ds(row, size), :] = scale
            return carry

        lax.fori_loop(0, count, body, 0)

    act1, taps = r.act1, r.taps
    act1[0:PAD, :] = jnp.zeros((PAD, HP), F32)
    act1[PAD + E :, :] = jnp.zeros((PAD, HP), F32)

    def keep_act1(row, act):
        act1[pl.ds(pl.multiple_of(row + PAD, 8), act.shape[0]), :] = act.astype(BF16).astype(F32)

    inner_norm(0, keep_act1, RIM, N // BLOCK, BLOCK)
    inner_norm(0, keep_act1, 0, 1, RIM)
    inner_norm(0, keep_act1, RIM + N, 1, RIM)
    for k, offset in enumerate(OFFSETS):
        taps[:, k * HP : (k + 1) * HP] = (
            act1[PAD + offset : PAD + offset + E, :] * r.mask[:, k : k + 1]
        ).astype(BF16)
    weights_corner(2, False)
    weights_corner(3, False)
    weights_across(1, False)

    def tap_term(k):
        return lax.dot_general(
            taps[:, k * HP : (k + 1) * HP], tap_weight(k), NT, preferred_element_type=F32
        )

    cote = r.cote
    edge_r = remote(cote.at[pl.ds(N, RIM)], cote.at[pl.ds(0, RIM)], right)
    edge_l = remote(cote.at[pl.ds(RIM, RIM)], cote.at[pl.ds(RIM + N, RIM)], left)
    sent.extend([edge_r, edge_l])

    def cotangent_in(at_end):
        def go():
            cot_own.wait()
            arrived(for_cot[0], some_cot)
            cote[RIM : RIM + N, :] = cot_t[...].T
            edge_r.start()
            edge_l.start()

        only(at_end, go)

    cotangent_in(False)
    weights_across(2, True)
    weights_ready(1)
    total = tap_term(0) + tap_term(1)
    for k in by_all:
        weights_along(k, False, third)
    cotangent_in(True)
    weights_across(2, False)
    weights_ready(2)
    for k in range(2, TAPS):
        total = total + tap_term(k)
        if k == 3:
            weights_across(3)
    r.hid[...] = total
    for k in by_all:
        weights_along(k, True)


    act2 = r.act2

    def keep_act2(row, act):
        act2[pl.ds(row, act.shape[0]), :] = act.astype(BF16)

    inner_norm(1, keep_act2, RIM, N // BLOCK, BLOCK)

    for k in [3, *by_all]:
        weights_ready(k)
    big, out_t = r.big, r.out_t
    some_out = r.out.at[pl.ds(0, T - 1)]
    for_out = shared(some_out)
    half_units = z.nd // 2
    own_half = layer // (Z // 2)
    for n in range(2):
        half = own_half if n == 0 else 1 - own_half
        units = [z.nd + TAPS * z.nh + half * half_units + j for j in range(half_units)]
        span = pl.ds(pl.multiple_of(half * half_units * LANES, LANES), half_units * LANES)
        rows = jnp.dot(
            act2[RIM : RIM + N, :],
            jnp.concatenate([unit(wg, u) for u in units], axis=1),
            preferred_element_type=F32,
        )
        rows = rows + xe[RIM : RIM + N, span].astype(F32)
        out_t[span, :] = rows.astype(BF16).T
        for i in range(T // 2):
            to = half * (T // 2) + lax.rem(t + i, T // 2)

            @pl.when(to != t)
            def _():
                push(out_t.at[features(to)], r.out.at[t], (s, to), *for_out)

    out_own = move(out_t.at[features(t)], r.out.at[t])

    cuts[:] = z.chunks

    g = r.g

    def grad_units(first, lhs, rhs, count):
        for j in range(0, count, 2):
            width = min(2, count - j)
            block = jnp.dot(
                lhs, rhs(j * LANES, width * LANES), preferred_element_type=F32
            ).astype(BF16)
            for i in range(width):
                u = first + j + i
                g[u % S, u // S] = block[:, i * LANES : (i + 1) * LANES].reshape(Z, 2, Hp, LANES)

    rc = r.rc
    swaps, plane1, plane2, along_back, first_copies = {}, {}, {}, {}, {}
    some_sums = r.ff.at[pl.ds(0, S - 1), pl.ds(0, z.NF)]
    spread_out = shared(some_sums)
    beside, over, z_sends, own_sums = {}, {}, {}, []

    plane_sends = {}
    for k in [3, *some_rest, 2, 1, 0]:
        place = every(g, k, every_chip, 1 - core)
        to = rc.at[pl.ds(0, z.rest), z.NF] if k == REST else rc.at[:, rounds(k)]
        if z.square and z.line and k != REST:
            a, b = cuts[k]
            plane_sends[k] = sendings()
            together.append((plane_sends[k], wg.at[pl.ds(0, b - a), pl.ds(0, 7), :, 0]))
        swaps[k] = remote(place, to, partner, None, plane_sends.get(k))
        if k not in plane_sends:
            sent.append(swaps[k])

    def add_swapped(k):
        swaps[k].wait_recv()
        at_ = [(q, z.NF) for q in range(z.rest)]
        if k != REST:
            at_ = [(q, n) for q in range(S) for n in range(*cuts[k])]
        for q, n in at_:
            g[q, n, :, core] = (g[q, n, :, core].astype(F32) + rc[q, n].astype(F32)).astype(BF16)

    near, far = pl.ds(0, Z // 2), pl.ds(Z // 2, Z // 2)

    def to_plane(k, at_end=None):
        span = rounds(k)
        if k not in plane1:
            if z.square:
                if k in plane_sends:
                    over_x, over_y = ((arrivals(1), plane_sends[k]) for _ in range(2))
                else:
                    over_x, over_y = shared(r.rx.at[:, span]), shared(r.ry.at[:, span])
                plane1[k] = [(over_x[0], r.rx.at[:, span]), (over_y[0], r.ry.at[:, span])]
                first_copies[k] = [
                    remote(g.at[sx, span, near, core], r.rx.at[0, span], x_side, *over_x),
                    remote(g.at[sd, span, near, core], r.rx.at[1, span], x_side, *over_x),
                    remote(g.at[sy, span, far, core], r.ry.at[0, span], y_side, *over_y),
                    remote(g.at[sd, span, far, core], r.ry.at[1, span], y_side, *over_y),
                ]
            else:
                others = r.rd.at[pl.ds(1, S - 1), span]
                over = shared(others)
                plane1[k] = [(over[0], others)]
                first_copies[k] = [
                    remote(g.at[seq_at(i), span, :, core], r.rd.at[i, span], (seq_at(i), t), *over)
                    for i in range(1, S)
                ]

        def go():
            add_swapped(k)
            for copy in first_copies[k]:
                copy.start()

        go() if at_end is None else only(at_end, go)

    def add_into(q, n, where, other):
        g[q, n, where, core] = (g[q, n, where, core].astype(F32) + other.astype(F32)).astype(BF16)

    def turn_plane(k):
        a, b = cuts[k]
        span = pl.ds(a, b - a)
        for arrival, place in plane1[k]:
            arrived(arrival, place)
        if not z.square:
            return
        for n in range(a, b):
            add_into(sy, n, near, r.rx[1, n])
            add_into(sx, n, far, r.ry[1, n])
        plane2[k] = [
            push(g.at[sy, span, near, core], r.ry2.at[span], y_side, None, plane_sends.get(k)),
            push(g.at[sx, span, far, core], r.rx2.at[span], x_side, None, plane_sends.get(k)),
        ]
        for n in range(a, b):
            add_into(s, n, near, r.rx[0, n])
            add_into(s, n, far, r.ry[0, n])

    def to_z(k):
        a, b = cuts[k]
        span = pl.ds(a, b - a)
        if z.square:
            for copy in plane2[k]:
                copy.wait_recv()
            for n in range(a, b):
                add_into(s, n, near, r.ry2[n])
                add_into(s, n, far, r.rx2[n])
        else:
            for n in range(a, b):
                sums = g[s, n, :, core].astype(F32)
                for i in range(1, S):
                    sums = sums + r.rd[i, n].astype(F32)
                g[s, n, :, core] = sums.astype(BF16)

    def sums_of(k):
        if k == REST:
            return [(q, z.NF, z.NF + q) for q in range(z.rest)]
        return [(s, n, n) for n in range(*cuts[k])]

    def rows_of(k):
        return pl.ds(z.NF, z.rest) if k == REST else rounds(k)

    def z_start(k):
        if z.line:
            beside[k] = arrivals(2)
            z_sends[k] = sendings()
            blocks = len(sums_of(k))
            together.append((z_sends[k], wg.at[pl.ds(0, blocks), pl.ds(0, 3), 0, 0]))
            for n, (which, to) in enumerate(
                [(pl.ds(2 - 2 * upper, 2), pl.ds(1 - upper, 2)), (middle, 2 * upper)]
            ):
                copy = remote(
                    carried(g, k, which, core),
                    r.rz_end.at[rows_of(k), to],
                    at_layer(middle),
                    beside[k] + n,
                    z_sends[k],
                )
                only(True, copy.start)
        else:
            along_back[k] = [
                push(carried(g, k, z_at(i), core), r.rz.at[i, rows_of(k)], dev_z(i)) for i in steps
            ]

    def z_over(k):
        if z.line:
            over[k] = arrivals(1)
            pair = pl.ds(2 - 2 * upper, 2)
            copy = remote(
                carried(g, k, pair, core), r.rz_pair.at[rows_of(k)], at_layer(3 - layer), over[k], z_sends[k]
            )

            @pl.when(inner == 1)
            def _():
                arrived(beside[k], r.rz_end.at[rows_of(k), pl.ds(1 - upper, 2)])
                for q, n, b in sums_of(k):
                    add_into(q, n, pair, r.rz_end[b, pl.ds(1 - upper, 2)])
                copy.start()

    def z_middle(k):
        if z.line:
            along_back[k] = remote(
                carried(g, k, end, core), r.rz_one.at[rows_of(k)], at_layer(end), None, z_sends[k]
            )

            @pl.when(inner == 1)
            def _():
                arrived(over[k], r.rz_pair.at[rows_of(k)])
                for q, n, b in sums_of(k):
                    add_into(q, n, pl.ds(2 * upper, 2), r.rz_pair[b])
                along_back[k].start()
                arrived(beside[k] + 1, r.rz_end.at[rows_of(k), 2 * upper])
                for q, n, b in sums_of(k):
                    sums = g[q, n, layer, core].astype(F32) + r.rz_end[b, 2 * upper].astype(F32)
                    r.ff_own[b] = sums.astype(BF16)

    own_copies = {}

    def to_all(k, at_end):
        place = r.ff_own.at[rows_of(k)]
        if k != REST and k not in own_copies:
            counts[2] += 1
            own_copies[k] = pltpu.make_async_copy(
                place, r.ff.at[s, rounds(k)], local.at[counts[2] - 1]
            )
            own_sums.append(own_copies[k])

        def go():
            if not z.line:
                for copy in along_back[k]:
                    copy.wait_recv()
                for q, n, b in sums_of(k):
                    sums = g[q, n, layer, core].astype(F32)
                    for i in steps:
                        sums = sums + r.rz[i, b].astype(F32)
                    r.ff_own[b] = sums.astype(BF16)
            elif at_end:
                along_back[k].wait_recv()
                for q, n, b in sums_of(k):
                    sums = g[q, n, layer, core].astype(F32) + r.rz_one[b].astype(F32)
                    r.ff_own[b] = sums.astype(BF16)
            for i in range(1, S):
                if k == REST:
                    push(place, r.others.at[i], (seq_at(i), t), *for_others)
                else:
                    push(place, r.ff.at[s, rounds(k)], (seq_at(i), t), *spread_out)
            if k != REST:
                own_copies[k].start()

        only(at_end, go)

    def rest_end():
        arrived(for_others[0], some_others)
        for q in range(z.rest):
            sums = r.ff_own[z.NF + q].astype(F32)
            for i in range(1, S):
                sums = sums + r.others[i, q].astype(F32)
            r.rest_sum[q] = sums.astype(BF16)
        own_sums.append(move(r.rest_sum, r.ff.at[pl.ds(0, z.rest), z.NF]))

    if z.rest:
        some_others = r.others.at[pl.ds(1, S - 1)]
        for_others = shared(some_others)
    for u in [] if z.rest else range(z.units, S * NR):
        g[u % S, u // S] = jnp.zeros((Z, 2, Hp, LANES), BF16)
    own = slice(RIM, RIM + N)

    def last_gradients(at_end):
        def go():
            act2_t = act2[own, :].astype(F32).T.astype(BF16)
            grad_units(z.nd + TAPS * z.nh, act2_t, lambda c, w: cote[own, c : c + w], z.nd)
            for k in [3, *some_rest]:
                swaps[k].start()

        only(at_end, go)

    def conv_gradients(at_end):
        def go():
            dhid2_t = dhid2[PAD + RIM : PAD + RIM + N, :].T.astype(BF16)
            ahead = max(z.chunks[2][0] * S - z.nd, 0)
            skip = ahead * LANES
            later_units = TAPS * z.nh - ahead
            grad_units(z.nd + ahead, dhid2_t, lambda c, w: taps[own, skip + c : skip + c + w], later_units)
            swaps[2].start()
            grad_units(z.nd, dhid2_t, lambda c, w: taps[own, c : c + w], ahead)
            if not at_end:
                swaps[1].start()

        only(at_end, go)

    def add_rest(at_end):
        for k in some_rest:
            only(at_end, functools.partial(add_swapped, k))

    last_gradients(True)
    inner_norm(1, keep_act2, 0, 1, RIM)
    inner_norm(1, keep_act2, RIM + N, 1, RIM)

    edge_r.wait_recv()
    edge_l.wait_recv()
    r.hid[...] = lax.dot_general(cote[...], last_weight(), NT, preferred_element_type=F32)
    r.acc1[...] = jnp.zeros_like(r.acc1)
    r.acc2[...] = jnp.zeros_like(r.acc2)
    r.acc0[...] = jnp.zeros_like(r.acc0)

    def inner_norm_back(which, first, count, size, grad_store, acc_ref=None):
        gain = r.gains[which : which + 1, :]
        xhat_ref, slope_ref, scale_ref = (
            (r.xhat1, r.slope1, r.scale1),
            (r.xhat2, r.slope2, r.scale2),
        )[which]

        def body(i, carry):
            row = pl.multiple_of(first + i * size, 16)
            xhat = cells(xhat_ref, row, size)
            dpre = cells(r.hid, row, size) * cells(slope_ref, row, size)
            if acc_ref is not None:
                dgain = dpre * xhat
                acc_ref[...] += sum(dgain[n : n + 8] for n in range(0, size, 8))
            dx = dpre * gain
            plain = jnp.sum(dx, axis=1, keepdims=True) / H
            cross = jnp.sum(dx * xhat, axis=1, keepdims=True) / H
            grad_store(row, cells(scale_ref, row, size) * (dx - plain - xhat * cross))
            return carry

        lax.fori_loop(0, count, body, 0)

    dhid2 = r.dhid2
    dhid2[0:PAD, :] = jnp.zeros((PAD, HP), F32)
    dhid2[PAD + E :, :] = jnp.zeros((PAD, HP), F32)

    def keep_dhid2(row, grad):
        dhid2[pl.ds(pl.multiple_of(row + PAD, 8), grad.shape[0]), :] = grad.astype(BF16).astype(F32)

    inner_norm_back(1, 0, 1, RIM, keep_dhid2)
    inner_norm_back(1, RIM, N // BLOCK, BLOCK, keep_dhid2, r.acc2)
    inner_norm_back(1, RIM + N, 1, RIM, keep_dhid2)

    to_plane(3, True)
    add_rest(True)
    for k in some_rest:
        z_start(k)
    conv_gradients(True)
    to_plane(2, True)
    only(True, swaps[1].start)

    back = r.back
    for j, offset in enumerate(OFFSETS):
        first = PAD + RIM + offset
        back[:, j * HP : (j + 1) * HP] = (
            dhid2[first : first + N, :] * r.mask[RIM : RIM + N, j : j + 1]
        ).astype(BF16)
    total = None
    for j in range(TAPS):
        term = jnp.dot(
            back[:, j * HP : (j + 1) * HP], tap_weight(TAPS - 1 - j), preferred_element_type=F32
        )
        total = term if total is None else total + term
    r.hid[RIM : RIM + N, :] = total

    dhid1 = r.dhid1

    def keep_dhid1(row, grad):
        dhid1[pl.ds(pl.multiple_of(row - RIM, 16), grad.shape[0]), :] = grad.astype(BF16)

    inner_norm_back(0, RIM, N // BLOCK, BLOCK, keep_dhid1, r.acc1)

    big[...] = jnp.dot(dhid1[...], first_weight(), preferred_element_type=F32)

    def first_norm_back(row, size):
        wide = row + RIM
        scale = cells(r.scale0, wide, size)
        xhat = (cells(xe, wide, size).astype(F32) - cells(r.mean0, wide, size)) * scale
        dpre = cells(big, row, size) * cells(r.slope0, wide, size)
        dgain = dpre * xhat
        r.acc0[...] += sum(dgain[n : n + 8] for n in range(0, size, 8))
        dx = dpre * gain0
        plain = jnp.sum(dx, axis=1, keepdims=True) / D
        cross = jnp.sum(dx * xhat, axis=1, keepdims=True) / D
        grad = scale * (dx - plain - xhat * cross)
        r.gi_own[pl.ds(row, size), :] = (cells(cote, wide, size).astype(F32) + grad).astype(BF16)

    gi, gi_own = r.gi, r.gi_own
    marks = [0, N // 4, N // 2, 3 * N // 4, 7 * N // 8, N]
    parts = len(marks) - 1

    def part_span(q):
        return pl.ds(marks[q], marks[q + 1] - marks[q])

    row_bases = {}
    core_rows = gi.at[pl.ds(0, Z)]
    for_rows = shared(core_rows)

    def rows_along(qs, js, at_end):
        def onward(j, place):
            return [remote(place, place, partner, *for_rows)]

        for j in js:
            for q in qs:
                span = part_span(q)
                place = gi.at[2 * origins[j] + core, span]
                take(row_bases[q], j, place, onward, at_end)

    def rows_own(q):
        span = part_span(q)
        return send_own(row_bases[q], gi_own.at[span], gi.at[t, span], q >= 2)

    later = []
    for q in range(parts):
        first_norm_back(marks[q], marks[q + 1] - marks[q])
        span = part_span(q)
        some = gi.at[pl.ds(0, Z + 1 if z.line else Z - 1), span]
        row_bases[q] = stream(gi_own.at[span], some)
        later.append(rows_own(q))
        push(gi_own.at[span], gi.at[t, span], partner, *for_rows)
    own_row = move(gi_own, gi.at[t])
    last_gradients(False)
    conv_gradients(False)

    vec = r.vec
    sum0 = jnp.sum(r.acc0[...], axis=0, keepdims=True)
    sum1 = jnp.sum(r.acc1[...], axis=0, keepdims=True)
    sum2 = jnp.sum(r.acc2[...], axis=0, keepdims=True)
    vec[...] = jnp.zeros_like(vec)
    for j in range(z.nd):
        vec[j : j + 1, :] = sum0[:, j * LANES : (j + 1) * LANES]
    for j in range(z.nh):
        vec[z.nd + j : z.nd + j + 1, :] = sum1[:, j * LANES : (j + 1) * LANES]
        vec[z.nd + z.nh + j : z.nd + z.nh + j + 1, :] = sum2[:, j * LANES : (j + 1) * LANES]
    vec_plane = shared(r.vec_plane.at[pl.ds(1, S - 1)])
    for i in range(1, S):
        push(vec, r.vec_plane.at[i], (seq_at(i), t), *vec_plane)

    dhid1_t = dhid1[...].astype(F32).T.astype(BF16)
    grad_units(0, dhid1_t, lambda c, w: r.act0[own, c : c + w], z.nd)
    swaps[0].start()
    to_plane(3, False)
    add_rest(False)
    to_plane(2, False)
    turn_plane(3)
    to_plane(1)
    turn_plane(2)
    to_plane(0)
    to_z(3)
    z_start(3)
    later[2]()
    rows_along([0, 1], [1], False)
    for k in some_rest:
        z_over(k)
    z_over(3)
    turn_plane(1)
    to_z(2)
    z_start(2)
    later[3]()
    later[4]()
    rows_along([0], [2], False)
    rows_along([2, 3, 4], [1], False)
    rows_along([1], [2], False)

    arrived(vec_plane[0], r.vec_plane.at[pl.ds(1, S - 1)])
    vec_sum = r.vec_sum
    vec_sum[...] = sum((r.vec_plane[i] for i in range(1, S)), vec[...])
    vec_z = shared(r.vec_z.at[pl.ds(0, Z - 1)])
    for i in range(1, Z):
        push(vec_sum, r.vec_z.at[i - 1], dev_z(i), *vec_z)

    turn_plane(0)
    z_over(2)
    rows_along([2], [2], False)
    for k in [*some_rest, 3]:
        z_middle(k)
        to_all(k, False)
    to_z(1)
    z_start(1)
    rows_along([0], [3], False)
    to_z(0)
    z_start(0)
    rows_along([1], [3], False)
    z_over(1)
    z_middle(2)
    to_all(2, False)
    z_over(0)
    rows_along([3, 4], [2], False)
    for k in some_rest:
        to_all(k, True)
    to_all(3, True)
    rows_along([2], [3], False)
    z_middle(1)
    to_all(1, False)
    rows_along([0, 1, 2, 3, 4], [1], True)
    rows_along([0, 1], [2], True)
    z_middle(0)
    to_all(0, False)
    for k in (2, 1, 0):
        to_all(k, True)
    rows_along([3, 4], [3], False)
    rows_along([2, 3, 4], [2], True)
    rows_along([0, 1], range(3, Z), True)

    arrived(vec_z[0], r.vec_z.at[pl.ds(0, Z - 1)])
    vec_half = r.vec_half
    vec_half[...] = sum((r.vec_z[i - 1] for i in range(1, Z)), vec_sum[...])
    vec_core = push(vec_half, r.gain_sums.at[1], partner)
    own_sums.append(move(vec_half, r.gain_sums.at[0]))
    rows_along([2, 3, 4], range(3, Z), True)
    arrived(spread_out[0], some_sums)

    vec_core.wait_recv()
    if z.rest:
        rest_end()
    for copy in own_sums:
        copy.wait()
    out_own.wait()
    arrived(for_out[0], some_out)
    own_row.wait()
    arrived(for_rows[0], core_rows)
    assert all(n <= sems.shape[0] for n, sems in zip(counts, (send, recv, local)))
    for copy in sent:
        copy.wait_send()
    for sends, place in together:
        remote(place, place, partner, 0, sends).wait_send()
    for when, sends, place in together_if:
        pl.when(when)(remote(place, place, partner, 0, sends).wait_send)
    for when, copy in sent_if:

        @pl.when(when)
        def _():
            copy.wait_send()


def finish(z, *refs):
    got, gi_got, ff, gain_sums = refs[:4]
    out, gi, grad_first, grad_conv, grad_last, grad_gain, grad_gain1, grad_gain2, *refs = refs[4:]
    first, conv, last, gain, gain1, gain2, sems = refs
    t = lax.axis_index("tp")
    copies = []

    def move(src, dst):
        copy = pltpu.make_async_copy(src, dst, sems.at[len(copies)])
        copy.start()
        copies.append(copy)

    for i in range(z.R):
        move(gi_got.at[i], gi.at[i])
    move(got, out)

    def summed(start, count):
        return jnp.concatenate(
            [ff[u % z.S, u // z.S].astype(F32) for u in range(start, start + count)], axis=1
        )

    first[...] = summed(0, z.nd)
    move(first, grad_first)
    for k in range(TAPS):
        conv[k] = summed(z.nd + k * z.nh, z.nh)
    move(conv, grad_conv)
    last[...] = summed(z.nd + TAPS * z.nh, z.nd)
    move(last, grad_last)
    sums = gain_sums[0] + gain_sums[1]

    def line(start, count):
        return jnp.concatenate([sums[j : j + 1, :] for j in range(start, start + count)], axis=1)

    def picked(row, width, step):
        return sum(
            jnp.where(t == j, row[:, j * step : j * step + width], 0.0) for j in range(z.T)
        )

    gain[...] = picked(line(0, z.nd), z.Dt, z.Dt)
    move(gain, grad_gain)
    gain1[...] = picked(line(z.nd, z.nh), z.Hs, z.Hp)
    move(gain1, grad_gain1)
    gain2[...] = picked(line(z.nd + z.nh, z.nh), z.Hs, z.Hp)
    move(gain2, grad_gain2)
    for copy in copies:
        copy.wait()


def shards(
    mesh,
    inputs,
    starts,
    first_proj,
    dilated_conv,
    last_proj,
    first_norm_gain,
    second_norm_gain,
    third_norm_gain,
    cotangent,
):
    z = Sizes(mesh, inputs, starts, first_proj, cotangent)
    S, T, Z, N, D, E, HP, Hp, NR = z.S, z.T, z.Z, z.N, z.D, z.E, z.HP, z.Hp, z.NR
    more = Hp - z.Hs
    first, last = first_proj.T, last_proj
    conv = dilated_conv.transpose(0, 2, 1)
    if more:
        first, last = (jnp.pad(part, ((0, more), (0, 0))) for part in (first, last))
        conv = jnp.pad(
            conv.reshape(TAPS, z.Hs, T, z.Hs), ((0, 0), (0, more), (0, 0), (0, more))
        ).reshape(TAPS, Hp, HP)
    vm, anywhere = pltpu.VMEM, pl.ANY
    ins = dict(
        x=(inputs, anywhere),
        starts=(starts, vm),
        w1=(first, anywhere),
        wc=(conv, anywhere),
        w3=(last, anywhere),
        g1=(first_norm_gain.reshape(z.nd, LANES), vm),
        g2=(second_norm_gain.reshape(1, z.Hs), vm),
        g3=(third_norm_gain.reshape(1, z.Hs), vm),
        cot=(cotangent.transpose(0, 2, 1), anywhere),
    )
    outs = dict(
        out=((z.R, z.Dt, N), BF16),
        gi=((z.R, N, D), BF16),
        ff=((S, NR, Hp, LANES), BF16),
        gain_sums=((2, 24, LANES), F32),
    )
    NB = z.NF + z.rest
    near = vm if z.line else jax.ShapeDtypeStruct
    scratch = dict(
        send=pltpu.SemaphoreType.DMA((46 if z.line else 800,)),
        recv=pltpu.SemaphoreType.DMA((123 if z.line else 800,)),
        local=pltpu.SemaphoreType.DMA((14,)),
        xe=vm((E, D), BF16),
        cote=vm((E, D), BF16),
        act0=vm((E, D), BF16),
        slope0=vm((E, D), F32),
        mean0=vm((E, 1), F32),
        scale0=vm((E, 1), F32),
        mask=vm((E, LANES), F32),
        flags_left=vm((z.R, N), jnp.int32),
        flags_right=vm((z.R, N), jnp.int32),
        gslots=vm((T, 8, LANES), F32),
        gains=vm((8, HP), F32),
        wg=vm((S, NR, Z, 2, Hp, LANES), BF16),
        hid=vm((E, HP), F32),
        xhat1=vm((E, HP), F32),
        slope1=vm((E, HP), F32),
        scale1=vm((E, 1), F32),
        xhat2=vm((E, HP), F32),
        slope2=vm((E, HP), F32),
        scale2=vm((E, 1), F32),
        act1=vm((E + 2 * PAD, HP), F32),
        dhid2=vm((E + 2 * PAD, HP), F32),
        taps=vm((E, TAPS * HP), BF16),
        back=vm((N, TAPS * HP), BF16),
        act2=vm((E, HP), BF16),
        dhid1=vm((N, HP), BF16),
        big=vm((N, D), F32),
        gi_own=vm((N, D), BF16),
        acc0=vm((8, D), F32),
        acc1=vm((8, HP), F32),
        acc2=vm((8, HP), F32),
        cot_t=vm((D, N), BF16),
        out_t=vm((D, N), BF16),
        w1_in=vm((Hp, D), BF16),
        wc_in=vm((TAPS, Hp, HP), BF16),
        w3_in=vm((Hp, D), BF16),
        gl=vm((8, LANES), F32),
        g=vm((S, NR, Z, 2, Hp, LANES), BF16),
        rc=vm((S, NR, Z, Hp, LANES), BF16),
        ff_own=vm((NB, Hp, LANES), BF16),
        vec=vm((24, LANES), F32),
        vec_sum=vm((24, LANES), F32),
        vec_plane=vm((S, 24, LANES), F32),
        vec_z=vm((Z, 24, LANES), F32),
        vec_half=vm((24, LANES), F32),
    )
    if z.line:
        scratch.update(rz_end=vm((NB, 3, Hp, LANES), BF16))
        scratch.update(rz_pair=vm((NB, 2, Hp, LANES), BF16), rz_one=vm((NB, Hp, LANES), BF16))
    if z.rest:
        scratch.update(others=vm((S, z.rest, Hp, LANES), BF16))
        scratch.update(rest_sum=vm((z.rest, Hp, LANES), BF16))
    else:
        scratch.update(rz=vm((Z, NB, Hp, LANES), BF16))
    if z.square:
        scratch.update(rx=vm((2, NR, Z // 2, Hp, LANES), BF16))
        scratch.update(ry=vm((2, NR, Z // 2, Hp, LANES), BF16))
        scratch.update(rx2=vm((NR, Z // 2, Hp, LANES), BF16))
        scratch.update(ry2=vm((NR, Z // 2, Hp, LANES), BF16))
    else:
        scratch.update(rd=vm((S, NR, Z, Hp, LANES), BF16))
    names = [*ins, *outs, *scratch]
    results = pl.pallas_call(
        functools.partial(kernel, z, names),
        out_shape=[near(shape, kind) for shape, kind in outs.values()],
        in_specs=[pl.BlockSpec(memory_space=space) for _, space in ins.values()],
        out_specs=[pl.BlockSpec(memory_space=anywhere)] * len(outs),
        scratch_shapes=list(scratch.values()),
        compiler_params=pltpu.CompilerParams(
            collective_id=0, has_side_effects=True, vmem_limit_bytes=(50 if z.line else 63) * 2**20
        ),
    )(*[array for array, _ in ins.values()])
    if z.line:
        results = [pltpu.with_memory_space_constraint(part, vm) for part in results]
    shape = jax.ShapeDtypeStruct
    out, gi, grad_first, grad_conv, grad_last, grad_gain, grad_gain1, grad_gain2 = pl.pallas_call(
        functools.partial(finish, z),
        out_shape=[
            shape((z.R, z.Dt, N), BF16),
            shape((z.R, N, D), BF16),
            shape((Hp, D), F32),
            shape((TAPS, Hp, HP), F32),
            shape((Hp, D), F32),
            shape((1, z.Dt), F32),
            shape((1, z.Hs), F32),
            shape((1, z.Hs), F32),
        ],
        in_specs=[pl.BlockSpec(memory_space=space) for space in (anywhere, anywhere, vm, vm)],
        out_specs=[pl.BlockSpec(memory_space=space) for space in [anywhere] * 8],
        scratch_shapes=[
            vm((Hp, D), F32),
            vm((TAPS, Hp, HP), F32),
            vm((Hp, D), F32),
            vm((1, z.Dt), F32),
            vm((1, z.Hs), F32),
            vm((1, z.Hs), F32),
            pltpu.SemaphoreType.DMA((z.R + 7,)),
        ],
        compiler_params=pltpu.CompilerParams(vmem_limit_bytes=12 * 2**20),
    )(*results)
    if more:
        grad_first, grad_last = grad_first[: z.Hs], grad_last[: z.Hs]
        grad_conv = grad_conv.reshape(TAPS, Hp, T, Hp)[:, : z.Hs, :, : z.Hs]
        grad_conv = grad_conv.reshape(TAPS, z.Hs, z.H)
    return (
        out.transpose(0, 2, 1),
        gi,
        grad_first.T,
        grad_conv.transpose(0, 2, 1),
        grad_last,
        grad_gain.reshape(-1),
        grad_gain1.reshape(-1),
        grad_gain2.reshape(-1),
    )


def solution(mesh):
    placed = (
        P(None, "seq", None),
        P(None, "seq"),
        P(None, "tp"),
        P(None, None, "tp"),
        P("tp", None),
        P(),
        P("tp"),
        P("tp"),
        P(None, "seq", "tp"),
    )
    return jax.shard_map(
        functools.partial(shards, mesh),
        mesh=mesh,
        in_specs=placed,
        out_specs=(
            P(None, "seq", "tp"),
            P(None, "seq", None),
            P(None, "tp"),
            P(None, None, "tp"),
            P("tp", None),
            P("tp"),
            P("tp"),
            P("tp"),
        ),
        check_vma=False,
    )
```
